32 devices in a mesh: dp: 2 (over y), row: 4 (over z), col: 4 (over x, core).
Axes of the slice: x: 2, y: 2, z: 4, core: 2. Of those that a mesh axis runs over, the one named last changes fastest.
Arguments:
- hidden_in: bfloat16 [4096, 2048], P(('dp', 'row'), 'col'), may hold values from -6 to 6
- gain_attn: bfloat16 [2048], P('col'), may hold values from 0.5 to 1.5
- router_attn: bfloat16 [2048, 8], P('col'), may hold values from -0.09375 to 0.09375
- query_weight: bfloat16 [8, 2048, 2048], P(None, 'col', 'row'), may hold values from -0.125 to 0.125
- kv_weight: bfloat16 [2, 2048, 2048], P(None, 'col', 'row'), may hold values from -0.125 to 0.125
- out_weight: bfloat16 [8, 2048, 2048], P(None, 'row', 'col'), may hold values from -1.5 to 1.5
- gain_ffn: bfloat16 [2048], P('col'), may hold values from 0.5 to 1.5
- router_ffn: bfloat16 [2048, 8], P('col'), may hold values from -0.09375 to 0.09375
- gate_weight: bfloat16 [8, 2048, 5632], P(None, 'col', 'row'), may hold values from -0.125 to 0.125
- up_weight: bfloat16 [8, 2048, 5632], P(None, 'col', 'row'), may hold values from -0.125 to 0.125
- down_weight: bfloat16 [8, 5632, 2048], P(None, 'row', 'col'), may hold values from -0.078125 to 0.078125
- attn_routes: int32 [4096, 2], P('dp'), may hold values from 0 to 7, all different within a row
- ffn_routes: int32 [4096, 2], P('dp'), may hold values from 0 to 7, all different within a row
- attn_order: int32 [2, 4096], P('dp'), may hold values from 0 to 4095, each once within a row
- ffn_order: int32 [2, 4096], P('dp'), may hold values from 0 to 4095, each once within a row
- segment_ids: int32 [8, 512], P(('dp', 'col')), may hold values from 0 to 4, as said below
- d_out: bfloat16 [4096, 2048], P(('dp', 'row'), 'col'), may hold values from -6 to 6
Outputs:
- layer_out: bfloat16 [4096, 2048], P(('dp', 'row'), 'col')
- input_grad: float32 [4096, 2048], P(('dp', 'row'), 'col')
- gain_attn_grad: float32 [2048], P('col')
- router_attn_grad: float32 [2048, 8], P('col', 'dp')
- query_grad: float32 [8, 2048, 2048], P('dp', 'col', 'row')
- kv_grad: float32 [2, 2048, 2048], P('dp', 'col', 'row')
- out_grad: float32 [8, 2048, 2048], P('dp', 'row', 'col')
- gain_ffn_grad: float32 [2048], P('col')
- router_ffn_grad: float32 [2048, 8], P('col', 'dp')
- gate_grad: float32 [8, 2048, 5632], P('dp', 'col', 'row')
- up_grad: float32 [8, 2048, 5632], P('dp', 'col', 'row')
- down_grad: float32 [8, 5632, 2048], P('dp', 'row', 'col')
The draws below stay inside these ranges and needn't reach their ends.
Inputs may be any that keep to these rules, and one draw needn't show every extreme that they name: `segment_ids`: in each group the prompt (segment 0) comes first and segments 1 to 4 follow in order, each at least one token long.
All inputs are finite; a program needn't handle non-finite values.
Results may differ from the reference program's by a relative error of at most 0.015.
Values may be sent and summed in bfloat16 or wider, within the bound.
No kernel may reach another device: no remote copies, remote signals or barrier semaphores. Data moves between devices by JAX's collectives and lax.ppermute only.
A program may use at most 448 MiB of HBM per device.

```python
import math
from functools import partial
import jax
import jax.numpy as jnp
from jax import lax

D = 2048
KVH = 16
HD = 128
F = 5632
AE = 8
FE = 8
SEQ = 512
CONT = 4
GROUPS = 8
TOKENS = 4096
BATCH = 2048
CAP = 640
FCAP = 640
N_DP = 2


def draw_segment_ids(key, part):
    key = jax.random.fold_in(key, 7)
    prompt_key, score_key = jax.random.split(key)
    prompt = jax.random.randint(prompt_key, (GROUPS, 1), 3 * SEQ // 8, 5 * SEQ // 8 + 1)
    places = jnp.arange(SEQ, dtype=jnp.int32)[None, :]
    scores = jax.random.randint(score_key, (GROUPS, SEQ), 0, 2 ** 19) * SEQ + places
    scores = jnp.where(places > prompt, scores, -1)
    cut_points = lax.top_k(scores, CONT - 1)[0] % SEQ
    past_cuts = jnp.sum((places[:, :, None] >= cut_points[:, None, :]).astype(jnp.int32), axis=2)
    return ((places >= prompt).astype(jnp.int32) + past_cuts).astype(jnp.int32)


def shard_levels(own_key, extent, shards, smallest, largest):
    def one(axis_at, shards_of):
        heights = jax.random.uniform(jax.random.fold_in(jax.random.fold_in(own_key, 6), axis_at), (shards_of,), jnp.float32, smallest / len(shards), largest / len(shards))
        return jnp.repeat(jnp.exp(heights), extent[axis_at] // shards_of).reshape((-1,) + (1,) * (len(extent) - axis_at - 1))

    loudness = one(*shards[0])
    for cut in shards[1:]:
        loudness = loudness * one(*cut)
    return loudness


def different_ones(stream_key, rows, number_of, top, lift):
    ranking = jax.random.permutation(jax.random.fold_in(stream_key, 1), number_of)
    favour = ranking
    for power in range(3):
        favour = favour * favour // number_of
    favour = favour * lift // number_of
    tickets = jax.random.randint(jax.random.fold_in(stream_key, 2), (rows, number_of), 0, 4096) + favour
    sure = jax.random.permutation(jax.random.fold_in(stream_key, 3), rows)[jnp.arange(number_of) % rows]
    tickets = jnp.where(jnp.arange(rows)[:, None] == sure[None, :], 1 << 14, tickets)
    score = tickets * number_of + jnp.arange(number_of)
    return lax.top_k(score.astype(jnp.int32), top)[1].astype(jnp.int32)


def noise(key, shape, width, most, cuts=(), kind=jnp.bfloat16):
    result = width * jax.random.normal(key, shape, jnp.float32)
    if cuts:
        result = result * shard_levels(key, shape, cuts, -0.22, 0.18)
    return jnp.clip(result, -most, most).astype(kind)


def setup_inputs(seed: int = 0) -> dict:
    key_of = jax.random.split(jax.random.key(seed), 18)
    return {
        "hidden_in": noise(key_of[0], (TOKENS, D), 1.0, 6.0, ((0, 8), (1, 4))),
        "gain_attn": jnp.clip(1.0 + 0.1 * jax.random.normal(key_of[1], (D,), jnp.float32), 0.5, 1.5).astype(jnp.bfloat16),
        "router_attn": noise(key_of[2], (D, AE), (2 * D) ** -0.5, 0.09375, ((0, 4),)),
        "query_weight": noise(key_of[3], (AE, D, KVH * HD), D ** -0.5, 0.125, ((1, 4), (2, 4))),
        "kv_weight": noise(key_of[4], (2, D, KVH * HD), D ** -0.5, 0.125, ((1, 4), (2, 4))),
        "out_weight": noise(key_of[5], (AE, KVH * HD, D), (KVH * HD * 4 // SEQ) ** -0.5, 1.5, ((1, 4), (2, 4))),
        "gain_ffn": jnp.clip(1.0 + 0.1 * jax.random.normal(key_of[6], (D,), jnp.float32), 0.5, 1.5).astype(jnp.bfloat16),
        "router_ffn": noise(key_of[7], (D, FE), (2 * D) ** -0.5, 0.09375, ((0, 4),)),
        "gate_weight": noise(key_of[8], (FE, D, F), D ** -0.5, 0.125, ((1, 4), (2, 4))),
        "up_weight": noise(key_of[9], (FE, D, F), D ** -0.5, 0.125, ((1, 4), (2, 4))),
        "down_weight": noise(key_of[10], (FE, F, D), F ** -0.5, 0.078125, ((1, 4), (2, 4))),
        "attn_routes": different_ones(key_of[11], TOKENS, AE, 2, 2048),
        "ffn_routes": different_ones(key_of[12], TOKENS, FE, 2, 2048),
        "attn_order": jax.vmap(lambda own: jax.random.permutation(own, 2 * BATCH))(jax.random.split(key_of[13], N_DP)).reshape((N_DP, 2 * BATCH)).astype(jnp.int32),
        "ffn_order": jax.vmap(lambda own: jax.random.permutation(own, 2 * BATCH))(jax.random.split(key_of[14], N_DP)).reshape((N_DP, 2 * BATCH)).astype(jnp.int32),
        "segment_ids": draw_segment_ids(jax.random.fold_in(key_of[17], 71), 0),
        "d_out": noise(key_of[16], (TOKENS, D), 1.0, 6.0, ((0, 8), (1, 4))),
    }


@jax.custom_vjp
def low(v):
    return lax.optimization_barrier(v.astype(jnp.bfloat16)).astype(jnp.float32)

@jax.custom_vjp
def low_back(v):
    return v

def low_keep(v):
    return (low(v), None)

def low_pass(kept, grad):
    return (grad,)

def back_keep(v):
    return (v, None)

def back_low(kept, grad):
    return (low(grad),)
low.defvjp(low_keep, low_pass)
low_back.defvjp(back_keep, back_low)
EPSILON = 1e-06
NEGATIVE = -1e+30
PRECISE = lax.Precision.HIGHEST

def rotate_half(values):
    half_size = values.shape[-1] // 2
    return jnp.concatenate([-values[..., half_size:], values[..., :half_size]], axis=-1)

def rotary(values, cosine, sine_rows):
    return values * cosine + rotate_half(values) * sine_rows

def rope_tables(segment_ids):
    labels = jnp.arange(CONT + 1, dtype=jnp.int32)
    member = (segment_ids[:, :, None] == labels[None, None, :]).astype(jnp.int32)
    before = jnp.cumsum(member, axis=1).astype(jnp.int32) - member
    within = lax.optimization_barrier(jnp.sum(before * member, axis=2)).astype(jnp.int32)
    prompt = lax.optimization_barrier(jnp.sum((segment_ids == 0).astype(jnp.int32), axis=1, keepdims=True)).astype(jnp.int32)
    places = (within + jnp.where(segment_ids > 0, prompt, 0)).astype(jnp.float32).reshape(-1)
    frequency = jnp.exp(jnp.arange(HD // 2, dtype=jnp.float32) * (-2.0 * math.log(10000.0) / HD))
    angles = places[:, None] * frequency[None, :]
    angles = jnp.concatenate([angles, angles], axis=1)
    return (jnp.cos(angles), jnp.sin(angles))

def slot_tables(routes, pair_order, experts, capacity):
    flat_routes = routes.reshape(-1)
    chosen = jnp.take(flat_routes, pair_order, axis=0)
    labels = jnp.arange(experts, dtype=jnp.int32)
    member = (chosen[:, None] == labels[None, :]).astype(jnp.int32)
    ranked = lax.optimization_barrier(jnp.sum((jnp.cumsum(member, axis=0).astype(jnp.int32) - member) * member, axis=1)).astype(jnp.int32)
    slot_count = experts * capacity
    placed = jnp.where(ranked < capacity, chosen * capacity + ranked, slot_count).astype(jnp.int32)
    pair_slot = jnp.zeros(flat_routes.shape, jnp.int32).at[pair_order].set(placed)
    pair_ids = jnp.arange(flat_routes.shape[0], dtype=jnp.int32)
    slot_pair = jnp.full((slot_count + 1,), flat_routes.shape[0], jnp.int32).at[pair_slot].set(pair_ids)
    return (pair_slot, slot_pair[:slot_count])

def global_tables(routes, pair_order, experts, capacity):
    batches = pair_order.shape[0]
    batch_rows = routes.shape[0] // batches
    tables = jax.vmap(partial(slot_tables, experts=experts, capacity=capacity))
    pair_slot, slot_pair = tables(routes.reshape(batches, batch_rows, 2), pair_order)
    slot_count = experts * capacity
    offsets = jnp.arange(batches, dtype=jnp.int32)[:, None]
    slot_src = jnp.where(slot_pair < 2 * batch_rows, offsets * (2 * batch_rows) + slot_pair, 2 * batch_rows * batches)
    slot_src = slot_src.reshape(batches, experts, capacity).transpose(1, 0, 2).reshape(-1).astype(jnp.int32)
    kept_mask = pair_slot < slot_count
    pair_src = jnp.where(kept_mask, pair_slot // capacity * (batches * capacity) + offsets * capacity + pair_slot % capacity, slot_count * batches)
    return (slot_src, pair_src.reshape(-1).astype(jnp.int32), kept_mask.reshape(-1, 2).astype(jnp.float32))

def take_rows(source_rows, row_index):
    return jnp.take(source_rows, row_index, axis=0, mode='fill', fill_value=0)

def gates_of(logits, routes):
    labels = jnp.arange(logits.shape[1], dtype=jnp.int32)
    member = (routes[:, :, None] == labels[None, None, :]).astype(logits.dtype)
    picked = lax.optimization_barrier(jnp.sum(member * logits[:, None, :], axis=2))
    return jax.nn.softmax(picked, axis=1)

def rms_norm(values, gain_row):
    factor = lax.rsqrt(lax.optimization_barrier(jnp.mean(values * values, axis=-1, keepdims=True)) + EPSILON)
    return low(values * factor * gain_row)

def block_mask(segments, block_start, group_base, block_rows):
    seg_query = lax.dynamic_slice_in_dim(segments, block_start, block_rows, 0)
    seg_key = lax.dynamic_slice_in_dim(segments, group_base, SEQ, 0)
    place_query = block_start - group_base + jnp.arange(block_rows, dtype=jnp.int32)
    place_key = jnp.arange(SEQ, dtype=jnp.int32)
    causal = place_key[None, :] <= place_query[:, None]
    shared = (seg_key[None, :] == 0) | (seg_key[None, :] == seg_query[:, None])
    return causal & shared

def attention(queries, key_heads, values, segments):
    block_rows = min(512, SEQ)
    starts = jnp.arange(queries.shape[0] // block_rows, dtype=jnp.int32) * block_rows

    def one_block(block_start):
        group_base = block_start // SEQ * SEQ
        query_rows = lax.dynamic_slice_in_dim(queries, block_start, block_rows, 0)
        key_rows = lax.dynamic_slice_in_dim(key_heads, group_base, SEQ, 0)
        value_rows = lax.dynamic_slice_in_dim(values, group_base, SEQ, 0)
        allowed = block_mask(segments, block_start, group_base, block_rows)
        scores = jnp.einsum('qkhe,she->qkhs', query_rows, key_rows, precision=PRECISE) * HD ** (-0.5)
        scores = jnp.where(allowed[:, None, None, :], low_back(scores), NEGATIVE)
        prob_rows = jax.nn.softmax(scores, axis=-1)
        return jnp.einsum('qkhs,she->qkhe', low(prob_rows), value_rows, precision=PRECISE)
    return lax.map(jax.checkpoint(one_block), starts).reshape(queries.shape)

def expert(operands):
    slot_rows, weight_gate, weight_up, weight_down, slot_gate = operands
    gate_pre = low_back(jnp.dot(slot_rows, weight_gate, precision=PRECISE))
    up_pre = low_back(jnp.dot(slot_rows, weight_up, precision=PRECISE))
    activation = low(jax.nn.silu(gate_pre) * up_pre * slot_gate)
    return jnp.dot(activation, weight_down, precision=PRECISE)

def reference(hidden_in, gain_attn, router_attn, query_weight, kv_weight, out_weight, gain_ffn, router_ffn, gate_weight, up_weight, down_weight, attn_routes, ffn_routes, attn_order, ffn_order, segment_ids, d_out):
    attn_src, attn_pairs, attn_kept = global_tables(attn_routes, attn_order, AE, CAP)
    ffn_src, ffn_pairs, ffn_kept = global_tables(ffn_routes, ffn_order, FE, FCAP)
    cosine, sine_rows = rope_tables(segment_ids)
    segments = segment_ids.reshape(-1)
    head_width = KVH * HD

    def forward(rows_in, gain_a, router_a, weight_q, weight_kv, weight_o, gain_f, router_f, weight_g, weight_u, weight_d):
        normed = rms_norm(rows_in, gain_a)
        logits_a = low_back(jnp.dot(normed, router_a, precision=PRECISE))
        gates_a = gates_of(logits_a, attn_routes) * attn_kept
        slots_a = take_rows(normed, attn_src // 2).reshape(AE, -1, D)
        query_slots = jnp.einsum('ecd,edw->ecw', slots_a, weight_q, precision=PRECISE).reshape(-1, head_width)
        query_pairs = take_rows(query_slots, attn_pairs).reshape(TOKENS, 2, KVH, HD)
        key_value = jnp.einsum('td,jdw->jtw', normed, weight_kv, precision=PRECISE).reshape(2, TOKENS, KVH, HD)
        queries = low(rotary(low_back(query_pairs), cosine[:, None, None, :], sine_rows[:, None, None, :]))
        key_heads = low(rotary(low_back(key_value[0]), cosine[:, None, :], sine_rows[:, None, :]))
        values = low(low_back(key_value[1]))
        head_out = low_back(attention(queries, key_heads, values, segments)).reshape(TOKENS, 2, head_width)
        gated_out = low(gates_a[:, :, None] * head_out)
        out_slots = take_rows(gated_out.reshape(-1, head_width), attn_src).reshape(AE, -1, head_width)
        projected = jnp.einsum('ecw,ewd->ecd', out_slots, weight_o, precision=PRECISE).reshape(-1, D)
        attn_sum = take_rows(projected, attn_pairs).reshape(TOKENS, 2, D).sum(axis=1)
        middle = rows_in + low_back(attn_sum)
        normed_f = rms_norm(middle, gain_f)
        logits_f = low_back(jnp.dot(normed_f, router_f, precision=PRECISE))
        gates_f = gates_of(logits_f, ffn_routes) * ffn_kept
        slots_f = take_rows(normed_f, ffn_src // 2).reshape(FE, -1, D)
        slot_gates = take_rows(gates_f.reshape(-1, 1), ffn_src).reshape(FE, -1, 1)
        expert_out = lax.map(jax.checkpoint(expert), (slots_f, weight_g, weight_u, weight_d, slot_gates)).reshape(-1, D)
        ffn_total = take_rows(expert_out, ffn_pairs).reshape(TOKENS, 2, D).sum(axis=1)
        return middle + ffn_total
    primals = (hidden_in.astype(jnp.float32), gain_attn.astype(jnp.float32), router_attn.astype(jnp.float32), query_weight.astype(jnp.float32), kv_weight.astype(jnp.float32), out_weight.astype(jnp.float32), gain_ffn.astype(jnp.float32), router_ffn.astype(jnp.float32), gate_weight.astype(jnp.float32), up_weight.astype(jnp.float32), down_weight.astype(jnp.float32))
    layer_out, pullback = jax.vjp(forward, *primals)
    gradients = pullback(d_out.astype(jnp.float32))
    return (layer_out.astype(jnp.bfloat16), gradients[0], gradients[1], gradients[2], gradients[3], gradients[4], gradients[5], gradients[6], gradients[7], gradients[8], gradients[9], gradients[10])
```

```python
import functools
import math

import jax
import jax.numpy as jnp
from jax import lax
from jax.experimental import pallas as pl
from jax.experimental.pallas import tpu as pltpu
from jax.sharding import PartitionSpec as P

D = 2048
HD = 128
SEQ = 512
CONT = 4

EPSILON = 1e-06
NEGATIVE = -1e30
VMEM_BYTES = 56 * 1024 * 1024
TILE = 128
WINDOW = TILE + 16
BF = jnp.bfloat16
F32 = jnp.float32


def after(value, *others):
    return lax.optimization_barrier((value,) + others)[0]


def rope_tables(segment_ids):
    labels = jnp.arange(CONT + 1, dtype=jnp.int32)
    member = (segment_ids[:, :, None] == labels[None, None, :]).astype(jnp.int32)
    before = jnp.cumsum(member, axis=1) - member
    within = jnp.sum(before * member, axis=2)
    prompt = jnp.sum((segment_ids == 0).astype(jnp.int32), axis=1, keepdims=True)
    places = (within + jnp.where(segment_ids > 0, prompt, 0)).astype(F32).reshape(-1)
    frequency = jnp.exp(jnp.arange(HD // 2, dtype=F32) * (-2.0 * math.log(10000.0) / HD))
    angles = places[:, None] * frequency[None, :]
    cosine, sine = jnp.cos(angles), jnp.sin(angles)
    return (
        jnp.concatenate([cosine, cosine], axis=1),
        jnp.concatenate([-sine, sine], axis=1),
    )


def kept_pairs(routes, pair_order, experts, capacity):
    pairs = pair_order.shape[0]
    side = 64
    digits = jnp.arange(side, dtype=jnp.int32)[None, :]
    high = (pair_order[:, None] // side == jnp.arange(pairs // side, dtype=jnp.int32)[None, :])
    high = high.astype(BF)
    low = (pair_order[:, None] % side == digits).astype(BF)
    table = routes.reshape(pairs // side, side).astype(BF)
    chosen = jnp.sum(jnp.dot(high, table, preferred_element_type=F32) * low, axis=1)
    labels = jnp.arange(experts, dtype=F32)
    member = (chosen[:, None] == labels[None, :]).astype(jnp.int32)
    ranked = jnp.sum((jnp.cumsum(member, axis=0) - member) * member, axis=1)
    placed = (ranked < capacity).astype(BF)
    kept = lax.dot_general(
        high * placed[:, None], low, (((0,), (0,)), ((), ())), preferred_element_type=F32
    )
    return kept.reshape(routes.shape).astype(jnp.int32)


def token_slots(routes, kept, labels, slots):
    member = (routes[:, :, None] == labels[None, None, :]).astype(jnp.int32)
    member = jnp.sum(member * kept[:, :, None], axis=1)
    ranked = jnp.cumsum(member, axis=0)
    starts = (ranked - member)[::TILE] // 16 * 16
    return (ranked * member - 1, jnp.minimum(starts, slots - WINDOW))


def pick_kernel(extra, transposed, blocks_ref, routes_ref, x_ref, w_ref, *rest):
    outs = rest[-2:]
    rows = x_ref[...]
    experts = w_ref.shape[0]
    width = w_ref.shape[1] if transposed else w_ref.shape[2]
    contract = (((1,), (1 if transposed else 0,)), ((), ()))
    first = jnp.broadcast_to(routes_ref[:, 0:1], (rows.shape[0], width))
    second = jnp.broadcast_to(routes_ref[:, 1:2], (rows.shape[0], width))
    picked = [jnp.zeros((rows.shape[0], width), F32) for _ in range(2)]
    for expert in range(experts):
        product = lax.dot_general(rows, w_ref[expert], contract, preferred_element_type=F32)
        picked[0] = jnp.where(first == expert, product, picked[0])
        picked[1] = jnp.where(second == expert, product, picked[1])
    for place in range(extra):
        picked.append(
            lax.dot_general(rows, rest[0][place], contract, preferred_element_type=F32)
        )
    picked = [item.astype(BF) for item in picked]
    for block, o_ref in enumerate(outs):

        @pl.when(pl.program_id(0) == block)
        def _():
            for place, item in enumerate(picked):
                o_ref[:, place * width : (place + 1) * width] = item


def pick_matmul(blocks, routes, rows, weight, extra_weight, block_rows, transposed):
    experts = weight.shape[0]
    depth = rows.shape[1]
    width = weight.shape[1] if transposed else weight.shape[2]
    tile = min(256, block_rows)
    tiles = block_rows // tile
    extra = 0 if extra_weight is None else extra_weight.shape[0]
    total = (2 + extra) * width
    in_specs = [
        pl.BlockSpec((tile, 2), lambda b, i, s: (s[b] * tiles + i, 0)),
        pl.BlockSpec((tile, depth), lambda b, i, s: (s[b] * tiles + i, 0)),
        pl.BlockSpec(weight.shape, lambda b, i, s: (0, 0, 0)),
    ]
    operands = [routes, rows, weight]
    if extra:
        in_specs.append(pl.BlockSpec(extra_weight.shape, lambda b, i, s: (0, 0, 0)))
        operands.append(extra_weight)
    flops = 4 * block_rows * depth * width * (experts + extra)
    return pl.pallas_call(
        functools.partial(pick_kernel, extra, transposed),
        out_shape=[jax.ShapeDtypeStruct((block_rows, total), BF)] * 2,
        grid_spec=pltpu.PrefetchScalarGridSpec(
            num_scalar_prefetch=1,
            grid=(2, tiles),
            in_specs=in_specs,
            out_specs=[
                pl.BlockSpec((tile, total), lambda b, i, s: (jnp.where(b == 0, i, tiles - 1), 0)),
                pl.BlockSpec((tile, total), lambda b, i, s: (jnp.where(b == 0, 0, i), 0)),
            ],
        ),
        compiler_params=pltpu.CompilerParams(vmem_limit_bytes=VMEM_BYTES),
        cost_estimate=pl.CostEstimate(
            flops=flops,
            bytes_accessed=2 * (weight.size + 2 * block_rows * (depth + total)),
            transcendentals=0,
        ),
    )(blocks, *operands)


def mixed_rows(routes_ref, rows_ref, expert):
    first = (routes_ref[:, 0:1] == expert).astype(F32).astype(BF)
    second = (routes_ref[:, 1:2] == expert).astype(F32).astype(BF)
    return rows_ref[0] * first + rows_ref[1] * second


def merge_kernel(extra, transposed, routes_ref, rows_ref, w_ref, *rest):
    o_ref = rest[-1]
    experts = w_ref.shape[0]
    contract = (((1,), (1 if transposed else 0,)), ((), ()))
    total = jnp.zeros(o_ref.shape, F32)
    for expert in range(experts):
        mixed = mixed_rows(routes_ref, rows_ref, expert)
        total += lax.dot_general(mixed, w_ref[expert], contract, preferred_element_type=F32)
    if extra:
        logits_ref, pair_ref, router_ref = rest[:3]
        for place in range(2):
            total += lax.dot_general(
                rows_ref[2 + place], pair_ref[place], contract, preferred_element_type=F32
            )
        total += lax.dot_general(
            logits_ref[...], router_ref[...], contract, preferred_element_type=F32
        )
    o_ref[...] = total.astype(o_ref.dtype)


def merge_matmul(routes, rows, weight, extras, transposed):
    parts, count, width = rows.shape
    depth = weight.shape[1] if transposed else weight.shape[2]
    tile = min(256, count)
    in_specs = [
        pl.BlockSpec((tile, 2), lambda i: (i, 0)),
        pl.BlockSpec((parts, tile, width), lambda i: (0, i, 0)),
        pl.BlockSpec(weight.shape, lambda i: (0, 0, 0)),
    ]
    if extras:
        in_specs.append(pl.BlockSpec((tile, extras[0].shape[1]), lambda i: (i, 0)))
        in_specs.append(pl.BlockSpec(extras[1].shape, lambda i: (0, 0, 0)))
        in_specs.append(pl.BlockSpec(extras[2].shape, lambda i: (0, 0)))
    flops = 2 * count * depth * width * (weight.shape[0] + len(extras))
    return pl.pallas_call(
        functools.partial(merge_kernel, len(extras), transposed),
        out_shape=jax.ShapeDtypeStruct((count, depth), BF),
        grid=(count // tile,),
        in_specs=in_specs,
        out_specs=pl.BlockSpec((tile, depth), lambda i: (i, 0)),
        compiler_params=pltpu.CompilerParams(vmem_limit_bytes=VMEM_BYTES),
        cost_estimate=pl.CostEstimate(
            flops=flops,
            bytes_accessed=2 * (weight.size + rows.size + count * depth),
            transcendentals=0,
        ),
    )(routes, rows, weight, *extras)


def right_grad_kernel(base_ref, routes_ref, left_ref, rows_ref, o_ref):
    expert = base_ref[0] + pl.program_id(0)
    mixed = mixed_rows(routes_ref, rows_ref, expert)
    product = jnp.dot(left_ref[...], mixed, preferred_element_type=F32)
    o_ref[0] = product.astype(o_ref.dtype)


def left_grad_kernel(base_ref, routes_ref, left_ref, rows_ref, o_ref):
    expert = base_ref[0] + pl.program_id(0)
    first = (routes_ref[0:1, :] == expert).astype(F32).astype(BF)
    second = (routes_ref[1:2, :] == expert).astype(F32).astype(BF)
    mixed = left_ref[0] * first + left_ref[1] * second
    product = jnp.dot(mixed, rows_ref[...], preferred_element_type=F32)
    o_ref[0] = product.astype(o_ref.dtype)


def expert_grads(kernel, base, count, routes, left, rows, shape, dtype):
    tokens = rows.shape[-2]
    whole = lambda array: pl.BlockSpec(array.shape, lambda i, s: (0,) * array.ndim)
    return pl.pallas_call(
        kernel,
        out_shape=jax.ShapeDtypeStruct((count,) + shape, dtype),
        grid_spec=pltpu.PrefetchScalarGridSpec(
            num_scalar_prefetch=1,
            grid=(count,),
            in_specs=[whole(routes), whole(left), whole(rows)],
            out_specs=pl.BlockSpec((1,) + shape, lambda i, s: (i, 0, 0)),
        ),
        compiler_params=pltpu.CompilerParams(vmem_limit_bytes=VMEM_BYTES),
        cost_estimate=pl.CostEstimate(
            flops=2 * count * shape[0] * shape[1] * tokens,
            bytes_accessed=2 * (left.size + rows.size) + 4 * count * shape[0] * shape[1],
            transcendentals=0,
        ),
    )(base, routes, left, rows)


def spread_kernel(groups, starts_ref, places_ref, rows_ref, *refs):
    outs, totals = refs[: len(groups)], refs[len(groups) :]
    blocks = [bits for group in groups for bits in group]
    tokens = rows_ref.shape[0]
    for total_ref in totals:
        total_ref[...] = jnp.zeros(total_ref.shape, F32)
    slot = lax.broadcasted_iota(jnp.int32, (WINDOW, TILE), 0)
    for index in range(tokens // TILE):
        span = slice(index * TILE, (index + 1) * TILE)
        rows = rows_ref[span, :]
        for bits, total_ref in zip(blocks, totals):
            start = pl.multiple_of(starts_ref[bits, index], 16)
            hot = (slot == places_ref[bits : bits + 1, span] - start).astype(F32).astype(BF)
            product = jnp.dot(hot, rows, preferred_element_type=F32)
            total_ref[pl.ds(start, WINDOW), :] += product
    place = 0
    for group, o_ref in zip(groups, outs):
        for lead in range(len(group)):
            value = totals[place][...].astype(BF)
            if len(group) == 1:
                o_ref[...] = value
            else:
                o_ref[lead] = value
            place += 1


def spread_rows(starts, places, rows, slots, groups):
    tokens, width = rows.shape
    shapes = [
        (slots, width) if len(group) == 1 else (len(group), slots, width) for group in groups
    ]
    count = sum(len(group) for group in groups)
    return pl.pallas_call(
        functools.partial(spread_kernel, groups),
        out_shape=[jax.ShapeDtypeStruct(shape, BF) for shape in shapes],
        grid_spec=pltpu.PrefetchScalarGridSpec(
            num_scalar_prefetch=1,
            grid=(1,),
            in_specs=[
                pl.BlockSpec(places.shape, lambda i, s: (0, 0)),
                pl.BlockSpec((tokens, width), lambda i, s: (0, 0)),
            ],
            out_specs=[
                pl.BlockSpec(shape, lambda i, s, n=len(shape): (0,) * n) for shape in shapes
            ],
            scratch_shapes=[pltpu.VMEM((slots, width), F32) for _ in range(count)],
        ),
        compiler_params=pltpu.CompilerParams(vmem_limit_bytes=VMEM_BYTES),
        cost_estimate=pl.CostEstimate(
            flops=4 * count * WINDOW * tokens * width,
            bytes_accessed=2 * (tokens + count * slots) * width,
            transcendentals=0,
        ),
    )(starts, places, rows)


def gather_kernel(tiles, starts_ref, places_ref, *refs):
    o_ref = refs[-1]
    slot = lax.broadcasted_iota(jnp.int32, (TILE, WINDOW), 1)
    for index in range(tiles):
        span = slice(index * TILE, (index + 1) * TILE)
        total = jnp.zeros((TILE, o_ref.shape[1]), F32)
        for block, block_ref in enumerate(refs[:-1]):
            start = pl.multiple_of(starts_ref[block, pl.program_id(0) * tiles + index], 16)
            hot = (slot == places_ref[span, block : block + 1] - start).astype(F32).astype(BF)
            total += jnp.dot(
                hot, block_ref[pl.ds(start, WINDOW), :], preferred_element_type=F32
            )
        o_ref[span, :] = total.astype(o_ref.dtype)


def gather_slots(starts, places, blocks):
    tokens = places.shape[0]
    slots, width = blocks[0].shape
    tiles = 4
    tile = tiles * TILE
    return pl.pallas_call(
        functools.partial(gather_kernel, tiles),
        out_shape=jax.ShapeDtypeStruct((tokens, width), BF),
        grid_spec=pltpu.PrefetchScalarGridSpec(
            num_scalar_prefetch=1,
            grid=(tokens // tile,),
            in_specs=[pl.BlockSpec((tile, places.shape[1]), lambda i, s: (i, 0))]
            + [pl.BlockSpec((slots, width), lambda i, s: (0, 0)) for _ in blocks],
            out_specs=pl.BlockSpec((tile, width), lambda i, s: (i, 0)),
        ),
        compiler_params=pltpu.CompilerParams(vmem_limit_bytes=VMEM_BYTES),
        cost_estimate=pl.CostEstimate(
            flops=4 * WINDOW * tokens * width * len(blocks),
            bytes_accessed=2 * (tokens + slots * len(blocks)) * width,
            transcendentals=0,
        ),
    )(starts, places, *blocks)


def dots_kernel(transposed, lead, terms, *refs):
    count = (len(refs) - terms) // (terms + 1)
    outs = refs[len(refs) - count :]
    contract = (((1,), (1 if transposed else 0,)), ((), ()))
    operands = [ref[0] if flag else ref[...] for ref, flag in zip(refs, lead)]
    for place, o_ref in enumerate(outs):
        total = None
        for term in range(terms):
            right = operands[terms * (1 + place) + term]
            product = lax.dot_general(
                operands[term], right, contract, preferred_element_type=F32
            )
            total = product if total is None else total + product
        o_ref[...] = total.astype(o_ref.dtype)


def dots(lefts, right_lists, transposed, dtype):
    operands, specs, lead = [], [], []
    rows = lefts[0][0].shape[1] if isinstance(lefts[0], tuple) else lefts[0].shape[0]
    tile = rows // 2 if rows % 32 == 0 else rows
    flops, size = 0, 0
    for side, items in enumerate([lefts] + list(right_lists)):
        for item in items:
            array, place = item if isinstance(item, tuple) else (item, None)
            shape = array.shape[-2:]
            block = (tile, shape[1]) if side == 0 else shape
            if place is None:
                specs.append(
                    pl.BlockSpec(block, (lambda i: (i, 0)) if side == 0 else (lambda i: (0, 0)))
                )
            elif side == 0:
                specs.append(pl.BlockSpec((1,) + block, lambda i, p=place: (p, i, 0)))
            else:
                specs.append(pl.BlockSpec((1,) + block, lambda i, p=place: (p, 0, 0)))
            operands.append(array)
            lead.append(place is not None)
            size += 2 * shape[0] * shape[1]
            if side:
                flops += 2 * rows * shape[0] * shape[1]
    width = shape[0] if transposed else shape[1]
    count = len(right_lists)
    return pl.pallas_call(
        functools.partial(dots_kernel, transposed, lead, len(lefts)),
        out_shape=[jax.ShapeDtypeStruct((rows, width), dtype)] * count,
        grid=(rows // tile,),
        in_specs=specs,
        out_specs=[pl.BlockSpec((tile, width), lambda i: (i, 0))] * count,
        compiler_params=pltpu.CompilerParams(vmem_limit_bytes=VMEM_BYTES),
        cost_estimate=pl.CostEstimate(
            flops=2 * flops, bytes_accessed=size + 2 * count * rows * width, transcendentals=0
        ),
    )(*operands)


def turned_kernel(count, lead, *refs):
    contract = (((0,), (0,)), ((), ()))
    outs = refs[len(refs) - count :]
    refs = refs[: len(refs) - count]
    lefts = [ref[0] if flag else ref[...] for ref, flag in zip(refs[:2], lead[:2])]
    for place, o_ref in enumerate(outs):
        rights = refs[2 + 2 * place : 4 + 2 * place]
        flags = lead[2 + 2 * place : 4 + 2 * place]
        total = None
        for left, ref, flag in zip(lefts, rights, flags):
            right = ref[0] if flag else ref[...]
            product = lax.dot_general(left, right, contract, preferred_element_type=F32)
            total = product if total is None else total + product
        o_ref[...] = total.astype(o_ref.dtype)


def turned_dots(lefts, rights, dtypes):
    operands, specs, lead = [], [], []
    flops = 0
    shapes = []
    for item in list(lefts) + [each for pair in rights for each in pair]:
        array, place = item if isinstance(item, tuple) else (item, None)
        shape = array.shape[-2:]
        if place is None:
            specs.append(pl.BlockSpec(shape, lambda i: (0, 0)))
        else:
            specs.append(pl.BlockSpec((1,) + shape, lambda i, p=place: (p, 0, 0)))
        operands.append(array)
        lead.append(place is not None)
        shapes.append(shape)
    depth = shapes[0][1]
    outs = []
    for place, dtype in enumerate(dtypes):
        width = shapes[2 + 2 * place][1]
        flops += 4 * shapes[0][0] * depth * width
        outs.append(jax.ShapeDtypeStruct((depth, width), dtype))
    return pl.pallas_call(
        functools.partial(turned_kernel, len(outs), lead),
        out_shape=outs,
        grid=(1,),
        in_specs=specs,
        out_specs=[pl.BlockSpec(out.shape, lambda i: (0, 0)) for out in outs],
        compiler_params=pltpu.CompilerParams(vmem_limit_bytes=VMEM_BYTES),
        cost_estimate=pl.CostEstimate(
            flops=flops, bytes_accessed=flops // 300, transcendentals=0
        ),
    )(*operands)


def expert_kernel(count, owner_ref, other_ref, own_ref, sent_ref, *refs):
    rows_refs, gate_refs = refs[:count], refs[count : 2 * count]
    up_refs, router_refs = refs[2 * count : 3 * count], refs[3 * count : 4 * count]
    act_ref, gate_out, up_out, logit_out = refs[4 * count :]
    gate_pre = up_pre = logits = None
    for index in range(count):
        rows = rows_refs[index][...]
        gate_part = jnp.dot(rows, gate_refs[index][...], preferred_element_type=F32)
        up_part = jnp.dot(rows, up_refs[index][...], preferred_element_type=F32)
        logit_part = jnp.dot(rows, router_refs[index][...], preferred_element_type=F32)
        gate_pre = gate_part if index == 0 else gate_pre + gate_part
        up_pre = up_part if index == 0 else up_pre + up_part
        logits = logit_part if index == 0 else logits + logit_part
    lane = lax.broadcasted_iota(jnp.int32, logits.shape, 1)
    signs = (lane == owner_ref[0]).astype(F32) - (lane == other_ref[...]).astype(F32)
    gate = jax.nn.sigmoid(jnp.sum(logits * signs, axis=1, keepdims=True))
    grad_act = own_ref[...] + sent_ref[...].astype(F32)
    sigmoid_gate = jax.nn.sigmoid(gate_pre)
    swish_gate = gate_pre * sigmoid_gate
    activation = swish_gate * up_pre
    act_ref[...] = (activation * gate).astype(BF)
    share = jnp.sum(grad_act * activation, axis=1, keepdims=True) * gate * (1.0 - gate)
    logit_out[...] = (share * signs).astype(BF)
    grad_activation = grad_act * gate
    swish_slope = sigmoid_gate * (1.0 + gate_pre * (1.0 - sigmoid_gate))
    gate_out[...] = (grad_activation * up_pre * swish_slope).astype(BF)
    up_out[...] = (grad_activation * swish_gate).astype(BF)


def expert_forward(owner, other, own, sent, rows, gates, ups, routers):
    slots, depth = rows[0].shape
    hidden = gates[0].shape[1]
    lanes = routers[0].shape[1]
    tile = slots // 2 if slots % 32 == 0 else slots
    row_spec = lambda width: pl.BlockSpec((tile, width), lambda i, s: (i, 0))
    whole = lambda array: pl.BlockSpec(array.shape, lambda i, s: (0, 0))
    out_shapes = [jax.ShapeDtypeStruct((slots, hidden), BF)] * 3
    out_shapes.append(jax.ShapeDtypeStruct((slots, lanes), BF))
    return pl.pallas_call(
        functools.partial(expert_kernel, len(rows)),
        out_shape=out_shapes,
        grid_spec=pltpu.PrefetchScalarGridSpec(
            num_scalar_prefetch=1,
            grid=(slots // tile,),
            in_specs=[row_spec(1), row_spec(hidden), row_spec(hidden)]
            + [row_spec(depth) for _ in rows]
            + [whole(item) for item in list(gates) + list(ups) + list(routers)],
            out_specs=[row_spec(item.shape[1]) for item in out_shapes],
        ),
        compiler_params=pltpu.CompilerParams(vmem_limit_bytes=VMEM_BYTES),
        cost_estimate=pl.CostEstimate(
            flops=4 * len(rows) * slots * depth * hidden,
            bytes_accessed=4 * len(rows) * depth * hidden + 12 * slots * hidden,
            transcendentals=slots * hidden,
        ),
    )(owner.reshape(1), other, own, sent, *rows, *gates, *ups, *routers)


def assemble_kernel(blocks_ref, *refs):
    for block, ref in enumerate(refs[:-1]):

        @pl.when(pl.program_id(0) == block)
        def _():
            refs[-1][0] = ref[...].astype(F32)


def assemble(order, blocks):
    count = len(blocks)
    rows, width = blocks[0].shape
    tiles = 2 if rows % 32 == 0 else 1

    def spec(place):
        return pl.BlockSpec(
            (rows // tiles, width),
            lambda b, i, s: (jnp.where(b == place, i, jnp.where(b < place, 0, tiles - 1)), 0),
        )

    return pl.pallas_call(
        assemble_kernel,
        out_shape=jax.ShapeDtypeStruct((count, rows, width), F32),
        grid_spec=pltpu.PrefetchScalarGridSpec(
            num_scalar_prefetch=1,
            grid=(count, tiles),
            in_specs=[spec(place) for place in range(count)],
            out_specs=pl.BlockSpec(
                (1, rows // tiles, width), lambda b, i, s: (s[b], i, 0)
            ),
        ),
        compiler_params=pltpu.CompilerParams(vmem_limit_bytes=VMEM_BYTES),
        cost_estimate=pl.CostEstimate(
            flops=0, bytes_accessed=7 * count * rows * width, transcendentals=0
        ),
    )(order, *blocks)


def allowed_keys(row_segments, column_segments):
    length = row_segments.shape[0]
    query = lax.broadcasted_iota(jnp.int32, (length, length), 0)
    key = lax.broadcasted_iota(jnp.int32, (length, length), 1)
    same = (column_segments == 0) | (column_segments == row_segments)
    return same & (key <= query)


def weights_of(query, key, allowed):
    scores = lax.dot_general(query, key, (((1,), (1,)), ((), ())), preferred_element_type=F32)
    scores = jnp.where(allowed, scores * HD ** (-0.5), NEGATIVE)
    weights = jnp.exp(scores - jnp.max(scores, axis=1, keepdims=True))
    return weights / jnp.sum(weights, axis=1, keepdims=True)


def attend_kernel(gates_ref, rows_ref, columns_ref, cos_ref, sin_ref, *refs):
    parts, (saved_ref, mixed_ref, gated_ref) = refs[:12], refs[12:]
    summed = [
        parts[place][...].astype(F32)
        + parts[4 + place][...].astype(F32)
        + parts[8 + place][...].astype(F32)
        for place in range(4)
    ]
    cosine, sine = cos_ref[...], sin_ref[...]
    turned = [
        (item * cosine + pltpu.roll(item, HD // 2, 1) * sine).astype(BF) for item in summed[:3]
    ]
    turned.append(summed[3].astype(BF))
    for place in range(4):
        saved_ref[place] = turned[place]
    allowed = allowed_keys(rows_ref[...], columns_ref[...])
    for place in range(2):
        probs = weights_of(turned[place], turned[2], allowed).astype(BF)
        mixed = jnp.dot(probs, turned[3], preferred_element_type=F32)
        mixed_ref[place] = mixed
        gated_ref[place] = (mixed * gates_ref[:, place : place + 1]).astype(BF)


def attend(gates, segments, cosine, sine, parts):
    length = gates.shape[0]
    heads = parts[0].shape[1] // (4 * HD)
    whole = lambda array: pl.BlockSpec(array.shape, lambda h: (0, 0))
    part_specs = [
        pl.BlockSpec((length, HD), lambda h, p=place: (0, p * heads + h))
        for _ in parts
        for place in range(4)
    ]
    small = [gates, segments.reshape(length, 1), segments.reshape(1, length), cosine, sine]
    return pl.pallas_call(
        attend_kernel,
        out_shape=[
            jax.ShapeDtypeStruct((4, length, heads * HD), BF),
            jax.ShapeDtypeStruct((2, length, heads * HD), F32),
            jax.ShapeDtypeStruct((2, length, heads * HD), BF),
        ],
        grid=(heads,),
        in_specs=[whole(item) for item in small] + part_specs,
        out_specs=[
            pl.BlockSpec((count, length, HD), lambda h: (0, 0, h)) for count in (4, 2, 2)
        ],
        compiler_params=pltpu.CompilerParams(vmem_limit_bytes=VMEM_BYTES),
        cost_estimate=pl.CostEstimate(
            flops=16 * heads * length * length * HD,
            bytes_accessed=12 * length * heads * HD * 4,
            transcendentals=2 * heads * length * length,
        ),
    )(*small, *[part for part in parts for _ in range(4)])


def attend_back_kernel(
    gates_ref, rows_ref, columns_ref, cos_ref, sin_ref, saved_ref, mixed_ref, *refs
):
    parts, (out_ref, share_ref) = refs[:6], refs[6:]
    allowed = allowed_keys(rows_ref[...], columns_ref[...])
    key, value = saved_ref[2], saved_ref[3]
    cosine, sine = cos_ref[...], sin_ref[...]
    scale = HD ** (-0.5)
    over_rows = (((0,), (0,)), ((), ()))
    over_last = (((1,), (1,)), ((), ()))

    def unturn(item):
        return (item * cosine - pltpu.roll(item, HD // 2, 1) * sine).astype(BF)

    @pl.when(pl.program_id(0) == 0)
    def _():
        share_ref[...] = jnp.zeros(share_ref.shape, F32)

    grad_key = grad_value = 0.0
    for place in range(2):
        grad = (
            parts[place][...].astype(F32)
            + parts[2 + place][...].astype(F32)
            + parts[4 + place][...].astype(F32)
        )
        share_ref[place] += jnp.sum(grad * mixed_ref[place], axis=1, keepdims=True)
        grad = (grad * gates_ref[:, place : place + 1]).astype(BF)
        query = saved_ref[place]
        probs = weights_of(query, key, allowed)
        grad_value += lax.dot_general(
            probs.astype(BF), grad, over_rows, preferred_element_type=F32
        )
        grad_probs = lax.dot_general(grad, value, over_last, preferred_element_type=F32)
        centred = jnp.sum(probs * grad_probs, axis=1, keepdims=True)
        grad_scores = (probs * (grad_probs - centred)).astype(BF)
        grad_query = jnp.dot(grad_scores, key, preferred_element_type=F32) * scale
        out_ref[place] = unturn(grad_query)
        grad_key += lax.dot_general(
            grad_scores, query, over_rows, preferred_element_type=F32
        )
    out_ref[2] = unturn(grad_key * scale)
    out_ref[3] = grad_value.astype(BF)


def attend_back(gates, segments, cosine, sine, saved, mixed, parts):
    length = gates.shape[0]
    heads = saved.shape[2] // HD
    whole = lambda array: pl.BlockSpec(array.shape, lambda h: (0, 0))
    part_specs = [
        pl.BlockSpec((length, HD), lambda h, p=place: (0, p * heads + h))
        for _ in parts
        for place in range(2)
    ]
    small = [gates, segments.reshape(length, 1), segments.reshape(1, length), cosine, sine]
    return pl.pallas_call(
        attend_back_kernel,
        out_shape=[
            jax.ShapeDtypeStruct((4, length, heads * HD), BF),
            jax.ShapeDtypeStruct((2, length, 1), F32),
        ],
        grid=(heads,),
        in_specs=[whole(item) for item in small]
        + [pl.BlockSpec((count, length, HD), lambda h: (0, 0, h)) for count in (4, 2)]
        + part_specs,
        out_specs=[
            pl.BlockSpec((4, length, HD), lambda h: (0, 0, h)),
            pl.BlockSpec((2, length, 1), lambda h: (0, 0, 0)),
        ],
        compiler_params=pltpu.CompilerParams(vmem_limit_bytes=VMEM_BYTES),
        cost_estimate=pl.CostEstimate(
            flops=40 * heads * length * length * HD,
            bytes_accessed=20 * length * heads * HD * 4,
            transcendentals=2 * heads * length * length,
        ),
    )(*small, saved, mixed, *[part for part in parts for _ in range(2)])


def swap(value, axes, bits, size):
    if bits == 0:
        return value
    return lax.ppermute(value, axes, [(i, i ^ bits) for i in range(size)])


def row_gather(values):
    return lax.all_gather(values, "row", axis=0, tiled=True)


def row_total(values):
    return lax.psum_scatter(values, "row", scatter_dimension=0, tiled=True).astype(F32)


def col_total(values):
    return lax.psum(values, "col")


def small_total(value, axes):
    for axis in axes:
        size = lax.axis_size(axis)
        bits = 1
        while bits < size:
            value = value + swap(value, axis, bits, size)
            bits *= 2
    return value


def norm_factor(rows_in):
    squares = col_total(jnp.sum(rows_in * rows_in, axis=1))
    return lax.rsqrt(squares / D + EPSILON)


def norm_backward(rows_in, factor, gain_row, grad_in):
    scaled = grad_in * gain_row
    inner_sum = col_total(jnp.sum(scaled * rows_in, axis=1))[:, None]
    gain_grad = jnp.sum(grad_in * rows_in * factor, axis=0)
    return (factor * scaled - rows_in * factor**3 * inner_sum / D, gain_grad)


def local(
    hidden_in,
    gain_attn,
    router_attn,
    query_weight,
    kv_weight,
    out_weight,
    gain_ffn,
    router_ffn,
    gate_weight,
    up_weight,
    down_weight,
    attn_routes,
    ffn_routes,
    attn_order,
    ffn_order,
    segment_ids,
    d_out,
):
    dp_count, col_count = lax.axis_size("dp"), lax.axis_size("col")
    dp_index, col_index = lax.axis_index("dp"), lax.axis_index("col")
    owners = dp_count * col_count
    owner = dp_index * col_count + col_index
    batch_rows = attn_routes.shape[0]
    group_rows = batch_rows // col_count
    features = hidden_in.shape[1]
    attn_experts = query_weight.shape[0]
    ffn_experts = gate_weight.shape[0]
    half_experts = attn_experts // dp_count
    attn_capacity = 5 * batch_rows // (2 * attn_experts)
    slots = 5 * batch_rows // (2 * ffn_experts)
    head_width = query_weight.shape[2]
    pair_axes = ("dp", "col")

    def at_owner(array, bits):
        return lax.dynamic_index_in_dim(array, owner ^ bits, 0, keepdims=False)

    def expert_weight(weight, *waits):
        blocks = {bits: at_owner(weight, bits) for bits in (2, 3, 1, 0)}
        for bits in blocks:
            block = after(blocks[bits], *waits) if waits else blocks[bits]
            blocks[bits] = swap(block, "col", bits, col_count)
        return [blocks[bits] for bits in range(col_count)]

    def col_gather(block, axis):
        blocks = {0: block, 2: swap(block, "col", 2, col_count)}
        blocks[1] = swap(block, "col", 1, col_count)
        blocks[3] = swap(blocks[2], "col", 1, col_count)
        shape = list(block.shape)
        shape[axis] *= col_count
        result = jnp.zeros(shape, block.dtype)
        for bits in (0, 1, 2, 3):
            start = (col_index ^ bits) * block.shape[axis]
            result = lax.dynamic_update_slice_in_dim(result, blocks[bits], start, axis)
        return result

    hidden_all = row_gather(hidden_in)
    gate_blocks = expert_weight(gate_weight)
    rows_in = hidden_in.astype(F32)
    factor_a = norm_factor(rows_in)
    factor_a_all = row_gather(factor_a)
    attn_order, ffn_order = lax.optimization_barrier((attn_order, ffn_order, factor_a_all))[:2]

    lane_router_f = jnp.pad(router_ffn, ((0, 0), (0, 128 - ffn_experts)))
    router_blocks = [swap(lane_router_f, "col", bits, col_count) for bits in range(col_count)]

    offsets = owner ^ jnp.arange(owners, dtype=jnp.int32)
    ffn_kept = kept_pairs(ffn_routes, ffn_order[0], ffn_experts, slots)
    owner_places, owner_starts = token_slots(ffn_routes, ffn_kept, offsets, slots)
    owner_starts, owner_rows = owner_starts.T, owner_places.T
    hidden_all, owner_rows, owner_starts, owner_places = lax.optimization_barrier(
        (hidden_all, owner_rows, owner_starts, owner_places, gate_blocks[2])
    )[:4]
    grad_out_all = row_gather(after(d_out, hidden_all))

    gain_a = gain_attn.astype(F32)
    normed_all = (hidden_all.astype(F32) * factor_a_all[:, None] * gain_a).astype(BF)
    near_blocks = jnp.stack([col_index, col_index ^ 1]).astype(jnp.int32)
    far_blocks = jnp.stack([col_index ^ 2, col_index ^ 3]).astype(jnp.int32)

    def col_scatter(rows, weight, extra_weight, transposed, waits):
        def part(blocks, rows):
            kept, sent = pick_matmul(
                blocks, attn_routes, rows, weight, extra_weight, group_rows, transposed
            )
            return kept, swap(sent, "col", 1, col_count)

        kept, received = part(far_blocks, rows)
        far = (kept.astype(F32) + received.astype(F32)).astype(BF)
        far = swap(after(far, *waits), "col", 2, col_count)
        kept, received = part(near_blocks, after(rows, received))
        return [kept, received, far]

    def group_block(array, bits, axis):
        start = (col_index ^ bits) * group_rows
        return lax.dynamic_slice_in_dim(array, start, group_rows, axis)

    logits_all = lax.dot_general(
        router_attn, normed_all, (((0,), (1,)), ((), ())), preferred_element_type=F32
    )
    logits_a = sum(
        swap(group_block(logits_all, bits, 1), "col", bits, col_count)
        for bits in range(col_count)
    )
    projected = col_scatter(
        normed_all, query_weight, kv_weight, False, [logits_a] + gate_blocks[1:]
    )
    attn_order = after(attn_order, projected[1])
    attn_kept = kept_pairs(attn_routes, attn_order[0], attn_experts, attn_capacity)
    kept_a = group_block(attn_kept, 0, 0).astype(F32)
    routes_a = group_block(attn_routes, 0, 0)
    member_a = (
        routes_a[:, :, None] == jnp.arange(attn_experts, dtype=jnp.int32)[None, None, :]
    ).astype(F32)
    gate_a = jax.nn.softmax(jnp.sum(member_a * logits_a.T[:, None, :], axis=2), axis=1)
    scaled_a = gate_a * kept_a
    cosine, sine_rows = rope_tables(segment_ids)
    segments = segment_ids.reshape(-1)

    half_bits = (0, 1, col_count, col_count + 1)
    grad_groups = spread_rows(
        owner_starts,
        owner_rows,
        after(grad_out_all, projected[1]),
        slots,
        [(bits, bits ^ 2) for bits in half_bits],
    )
    route_sums = jnp.sum(ffn_routes, axis=1).astype(BF)
    route_sums = jnp.broadcast_to(route_sums[:, None], (batch_rows, 128))
    near_sums, far_sums = spread_rows(
        owner_starts, owner_rows, route_sums, slots, [(0,), (col_count,)]
    )
    far_sums = swap(far_sums[:, 0:8], pair_axes, col_count, owners)
    slot_other = [item[:, 0:1].astype(jnp.int32) - owner for item in (near_sums, far_sums)]
    grad_pairs = [
        swap(group, pair_axes, bits, owners) for bits, group in zip(half_bits, grad_groups)
    ]
    down_pairs = [
        swap(
            jnp.stack([at_owner(down_weight, bits), at_owner(down_weight, bits ^ 2)]),
            "col",
            bits,
            col_count,
        )
        for bits in (0, 1)
    ]
    scaled_a, cosine, sine_rows = lax.optimization_barrier(
        (scaled_a, cosine, sine_rows, *grad_groups, *slot_other)
    )[:3]
    saved, attended, gated_out = attend(scaled_a, segments, cosine, sine_rows, projected)
    gated_all = col_gather(gated_out, 1)
    up_blocks = expert_weight(up_weight, gated_all)
    attn_part = merge_matmul(attn_routes, gated_all, out_weight, (), False)

    def grad_act_part(batch, lead, dtype):
        return dots(
            [(grad_pairs[2 * batch + near], lead) for near in (0, 1)],
            [[(down_pairs[near], lead) for near in (0, 1)]],
            True,
            dtype,
        )[0]

    grad_pairs = [after(pair, gated_all) for pair in grad_pairs]
    grad_act_out = [grad_act_part(batch, 1, BF) for batch in (0, 1)]
    attn_sum = row_total(attn_part)
    attn_sum = after(attn_sum, up_blocks[2], *grad_act_out)
    grad_act_sent = [swap(part, "col", 2, col_count) for part in grad_act_out]
    grad_act_own = [grad_act_part(batch, 0, F32) for batch in (0, 1)]
    middle = rows_in + attn_sum

    gain_f = gain_ffn.astype(F32)
    factor_f = norm_factor(middle)[:, None]
    normed_f = (middle * factor_f * gain_f).astype(BF)
    normed_f_all = row_gather(normed_f)
    normed_f_all = after(normed_f_all, up_blocks[3], grad_act_sent[0], *grad_act_own)
    order = [(2,), (3,), (6,), (7,)], [(4,), (5,), (1,), (0,)]
    slots_f = {}
    for part in order:
        blocks = spread_rows(owner_starts, owner_rows, normed_f_all, slots, part)
        for group, block in zip(part, blocks):
            slots_f[group[0]] = swap(block, pair_axes, group[0], owners)
        normed_f_all = after(normed_f_all, *blocks)
    acts, grad_gates, grad_ups, grad_logits = [], [], [], []
    for batch in (0, 1):
        act, grad_gate, grad_up, grad_logit = expert_forward(
            owner.astype(jnp.int32),
            slot_other[batch],
            grad_act_own[batch],
            grad_act_sent[batch],
            [slots_f[batch * col_count + bits] for bits in range(col_count)],
            gate_blocks,
            up_blocks,
            router_blocks,
        )
        acts.append(act)
        grad_gates.append(grad_gate)
        grad_ups.append(grad_up)
        grad_logits.append(grad_logit)

    back_blocks = {}
    for pair in ((2, 3), (6, 7), (4, 5), (1, 0)):
        batch = pair[0] // col_count
        blocks = dots(
            [grad_gates[batch], grad_ups[batch], grad_logits[batch]],
            [
                [gate_blocks[bits % col_count], up_blocks[bits % col_count], router_blocks[bits % col_count]]
                for bits in pair
            ],
            True,
            BF,
        )
        for bits, block in zip(pair, blocks):
            back_blocks[bits] = swap(block, pair_axes, bits, owners)
    back_sent = blocks[0]

    gate_grads, up_grads, router_parts = {}, {}, {}
    for bits in (2, 3, 1, 0):
        dtype = BF if bits else F32
        gate_part, up_part, router_part = turned_dots(
            [after(slots_f[bits], back_sent), slots_f[bits + col_count]],
            [grad_gates, grad_ups, grad_logits],
            [dtype, dtype, F32],
        )
        gate_grads[bits], up_grads[bits] = gate_part, up_part
        router_parts[bits] = router_part[:, :ffn_experts].T
    back_blocks = [after(back_blocks[bits], *gate_grads.values()) for bits in range(owners)]
    grad_normed_f_part = gather_slots(owner_starts, owner_places, back_blocks)

    acts = [after(act, grad_normed_f_part) for act in acts]
    act_pairs = [(act, swap(act, "col", 2, col_count)) for act in acts]
    grad_normed_f = row_total(grad_normed_f_part)
    grad_normed_f = after(grad_normed_f, act_pairs[0][1])

    middle_norm_grad, gain_ffn_grad = norm_backward(middle, factor_f, gain_f, grad_normed_f)
    grad_middle = d_out.astype(F32) + middle_norm_grad
    grad_middle_all = row_gather(grad_middle.astype(BF))
    gate_grads = {
        bits: swap(after(gate_grads[bits], act_pairs[1][1]), "col", bits, col_count)
        for bits in (2, 3, 1, 0)
    }
    grad_middle_all = after(grad_middle_all, act_pairs[1][1])

    grad_gated = col_scatter(grad_middle_all, out_weight, None, True, [gate_grads[2]])

    down_blocks = {}
    for slot, bits in enumerate(half_bits):
        pair = jnp.stack(
            [
                jnp.dot(
                    act_pairs[slot // 2][lead],
                    down_pairs[slot % 2][lead],
                    preferred_element_type=F32,
                ).astype(BF)
                for lead in (0, 1)
            ]
        )
        pair = swap(pair, pair_axes, bits, owners)
        down_blocks[bits], down_blocks[bits ^ 2] = pair[0], pair[1]

    pieces, shares = attend_back(
        scaled_a, segments, cosine, sine_rows, saved, attended, grad_gated
    )
    pieces_all = col_gather(pieces, 1)
    shares = shares[:, :, 0] * kept_a.T * (gate_a[:, 0] * gate_a[:, 1])
    grad_logits_a = (shares[0] - shares[1])[:, None] * (member_a[:, 0] - member_a[:, 1])
    grad_logits_a = jnp.pad(grad_logits_a, ((0, 0), (0, 128 - attn_experts))).astype(BF)
    logits_back = col_gather(grad_logits_a, 0)
    lane_router = jnp.pad(router_attn, ((0, 0), (0, 128 - attn_experts)))
    normed_part = merge_matmul(
        attn_routes, pieces_all, query_weight, (logits_back, kv_weight, lane_router), True
    )
    grad_normed = row_total(normed_part)
    input_norm_grad, gain_attn_grad = norm_backward(
        rows_in, factor_a[:, None], gain_a, grad_normed
    )
    input_grad = grad_middle + input_norm_grad

    ffn_part = gather_slots(
        owner_starts, owner_places, [down_blocks[bits] for bits in range(owners)]
    )
    layer_out = (middle + row_total(ffn_part)).astype(BF)
    down_near = [
        turned_dots(
            [act_pairs[0][lead], act_pairs[1][lead]],
            [[(grad_pairs[0], lead), (grad_pairs[2], lead)]],
            [F32],
        )[0]
        for lead in (0, 1)
    ]
    down_away = [
        swap(
            turned_dots(
                [act_pairs[0][lead], act_pairs[1][lead]],
                [[(grad_pairs[1], lead), (grad_pairs[3], lead)]],
                [BF],
            )[0],
            "col",
            1,
            col_count,
        )
        for lead in (0, 1)
    ]
    expert_order = (col_index ^ jnp.arange(col_count, dtype=jnp.int32)).astype(jnp.int32)
    down_grad = assemble(expert_order, [down_near[0], down_away[0], down_near[1], down_away[1]])
    gate_grad = assemble(expert_order, [gate_grads[bits] for bits in range(col_count)])
    up_grads = {
        bits: swap(after(up_grads[bits], pieces_all), "col", bits, col_count)
        for bits in (2, 3, 1, 0)
    }
    up_grad = assemble(expert_order, [up_grads[bits] for bits in range(col_count)])
    router_ffn_grad = sum(
        swap(router_parts[bits], "col", bits, col_count) for bits in range(col_count)
    )

    own_base = (dp_index * half_experts).astype(jnp.int32).reshape(1)
    away_base = ((1 - dp_index) * half_experts).astype(jnp.int32).reshape(1)

    def dp_grads(kernel, routes, left, rows, shape):
        away = expert_grads(kernel, away_base, half_experts, routes, left, rows, shape, BF)
        away = swap(away, "dp", 1, dp_count)
        own = expert_grads(kernel, own_base, half_experts, routes, left, rows, shape, F32)
        return own + away.astype(F32)

    out_grad = dp_grads(
        left_grad_kernel,
        attn_routes.T,
        jnp.swapaxes(gated_all, 1, 2),
        grad_middle_all,
        (head_width, features),
    )
    normed_turned = normed_all.T
    query_grad = dp_grads(
        right_grad_kernel, attn_routes, normed_turned, pieces_all[:2], (features, head_width)
    )
    kv_own = lax.dynamic_index_in_dim(pieces_all, 2 + dp_index, 0, keepdims=False)
    kv_away = lax.dynamic_index_in_dim(pieces_all, 3 - dp_index, 0, keepdims=False)
    kv_away = jnp.dot(normed_turned, kv_away, preferred_element_type=F32).astype(BF)
    kv_away = swap(kv_away, "dp", 1, dp_count).astype(F32)
    kv_grad = (jnp.dot(normed_turned, kv_own, preferred_element_type=F32) + kv_away)[None]
    router_attn_grad = jnp.dot(normed_turned, logits_back, preferred_element_type=F32)
    router_attn_grad = router_attn_grad[:, :attn_experts].T
    ffn_small = jnp.concatenate([router_ffn_grad, gain_ffn_grad[None]], axis=0)
    ffn_small = small_total(ffn_small, ("row", "dp"))
    router_attn_grad = small_total(router_attn_grad, ("row", "dp"))
    gain_attn_grad = small_total(gain_attn_grad, ("row", "dp"))
    gain_ffn_grad = ffn_small[ffn_experts]
    router_attn_grad = lax.dynamic_slice_in_dim(
        router_attn_grad, dp_index * half_experts, half_experts, 0
    ).T
    ffn_half = ffn_experts // dp_count
    router_ffn_grad = lax.dynamic_slice_in_dim(ffn_small, dp_index * ffn_half, ffn_half, 0).T
    return (
        layer_out,
        input_grad,
        gain_attn_grad,
        router_attn_grad,
        query_grad,
        kv_grad,
        out_grad,
        gain_ffn_grad,
        router_ffn_grad,
        gate_grad,
        up_grad,
        down_grad,
    )


def solution(mesh):
    in_specs = (
        P(("dp", "row"), "col"),
        P("col"),
        P("col", None),
        P(None, "col", "row"),
        P(None, "col", "row"),
        P(None, "row", "col"),
        P("col"),
        P("col", None),
        P(None, "col", "row"),
        P(None, "col", "row"),
        P(None, "row", "col"),
        P("dp", None),
        P("dp", None),
        P("dp", None),
        P("dp", None),
        P(("dp", "col"), None),
        P(("dp", "row"), "col"),
    )
    out_specs = (
        P(("dp", "row"), "col"),
        P(("dp", "row"), "col"),
        P("col"),
        P("col", "dp"),
        P("dp", "col", "row"),
        P("dp", "col", "row"),
        P("dp", "row", "col"),
        P("col"),
        P("col", "dp"),
        P("dp", "col", "row"),
        P("dp", "col", "row"),
        P("dp", "row", "col"),
    )
    return jax.shard_map(local, mesh=mesh, in_specs=in_specs, out_specs=out_specs, check_vma=False)
```

```python
import functools
import math

import jax
import jax.numpy as jnp
from jax import lax
from jax.experimental import pallas as pl
from jax.experimental.pallas import tpu as pltpu
from jax.sharding import PartitionSpec as P

D = 2048
HD = 128
SEQ = 512

EPSILON = 1e-06
NEGATIVE = -1e30
VMEM_BYTES = 56 * 1024 * 1024
TILE = 128
WINDOW = TILE + 16
COST = 1 << 20
ASSEMBLE = 2
BF = jnp.bfloat16
F32 = jnp.float32


def cost(flops, size, scale=COST):
    return pl.CostEstimate(flops=flops // scale, bytes_accessed=size // scale, transcendentals=0)


def after(value, *others):
    return lax.optimization_barrier((value,) + others)[0]


def rope_lines(row_segments, column_segments):
    length = row_segments.shape[0]
    query = lax.broadcasted_iota(jnp.int32, (length, length), 0)
    key = lax.broadcasted_iota(jnp.int32, (length, length), 1)
    before = (column_segments == row_segments) & (key < query)
    within = jnp.sum(before.astype(F32), axis=1, keepdims=True)
    prompt = jnp.sum((column_segments == 0).astype(F32), axis=1, keepdims=True)
    places = within + jnp.where(row_segments > 0, prompt, 0.0)
    lane = lax.broadcasted_iota(jnp.int32, (1, HD), 1)
    step = jnp.where(lane < HD // 2, lane, lane - HD // 2).astype(F32)
    frequency = jnp.exp(step * (-2.0 * math.log(10000.0) / HD))
    angles = places * frequency
    sine = jnp.sin(angles)
    return jnp.cos(angles), jnp.where(lane < HD // 2, -sine, sine)


def kept_table(capacity, experts, order_ref, table_ref, turned_ref):
    lines, lanes = table_ref.shape
    pairs = order_ref.shape[1]
    order = order_ref[...]
    token = order // 2
    line = (order % 2) * (lines // 2) + token // lanes
    high = (lax.broadcasted_iota(jnp.int32, (lines, pairs), 0) == line).astype(F32).astype(BF)
    low = lax.broadcasted_iota(jnp.int32, (lanes, pairs), 0) == token % lanes
    low = low.astype(F32).astype(BF)
    chosen = jnp.dot(turned_ref[...].astype(BF), high, preferred_element_type=F32)
    chosen = jnp.sum(chosen * low.astype(F32), axis=0, keepdims=True)
    label = lax.broadcasted_iota(jnp.int32, (experts, pairs), 0).astype(F32)
    member = (label == chosen).astype(F32)
    step = 256
    row = lax.broadcasted_iota(jnp.int32, (step, step), 0)
    upto = row <= lax.broadcasted_iota(jnp.int32, (step, step), 1)
    upto = upto.astype(F32).astype(BF)
    carry = jnp.zeros((experts, 1), F32)
    placed = []
    for start in range(0, pairs, step):
        part = member[:, start : start + step]
        count = jnp.dot(part.astype(BF), upto, preferred_element_type=F32) + carry
        carry = count[:, step - 1 : step]
        ranked = jnp.sum(count * part, axis=0, keepdims=True)
        placed.append((ranked <= capacity).astype(F32))
    placed = jnp.concatenate(placed, axis=1)
    return lax.dot_general(
        high * placed.astype(BF), low, (((1,), (1,)), ((), ())), preferred_element_type=F32
    )


def kept_kernel(capacity, experts, order_ref, table_ref, turned_ref, kept_ref):
    kept_ref[...] = kept_table(capacity, experts, order_ref, table_ref, turned_ref)


def slots_kernel(
    capacity, experts, labels_ref, order_ref, table_ref, turned_ref, places_ref, starts_ref
):
    kept = kept_table(capacity, experts, order_ref, table_ref, turned_ref)
    lines, lanes = table_ref.shape
    tiles = lines // 2
    row = lax.broadcasted_iota(jnp.int32, (lanes, lanes), 0)
    upto = (row <= lax.broadcasted_iota(jnp.int32, (lanes, lanes), 1)).astype(F32).astype(BF)
    first = lax.broadcasted_iota(jnp.int32, (tiles, tiles), 0)
    second = lax.broadcasted_iota(jnp.int32, (tiles, tiles), 1)
    above = (second < first).astype(F32).astype(BF)
    before = (first < second).astype(F32).astype(BF)
    ones = jnp.ones((8, lanes), BF)
    table = table_ref[...]
    for place in range(places_ref.shape[0]):
        member = (table == labels_ref[place].astype(F32)).astype(F32) * kept
        member = member[:tiles] + member[tiles:]
        inside = jnp.dot(member.astype(BF), upto, preferred_element_type=F32)
        past = jnp.dot(above, inside.astype(BF), preferred_element_type=F32)
        count = inside + past[:, lanes - 1 : lanes]
        slot = (count * member - 1.0).astype(jnp.int32)
        for tile in range(tiles):
            places_ref[place : place + 1, tile * lanes : (tile + 1) * lanes] = slot[tile : tile + 1]
        sums = lax.dot_general(
            ones, member.astype(BF), (((1,), (1,)), ((), ())), preferred_element_type=F32
        )
        start = jnp.dot(sums.astype(BF), before, preferred_element_type=F32)[0:1]
        start = start.astype(jnp.int32) // 16 * 16
        starts_ref[place : place + 1, :] = jnp.minimum(start, capacity - WINDOW)


def route_table(routes):
    return routes.astype(F32).T.reshape(-1, TILE)


def kept_pairs(routes, pair_order, experts, capacity):
    table = route_table(routes)
    return pl.pallas_call(
        functools.partial(kept_kernel, capacity, experts),
        out_shape=jax.ShapeDtypeStruct(table.shape, F32),
        compiler_params=pltpu.CompilerParams(vmem_limit_bytes=VMEM_BYTES),
        cost_estimate=cost(0, 0),
    )(pair_order, table, table.T)


def token_slots(routes, pair_order, labels, experts, capacity):
    table = route_table(routes)
    whole = lambda array: pl.BlockSpec(array.shape, lambda i, s: (0, 0))
    tiles = table.shape[0] // 2
    shapes = [(labels.shape[0], routes.shape[0]), (labels.shape[0], tiles)]
    return pl.pallas_call(
        functools.partial(slots_kernel, capacity, experts),
        out_shape=[jax.ShapeDtypeStruct(shape, jnp.int32) for shape in shapes],
        grid_spec=pltpu.PrefetchScalarGridSpec(
            num_scalar_prefetch=1,
            grid=(1,),
            in_specs=[whole(pair_order), whole(table), whole(table.T)],
            out_specs=[pl.BlockSpec(shape, lambda i, s: (0, 0)) for shape in shapes],
        ),
        compiler_params=pltpu.CompilerParams(vmem_limit_bytes=VMEM_BYTES),
        cost_estimate=cost(0, 0),
    )(labels, pair_order, table, table.T)


def copy_kernel(index_ref, block_ref, o_ref):
    o_ref[...] = block_ref[...]


def take_blocks(array, index, start, step, count):
    shape = array.shape[1:]
    return pl.pallas_call(
        copy_kernel,
        out_shape=jax.ShapeDtypeStruct((count,) + shape, array.dtype),
        grid_spec=pltpu.PrefetchScalarGridSpec(
            num_scalar_prefetch=1,
            grid=(count,),
            in_specs=[pl.BlockSpec((1,) + shape, lambda i, s: (s[start + step * i], 0, 0))],
            out_specs=pl.BlockSpec((1,) + shape, lambda i, s: (i, 0, 0)),
        ),
        compiler_params=pltpu.CompilerParams(vmem_limit_bytes=VMEM_BYTES),
        cost_estimate=cost(0, 0),
    )(index, array)


def lead_block(array, place):
    shape = (1,) + array.shape[1:]
    return pl.pallas_call(
        lead_kernel,
        out_shape=jax.ShapeDtypeStruct(shape, array.dtype),
        grid=(1,),
        in_specs=[pl.BlockSpec(shape, lambda i: (place, 0, 0))],
        out_specs=pl.BlockSpec(shape, lambda i: (0, 0, 0)),
        compiler_params=pltpu.CompilerParams(vmem_limit_bytes=VMEM_BYTES),
        cost_estimate=cost(0, 0),
    )(array)


def lead_kernel(block_ref, o_ref):
    o_ref[...] = block_ref[...]


def join_kernel(kept_ref, *refs):
    o_ref = refs[-1]
    start = 0
    for ref in refs[:-1]:
        span = slice(start, start + ref.shape[1])
        o_ref[:, span] = (kept_ref[:, span].astype(F32) + ref[...].astype(F32)).astype(BF)
        start += ref.shape[1]


def join_halves(kept, halves):
    rows, width = kept.shape
    tile = rows // 4 if rows % 64 == 0 else rows
    spec = lambda array: pl.BlockSpec((tile, array.shape[1]), lambda i: (i, 0))
    return pl.pallas_call(
        join_kernel,
        out_shape=jax.ShapeDtypeStruct(kept.shape, BF),
        grid=(rows // tile,),
        in_specs=[spec(kept)] + [spec(half) for half in halves],
        out_specs=spec(kept),
        compiler_params=pltpu.CompilerParams(vmem_limit_bytes=VMEM_BYTES),
        cost_estimate=cost(0, 0),
    )(kept, *halves)


def tip_kernel(rows_ref, o_ref):
    o_ref[...] = rows_ref[...].astype(BF)


def tip(rows):
    lead = rows.ndim - 2
    block = (None,) * lead + (16, 128)
    return pl.pallas_call(
        tip_kernel,
        out_shape=jax.ShapeDtypeStruct((16, 128), BF),
        grid=(1,),
        in_specs=[pl.BlockSpec(block, lambda i: (0,) * rows.ndim)],
        out_specs=pl.BlockSpec((16, 128), lambda i: (0, 0)),
        compiler_params=pltpu.CompilerParams(vmem_limit_bytes=VMEM_BYTES),
        cost_estimate=cost(0, 0),
    )(rows)


def add_kernel(own_ref, away_ref, o_ref):
    o_ref[...] = own_ref[...] + away_ref[...].astype(F32)


def add_wide(own, away):
    spec = pl.BlockSpec((1,) + own.shape[1:], lambda i: (i, 0, 0))
    return pl.pallas_call(
        add_kernel,
        out_shape=jax.ShapeDtypeStruct(own.shape, F32),
        grid=(own.shape[0],),
        in_specs=[spec, spec],
        out_specs=spec,
        compiler_params=pltpu.CompilerParams(vmem_limit_bytes=VMEM_BYTES),
        cost_estimate=cost(0, 0),
    )(own, away)


def pick_kernel(extra, transposed, blocks_ref, routes_ref, x_ref, w_ref, *rest):
    outs = rest[-3:]
    rows = x_ref[...]
    experts = w_ref.shape[0]
    width = w_ref.shape[1] if transposed else w_ref.shape[2]
    contract = (((1,), (1 if transposed else 0,)), ((), ()))
    first = jnp.broadcast_to(routes_ref[:, 0:1], (rows.shape[0], width))
    second = jnp.broadcast_to(routes_ref[:, 1:2], (rows.shape[0], width))
    picked = [jnp.zeros((rows.shape[0], width), F32) for _ in range(2)]
    for expert in range(experts):
        product = lax.dot_general(rows, w_ref[expert], contract, preferred_element_type=F32)
        picked[0] = jnp.where(first == expert, product, picked[0])
        picked[1] = jnp.where(second == expert, product, picked[1])
    for place in range(extra):
        picked.append(
            lax.dot_general(rows, rest[0][place], contract, preferred_element_type=F32)
        )
    picked = [item.astype(BF) for item in picked]
    half = len(picked) // 2

    @pl.when(pl.program_id(0) == 0)
    def _():
        for place, item in enumerate(picked):
            outs[0][:, place * width : (place + 1) * width] = item

    @pl.when(pl.program_id(0) == 1)
    def _():
        for place, item in enumerate(picked):
            start = place % half * width
            outs[1 + place // half][:, start : start + width] = item


def pick_matmul(blocks, routes, rows, weight, extra_weight, block_rows, transposed, scale):
    experts = weight.shape[0]
    depth = rows.shape[1]
    width = weight.shape[1] if transposed else weight.shape[2]
    tile = min(256, block_rows)
    tiles = block_rows // tile
    extra = 0 if extra_weight is None else extra_weight.shape[0]
    total = (2 + extra) * width
    in_specs = [
        pl.BlockSpec((tile, 2), lambda b, i, s: (s[b] * tiles + i, 0)),
        pl.BlockSpec((tile, depth), lambda b, i, s: (s[b] * tiles + i, 0)),
        pl.BlockSpec(weight.shape, lambda b, i, s: (0, 0, 0)),
    ]
    operands = [routes, rows, weight]
    if extra:
        in_specs.append(pl.BlockSpec(extra_weight.shape, lambda b, i, s: (0, 0, 0)))
        operands.append(extra_weight)
    flops = 4 * block_rows * depth * width * (experts + extra)
    return pl.pallas_call(
        functools.partial(pick_kernel, extra, transposed),
        out_shape=[jax.ShapeDtypeStruct((block_rows, total), BF)]
        + [jax.ShapeDtypeStruct((block_rows, total // 2), BF)] * 2,
        grid_spec=pltpu.PrefetchScalarGridSpec(
            num_scalar_prefetch=1,
            grid=(2, tiles),
            in_specs=in_specs,
            out_specs=[
                pl.BlockSpec((tile, total), lambda b, i, s: (jnp.where(b == 0, i, tiles - 1), 0)),
            ]
            + [
                pl.BlockSpec((tile, total // 2), lambda b, i, s: (jnp.where(b == 0, 0, i), 0))
            ]
            * 2,
        ),
        compiler_params=pltpu.CompilerParams(vmem_limit_bytes=VMEM_BYTES),
        cost_estimate=cost(
            flops,
            2 * (weight.size + 2 * block_rows * (depth + total)),
            scale,
        ),
    )(blocks, *operands)


def logits_kernel(order_ref, rows_ref, router_ref, *outs):
    product = lax.dot_general(
        router_ref[...], rows_ref[...], (((0,), (1,)), ((), ())), preferred_element_type=F32
    )
    for block, o_ref in enumerate(outs):

        @pl.when(pl.program_id(0) == block)
        def _():
            o_ref[...] = product


def block_logits(order, rows, router, length):
    depth, experts = router.shape
    count = rows.shape[0] // length
    return pl.pallas_call(
        logits_kernel,
        out_shape=[jax.ShapeDtypeStruct((experts, length), F32)] * count,
        grid_spec=pltpu.PrefetchScalarGridSpec(
            num_scalar_prefetch=1,
            grid=(count,),
            in_specs=[
                pl.BlockSpec((length, depth), lambda i, s: (s[i], 0)),
                pl.BlockSpec((depth, experts), lambda i, s: (0, 0)),
            ],
            out_specs=[pl.BlockSpec((experts, length), lambda i, s: (0, 0))] * count,
        ),
        compiler_params=pltpu.CompilerParams(vmem_limit_bytes=VMEM_BYTES),
        cost_estimate=cost(0, 0),
    )(order, rows, router)


def mixed_rows(routes, rows, expert):
    first = (routes[:, 0:1] == expert).astype(F32).astype(BF)
    second = (routes[:, 1:2] == expert).astype(F32).astype(BF)
    return rows[0] * first + rows[1] * second


def merge_kernel(count, extra, transposed, blocks_ref, routes_ref, *refs):
    rows_refs, refs = refs[:count], refs[count:]
    logit_refs, refs = (refs[:count], refs[count:]) if extra else ((), refs)
    w_ref, o_ref, rows_ref = refs[0], refs[-3], refs[-2]
    logits_ref = refs[-1]
    for block in range(count):

        @pl.when(pl.program_id(0) == block)
        def _():
            rows_ref[...] = rows_refs[block][...]
            if extra:
                logits_ref[...] = logit_refs[block][...]

    experts = w_ref.shape[0]
    contract = (((1,), (1 if transposed else 0,)), ((), ()))
    routes = routes_ref[...]
    total = jnp.zeros(o_ref.shape, F32)
    for expert in range(experts):
        mixed = mixed_rows(routes, rows_ref, expert)
        total += lax.dot_general(mixed, w_ref[expert], contract, preferred_element_type=F32)
    if extra:
        pair_ref, router_ref = refs[1:3]
        for place in range(2):
            total += lax.dot_general(
                rows_ref[2 + place], pair_ref[place], contract, preferred_element_type=F32
            )
        total += lax.dot_general(
            logits_ref[...], router_ref[...], contract, preferred_element_type=F32
        )
    o_ref[...] = total.astype(o_ref.dtype)


def merge_matmul(order, routes, blocks, weight, extras, transposed):
    count = len(blocks)
    parts, length, width = blocks[0].shape
    depth = weight.shape[1] if transposed else weight.shape[2]
    tile = min(256, length)
    tiles = length // tile

    def own_tile(place):
        return lambda b, i: jnp.where(b == place, i, jnp.where(b < place, 0, tiles - 1))

    def rows_spec(place):
        index = own_tile(place)
        return pl.BlockSpec((parts, tile, width), lambda b, i, s: (0, index(b, i), 0))

    def logits_spec(place, lanes):
        index = own_tile(place)
        return pl.BlockSpec((tile, lanes), lambda b, i, s: (index(b, i), 0))

    in_specs = [pl.BlockSpec((tile, 2), lambda b, i, s: (s[b] * tiles + i, 0))]
    in_specs += [rows_spec(place) for place in range(count)]
    operands = [routes, *blocks]
    lanes = 128
    if extras:
        logit_blocks, pair, router = extras
        lanes = logit_blocks[0].shape[1]
        in_specs += [logits_spec(place, lanes) for place in range(count)]
        operands += logit_blocks
    in_specs.append(pl.BlockSpec(weight.shape, lambda b, i, s: (0, 0, 0)))
    operands.append(weight)
    if extras:
        in_specs.append(pl.BlockSpec(pair.shape, lambda b, i, s: (0, 0, 0)))
        in_specs.append(pl.BlockSpec(router.shape, lambda b, i, s: (0, 0)))
        operands += [pair, router]
    return pl.pallas_call(
        functools.partial(merge_kernel, count, bool(extras), transposed),
        out_shape=jax.ShapeDtypeStruct((count * length, depth), BF),
        grid_spec=pltpu.PrefetchScalarGridSpec(
            num_scalar_prefetch=1,
            grid=(count, tiles),
            in_specs=in_specs,
            out_specs=pl.BlockSpec((tile, depth), lambda b, i, s: (s[b] * tiles + i, 0)),
            scratch_shapes=[pltpu.VMEM((parts, tile, width), BF), pltpu.VMEM((tile, lanes), BF)],
        ),
        compiler_params=pltpu.CompilerParams(vmem_limit_bytes=VMEM_BYTES),
        cost_estimate=cost(
            2 * count * length * depth * width * (weight.shape[0] + 2 * bool(extras)),
            2 * (weight.size + count * length * (parts * width + depth)),
        ),
    )(order, *operands)


def right_grad_kernel(scalars_ref, routes_ref, left_ref, *refs):
    blocks, o_ref = refs[:-1], refs[-1]
    expert = scalars_ref[len(blocks)] + pl.program_id(0)
    total = None
    for place, block_ref in enumerate(blocks):
        length = block_ref.shape[1]
        span = pl.ds(pl.multiple_of(scalars_ref[place] * length, length), length)
        mixed = mixed_rows(routes_ref[span, :], block_ref, expert)
        product = jnp.dot(left_ref[:, span], mixed, preferred_element_type=F32)
        total = product if total is None else total + product
    o_ref[0] = total.astype(o_ref.dtype)


def left_grad_kernel(scalars_ref, routes_ref, rows_ref, *refs):
    blocks, o_ref = refs[:-1], refs[-1]
    expert = scalars_ref[len(blocks)] + pl.program_id(0)
    total = None
    for place, block_ref in enumerate(blocks):
        length = block_ref.shape[2]
        span = pl.ds(pl.multiple_of(scalars_ref[place] * length, length), length)
        first = (routes_ref[0:1, span] == expert).astype(F32).astype(BF)
        second = (routes_ref[1:2, span] == expert).astype(F32).astype(BF)
        mixed = block_ref[0] * first + block_ref[1] * second
        product = jnp.dot(mixed, rows_ref[span, :], preferred_element_type=F32)
        total = product if total is None else total + product
    o_ref[0] = total.astype(o_ref.dtype)


def expert_grads(kernel, order, base, count, routes, rows, blocks, shape, dtype):
    whole = lambda array: pl.BlockSpec(array.shape, lambda i, s: (0,) * array.ndim)
    scalars = jnp.concatenate([order, base.astype(jnp.int32).reshape(1)])
    tokens = len(blocks) * blocks[0].shape[1]
    return pl.pallas_call(
        kernel,
        out_shape=jax.ShapeDtypeStruct((count,) + shape, dtype),
        grid_spec=pltpu.PrefetchScalarGridSpec(
            num_scalar_prefetch=1,
            grid=(count,),
            in_specs=[whole(routes), whole(rows)]
            + [pl.BlockSpec((2,) + item.shape[1:], lambda i, s: (0, 0, 0)) for item in blocks],
            out_specs=pl.BlockSpec((1,) + shape, lambda i, s: (i, 0, 0)),
        ),
        compiler_params=pltpu.CompilerParams(vmem_limit_bytes=VMEM_BYTES),
        cost_estimate=cost(
            2 * count * shape[0] * shape[1] * tokens,
            2 * rows.size + 4 * tokens * shape[1] + 4 * count * shape[0] * shape[1],
        ),
    )(scalars, routes, rows, *blocks)


def plain_grad_kernel(scalars_ref, left_ref, *refs):
    blocks, o_ref = refs[:-1], refs[-1]
    total = None
    for place, block_ref in enumerate(blocks):
        length = block_ref.shape[1]
        span = pl.ds(pl.multiple_of(scalars_ref[place] * length, length), length)
        if len(o_ref.shape) == 2:
            product = lax.dot_general(
                block_ref[0], left_ref[:, span], (((0,), (1,)), ((), ())),
                preferred_element_type=F32,
            )[: o_ref.shape[0]]
        else:
            product = jnp.dot(left_ref[:, span], block_ref[0], preferred_element_type=F32)
        total = product if total is None else total + product
    o_ref[...] = total.astype(o_ref.dtype).reshape(o_ref.shape)


def plain_grad(order, part, left, blocks, dtype, lines=0):
    depth = left.shape[0]
    _, length, width = blocks[0].shape
    scalars = jnp.concatenate([order, jnp.asarray(part, jnp.int32).reshape(1)])
    count = len(blocks)
    shape = (lines, depth) if lines else (1, depth, width)
    return pl.pallas_call(
        plain_grad_kernel,
        out_shape=jax.ShapeDtypeStruct(shape, dtype),
        grid_spec=pltpu.PrefetchScalarGridSpec(
            num_scalar_prefetch=1,
            grid=(1,),
            in_specs=[pl.BlockSpec(left.shape, lambda i, s: (0, 0))]
            + [pl.BlockSpec((1, length, width), lambda i, s: (s[count], 0, 0)) for _ in blocks],
            out_specs=pl.BlockSpec(shape, lambda i, s: (0,) * len(shape)),
        ),
        compiler_params=pltpu.CompilerParams(vmem_limit_bytes=VMEM_BYTES),
        cost_estimate=cost(
            2 * left.size * width, 2 * (left.size + count * length * width) + 4 * depth * width
        ),
    )(scalars, left, *blocks)


def turn_kernel(*refs):
    count = len(refs) // 2
    for rows_ref, o_ref in zip(refs[:count], refs[count:]):
        o_ref[0] = rows_ref[0].T


def turn(blocks):
    lead, rows, width = blocks[0].shape
    return pl.pallas_call(
        turn_kernel,
        out_shape=[jax.ShapeDtypeStruct((lead, width, rows), item.dtype) for item in blocks],
        grid=(lead,),
        in_specs=[pl.BlockSpec((1, rows, width), lambda i: (i, 0, 0)) for _ in blocks],
        out_specs=[pl.BlockSpec((1, width, rows), lambda i: (i, 0, 0)) for _ in blocks],
        compiler_params=pltpu.CompilerParams(vmem_limit_bytes=VMEM_BYTES),
        cost_estimate=cost(0, 4 * len(blocks) * lead * rows * width),
    )(*blocks)


def spread_kernel(groups, starts_ref, places_ref, rows_ref, *refs):
    outs, totals = refs[: len(groups)], refs[len(groups) :]
    blocks = [bits for group in groups for bits in group]
    tokens = rows_ref.shape[0]
    for total_ref in totals:
        total_ref[...] = jnp.zeros(total_ref.shape, F32)
    slot = lax.broadcasted_iota(jnp.int32, (WINDOW, TILE), 0)
    for index in range(tokens // TILE):
        span = slice(index * TILE, (index + 1) * TILE)
        rows = rows_ref[span, :]
        for bits, total_ref in zip(blocks, totals):
            start = pl.multiple_of(starts_ref[bits, index], 16)
            hot = (slot == places_ref[bits : bits + 1, span] - start).astype(F32).astype(BF)
            product = jnp.dot(hot, rows, preferred_element_type=F32)
            total_ref[pl.ds(start, WINDOW), :] += product
    place = 0
    for group, o_ref in zip(groups, outs):
        for lead in range(len(group)):
            value = totals[place][...].astype(BF)
            if len(group) == 1:
                o_ref[...] = value
            else:
                o_ref[lead] = value
            place += 1


def spread_rows(starts, places, rows, slots, groups):
    tokens, width = rows.shape
    shapes = [
        (slots, width) if len(group) == 1 else (len(group), slots, width) for group in groups
    ]
    count = sum(len(group) for group in groups)
    return pl.pallas_call(
        functools.partial(spread_kernel, groups),
        out_shape=[jax.ShapeDtypeStruct(shape, BF) for shape in shapes],
        grid_spec=pltpu.PrefetchScalarGridSpec(
            num_scalar_prefetch=1,
            grid=(1,),
            in_specs=[
                pl.BlockSpec(places.shape, lambda i, s: (0, 0)),
                pl.BlockSpec((tokens, width), lambda i, s: (0, 0)),
            ],
            out_specs=[
                pl.BlockSpec(shape, lambda i, s, n=len(shape): (0,) * n) for shape in shapes
            ],
            scratch_shapes=[pltpu.VMEM((slots, width), F32) for _ in range(count)],
        ),
        compiler_params=pltpu.CompilerParams(vmem_limit_bytes=VMEM_BYTES),
        cost_estimate=cost(
            4 * count * WINDOW * tokens * width,
            2 * (tokens + count * slots) * width,
        ),
    )(starts, places, rows)


def gather_kernel(tiles, starts_ref, places_ref, *refs):
    o_ref = refs[-1]
    slot = lax.broadcasted_iota(jnp.int32, (TILE, WINDOW), 1)
    for index in range(tiles):
        span = slice(index * TILE, (index + 1) * TILE)
        total = jnp.zeros((TILE, o_ref.shape[1]), F32)
        for block, block_ref in enumerate(refs[:-1]):
            start = pl.multiple_of(starts_ref[block, pl.program_id(0) * tiles + index], 16)
            hot = (slot == places_ref[span, block : block + 1] - start).astype(F32).astype(BF)
            window = pl.ds(start, WINDOW)
            rows = block_ref[0, window, :] if len(block_ref.shape) == 3 else block_ref[window, :]
            total += jnp.dot(hot, rows, preferred_element_type=F32)
        o_ref[span, :] = total.astype(o_ref.dtype)


def gather_slots(starts, places, blocks):
    tokens = places.shape[0]
    lists = [item if isinstance(item, tuple) else (item, None) for item in blocks]
    slots, width = lists[0][0].shape[-2:]
    tiles = 4

    def spec(place):
        if place is None:
            return pl.BlockSpec((slots, width), lambda i, s: (0, 0))
        return pl.BlockSpec((1, slots, width), lambda i, s: (place, 0, 0))

    tile = tiles * TILE
    return pl.pallas_call(
        functools.partial(gather_kernel, tiles),
        out_shape=jax.ShapeDtypeStruct((tokens, width), BF),
        grid_spec=pltpu.PrefetchScalarGridSpec(
            num_scalar_prefetch=1,
            grid=(tokens // tile,),
            in_specs=[pl.BlockSpec((tile, places.shape[1]), lambda i, s: (i, 0))]
            + [spec(place) for _, place in lists],
            out_specs=pl.BlockSpec((tile, width), lambda i, s: (i, 0)),
        ),
        compiler_params=pltpu.CompilerParams(vmem_limit_bytes=VMEM_BYTES),
        cost_estimate=cost(
            4 * WINDOW * tokens * width * len(blocks),
            2 * (tokens + slots * len(blocks)) * width,
        ),
    )(starts, places, *[item for item, _ in lists])


def dots_kernel(transposed, lead, terms, count, stacked, *refs):
    outs = refs[terms * (1 + count) :]
    contract = (((1,), (1 if transposed else 0,)), ((), ()))
    operands = [ref[0] if flag else ref[...] for ref, flag in zip(refs, lead)]
    for place in range(count):
        o_ref = outs[0 if stacked else place]
        total = None
        for term in range(terms):
            right = operands[terms * (1 + place) + term]
            product = lax.dot_general(
                operands[term], right, contract, preferred_element_type=F32
            )
            total = product if total is None else total + product
        if stacked:
            outs[0][place] = total.astype(outs[0].dtype)
        else:
            o_ref[...] = total.astype(o_ref.dtype)


def dots(lefts, right_lists, transposed, dtype, stacked=False):
    operands, specs, lead = [], [], []
    rows = lefts[0][0].shape[1] if isinstance(lefts[0], tuple) else lefts[0].shape[0]
    tile = rows // 2 if rows % 32 == 0 else rows
    flops, size = 0, 0
    for side, items in enumerate([lefts] + list(right_lists)):
        for item in items:
            array, place = item if isinstance(item, tuple) else (item, None)
            shape = array.shape[-2:]
            block = (tile, shape[1]) if side == 0 else shape
            if place is None:
                specs.append(
                    pl.BlockSpec(block, (lambda i: (i, 0)) if side == 0 else (lambda i: (0, 0)))
                )
            elif side == 0:
                specs.append(pl.BlockSpec((1,) + block, lambda i, p=place: (p, i, 0)))
            else:
                specs.append(pl.BlockSpec((1,) + block, lambda i, p=place: (p, 0, 0)))
            operands.append(array)
            lead.append(place is not None)
            size += 2 * shape[0] * shape[1]
            if side:
                flops += 2 * rows * shape[0] * shape[1]
    width = shape[0] if transposed else shape[1]
    count = len(right_lists)
    if stacked:
        out_shape = [jax.ShapeDtypeStruct((count, rows, width), dtype)]
        out_specs = [pl.BlockSpec((count, tile, width), lambda i: (0, i, 0))]
    else:
        out_shape = [jax.ShapeDtypeStruct((rows, width), dtype)] * count
        out_specs = [pl.BlockSpec((tile, width), lambda i: (i, 0))] * count
    return pl.pallas_call(
        functools.partial(dots_kernel, transposed, lead, len(lefts), count, stacked),
        out_shape=out_shape,
        grid=(rows // tile,),
        in_specs=specs,
        out_specs=out_specs,
        compiler_params=pltpu.CompilerParams(vmem_limit_bytes=VMEM_BYTES),
        cost_estimate=cost(
            2 * flops,
            size + 2 * count * rows * width,
        ),
    )(*operands)


def pair_kernel(count, own_ref, other_ref, *refs):
    for place in range(count):
        for lead, left_ref in enumerate((own_ref, other_ref)):

            @pl.when(pl.program_id(0) == 2 * place + lead)
            def _():
                product = jnp.dot(left_ref[...], refs[place][0], preferred_element_type=F32)
                refs[count][0] = product.astype(refs[count].dtype)


def pair_dots(lefts, right_list, scale=COST):
    rows, depth = lefts[0].shape
    width = right_list[0].shape[2]
    count = len(right_list)

    def spec(place):
        return pl.BlockSpec(
            (1, depth, width), lambda i: (jnp.clip(i - 2 * place, 0, 1), 0, 0)
        )

    return pl.pallas_call(
        functools.partial(pair_kernel, count),
        out_shape=jax.ShapeDtypeStruct((2 * count, rows, width), BF),
        grid=(2 * count,),
        in_specs=[pl.BlockSpec((rows, depth), lambda i: (0, 0))] * 2
        + [spec(place) for place in range(count)],
        out_specs=pl.BlockSpec((1, rows, width), lambda i: (i, 0, 0)),
        compiler_params=pltpu.CompilerParams(vmem_limit_bytes=VMEM_BYTES),
        cost_estimate=cost(4 * count * rows * depth * width, 4 * rows * depth, scale),
    )(*lefts, *right_list)


def turned_kernel(pairs, rights, lead, merged, *refs):
    contract = (((0,), (0,)), ((), ()))
    outs = list(refs[2 * pairs + 2 * rights :])
    if merged:
        outs.insert(0, outs[0])
    operands = [ref[0] if flag else ref[...] for ref, flag in zip(refs, lead)]
    for pair in range(pairs):
        for place, o_ref in enumerate(outs):
            total = None
            for batch in (0, 1):
                left = operands[2 * pair + batch]
                right = operands[2 * pairs + 2 * place + batch]
                if len(outs) == 3 and place == 2:
                    left, right = right, left
                product = lax.dot_general(left, right, contract, preferred_element_type=F32)
                total = product if total is None else total + product
            lead = pair
            if merged and place == 1:
                lead += pairs
            o_ref[lead] = total[: o_ref.shape[1]].astype(o_ref.dtype)


def turned_dots(lefts, rights, dtypes, merged=False):
    operands, specs, lead, shapes = [], [], [], []
    for item in [each for pair in list(lefts) + list(rights) for each in pair]:
        array, place = item if isinstance(item, tuple) else (item, None)
        shape = array.shape[-2:]
        if place is None:
            specs.append(pl.BlockSpec(shape, lambda i: (0, 0)))
        else:
            specs.append(pl.BlockSpec((1,) + shape, lambda i, p=place: (p, 0, 0)))
        operands.append(array)
        lead.append(place is not None)
        shapes.append(shape)
    pairs, depth = len(lefts), shapes[0][1]
    outs = []
    flops = 0
    for place, dtype in enumerate(dtypes):
        width = shapes[2 * pairs + 2 * place][1]
        flops += 4 * pairs * shapes[0][0] * depth * width
        shape = (pairs, 8, depth) if place == 2 else (pairs, depth, width)
        if merged and place == 0:
            shape = (2 * pairs, depth, width)
        if not (merged and place == 1):
            outs.append(jax.ShapeDtypeStruct(shape, dtype))
    return pl.pallas_call(
        functools.partial(turned_kernel, pairs, len(rights), lead, merged),
        out_shape=outs,
        grid=(1,),
        in_specs=specs,
        out_specs=[pl.BlockSpec(out.shape, lambda i: (0, 0, 0)) for out in outs],
        compiler_params=pltpu.CompilerParams(vmem_limit_bytes=VMEM_BYTES),
        cost_estimate=cost(flops, flops // 300),
    )(*operands)


def flat(ref):
    return ref[0] if len(ref.shape) == 3 else ref[...]


def expert_kernel(count, owner_ref, other_ref, own_ref, sent_ref, *refs):
    rows_refs, gate_refs = refs[:count], refs[count : 2 * count]
    up_refs, router_refs = refs[2 * count : 3 * count], refs[3 * count : 4 * count]
    act_ref, gate_out, up_out, logit_out = refs[4 * count :]
    gate_pre = up_pre = logits = None
    for index in range(count):
        rows = flat(rows_refs[index])
        gate_part = jnp.dot(rows, flat(gate_refs[index]), preferred_element_type=F32)
        up_part = jnp.dot(rows, flat(up_refs[index]), preferred_element_type=F32)
        logit_part = jnp.dot(rows, router_refs[index][...], preferred_element_type=F32)
        gate_pre = gate_part if index == 0 else gate_pre + gate_part
        up_pre = up_part if index == 0 else up_pre + up_part
        logits = logit_part if index == 0 else logits + logit_part
    lane = lax.broadcasted_iota(jnp.int32, logits.shape, 1)
    signs = (lane == owner_ref[0]).astype(F32) - (lane == other_ref[...]).astype(F32)
    gate = jax.nn.sigmoid(jnp.sum(logits * signs, axis=1, keepdims=True))
    grad_act = own_ref[...] + sent_ref[...].astype(F32)
    sigmoid_gate = jax.nn.sigmoid(gate_pre)
    swish_gate = gate_pre * sigmoid_gate
    activation = swish_gate * up_pre
    act_ref[...] = (activation * gate).astype(BF)
    share = jnp.sum(grad_act * activation, axis=1, keepdims=True) * gate * (1.0 - gate)
    logit_out[...] = (share * signs).astype(BF)
    grad_activation = grad_act * gate
    swish_slope = sigmoid_gate * (1.0 + gate_pre * (1.0 - sigmoid_gate))
    gate_out[...] = (grad_activation * up_pre * swish_slope).astype(BF)
    up_out[...] = (grad_activation * swish_gate).astype(BF)


def expert_forward(owner, other, own, sent, rows, gates, ups, routers):
    slots, depth = own.shape[0], routers[0].shape[0]
    hidden = own.shape[1]
    lanes = routers[0].shape[1]
    tile = slots // 2 if slots % 32 == 0 else slots
    row_spec = lambda width: pl.BlockSpec((tile, width), lambda i, s: (i, 0))

    def rows_spec(item):
        if isinstance(item, tuple):
            return pl.BlockSpec((1, tile, depth), lambda i, s: (item[1], i, 0))
        return row_spec(depth)


    def whole(item):
        if isinstance(item, tuple):
            return pl.BlockSpec((1,) + item[0].shape[1:], lambda i, s: (item[1], 0, 0))
        return pl.BlockSpec(item.shape, lambda i, s: (0, 0))

    weights = list(gates) + list(ups) + list(routers)
    out_shapes = [jax.ShapeDtypeStruct((slots, hidden), BF)] * 3
    out_shapes.append(jax.ShapeDtypeStruct((slots, lanes), BF))
    return pl.pallas_call(
        functools.partial(expert_kernel, len(rows)),
        out_shape=out_shapes,
        grid_spec=pltpu.PrefetchScalarGridSpec(
            num_scalar_prefetch=1,
            grid=(slots // tile,),
            in_specs=[row_spec(1), row_spec(hidden), row_spec(hidden)]
            + [rows_spec(item) for item in rows]
            + [whole(item) for item in weights],
            out_specs=[row_spec(item.shape[1]) for item in out_shapes],
        ),
        compiler_params=pltpu.CompilerParams(vmem_limit_bytes=VMEM_BYTES),
        cost_estimate=cost(
            4 * len(rows) * slots * depth * hidden,
            4 * len(rows) * depth * hidden + 12 * slots * hidden,
        ),
    )(
        owner.reshape(1),
        other,
        own,
        sent,
        *[item[0] if isinstance(item, tuple) else item for item in list(rows) + weights],
    )


def assemble_kernel(order_ref, *refs):
    for block, ref in enumerate(refs[:-1]):

        @pl.when(pl.program_id(0) == block)
        def _():
            refs[-1][0] = flat(ref).astype(F32)


def assemble(order, blocks):
    count = len(blocks)
    arrays = [item[0] if isinstance(item, tuple) else item for item in blocks]
    rows, width = arrays[0].shape[-2:]
    tiles = ASSEMBLE if rows % (16 * ASSEMBLE) == 0 else 1

    def spec(place, item):
        def tile_of(b, i):
            return jnp.where(b == place, i, jnp.where(b < place, 0, tiles - 1))

        if isinstance(item, tuple):
            return pl.BlockSpec(
                (1, rows // tiles, width), lambda b, i, s: (item[1], tile_of(b, i), 0)
            )
        return pl.BlockSpec((rows // tiles, width), lambda b, i, s: (tile_of(b, i), 0))

    return pl.pallas_call(
        assemble_kernel,
        out_shape=jax.ShapeDtypeStruct((count, rows, width), F32),
        grid_spec=pltpu.PrefetchScalarGridSpec(
            num_scalar_prefetch=1,
            grid=(count, tiles),
            in_specs=[spec(place, item) for place, item in enumerate(blocks)],
            out_specs=pl.BlockSpec(
                (1, rows // tiles, width), lambda b, i, s: (s[b], i, 0)
            ),
        ),
        compiler_params=pltpu.CompilerParams(vmem_limit_bytes=VMEM_BYTES),
        cost_estimate=cost(0, 7 * count * rows * width),
    )(order, *arrays)


def allowed_keys(row_segments, column_segments):
    length = row_segments.shape[0]
    query = lax.broadcasted_iota(jnp.int32, (length, length), 0)
    key = lax.broadcasted_iota(jnp.int32, (length, length), 1)
    same = (column_segments == 0) | (column_segments == row_segments)
    return same & (key <= query)


def weights_of(query, key, allowed):
    scores = lax.dot_general(query, key, (((1,), (1,)), ((), ())), preferred_element_type=F32)
    scores = jnp.where(allowed, scores * HD ** (-0.5), NEGATIVE)
    weights = jnp.exp(scores - jnp.max(scores, axis=1, keepdims=True))
    return weights / jnp.sum(weights, axis=1, keepdims=True)


def attend_kernel(
    logits_ref, routes_ref, kept_ref, rows_ref, columns_ref, *refs
):
    parts, refs = refs[:12], refs[12:]
    saved_ref, mixed_ref, gated_ref, side_ref, cos_ref, sin_ref = refs

    @pl.when(pl.program_id(0) == 0)
    def _():
        logits = logits_ref[...]
        label = lax.broadcasted_iota(jnp.int32, logits.shape, 0)
        picked = [
            jnp.sum(jnp.where(label == routes_ref[place : place + 1, :], logits, 0.0), axis=0)
            for place in (0, 1)
        ]
        gates = [
            jax.nn.sigmoid(picked[place] - picked[1 - place])[None, :] for place in (0, 1)
        ]
        lines = [gates[place] * kept_ref[place : place + 1, :] for place in (0, 1)]
        lines.append(gates[0] * gates[1])
        lines += [routes_ref[place : place + 1, :].astype(F32) for place in (0, 1)]
        lines += [kept_ref[place : place + 1, :] for place in (0, 1)]
        lines.append(jnp.zeros((128 - len(lines), logits.shape[1]), F32))
        side_ref[...] = jnp.concatenate(lines, axis=0).T
        cos_ref[...], sin_ref[...] = rope_lines(rows_ref[...], columns_ref[...])

    summed = [
        parts[place][...].astype(F32)
        + parts[4 + place][...].astype(F32)
        + parts[8 + place][...].astype(F32)
        for place in range(4)
    ]
    cosine, sine = cos_ref[...], sin_ref[...]
    turned = [
        (item * cosine + pltpu.roll(item, HD // 2, 1) * sine).astype(BF) for item in summed[:3]
    ]
    turned.append(summed[3].astype(BF))
    for place in range(4):
        saved_ref[place] = turned[place]
    allowed = allowed_keys(rows_ref[...], columns_ref[...])
    for place in range(2):
        probs = weights_of(turned[place], turned[2], allowed).astype(BF)
        mixed = jnp.dot(probs, turned[3], preferred_element_type=F32)
        mixed_ref[place] = mixed
        gated_ref[place] = (mixed * side_ref[:, place : place + 1]).astype(BF)


def head_parts(parts, count, length, heads):
    specs, arrays = [], []
    for part in parts:
        each = count // len(part)
        for place in range(count):
            start = place % each * heads
            specs.append(pl.BlockSpec((length, HD), lambda h, s=start: (0, s + h)))
            arrays.append(part[place // each])
    return specs, arrays


def attend(logits, routes, kept, segments, parts):
    length = logits.shape[1]
    heads = parts[0][0].shape[1] // (4 * HD)
    whole = lambda array: pl.BlockSpec(array.shape, lambda h: (0, 0))
    part_specs, part_arrays = head_parts(parts, 4, length, heads)
    small = [logits, routes, kept, segments.reshape(length, 1), segments.reshape(1, length)]
    return pl.pallas_call(
        attend_kernel,
        out_shape=[
            jax.ShapeDtypeStruct((4, length, heads * HD), BF),
            jax.ShapeDtypeStruct((2, length, heads * HD), F32),
            jax.ShapeDtypeStruct((2, length, heads * HD), BF),
        ]
        + [jax.ShapeDtypeStruct((length, 128), F32)] * 3,
        grid=(heads,),
        in_specs=[whole(item) for item in small] + part_specs,
        out_specs=[
            pl.BlockSpec((count, length, HD), lambda h: (0, 0, h)) for count in (4, 2, 2)
        ]
        + [pl.BlockSpec((length, 128), lambda h: (0, 0))] * 3,
        compiler_params=pltpu.CompilerParams(vmem_limit_bytes=VMEM_BYTES),
        cost_estimate=cost(
            16 * heads * length * length * HD,
            12 * length * heads * HD * 4,
        ),
    )(*small, *part_arrays)


def attend_back_kernel(
    side_ref, rows_ref, columns_ref, cos_ref, sin_ref, saved_ref, mixed_ref, *refs
):
    parts, (out_ref, logit_ref, share_ref) = refs[:6], refs[6:]
    allowed = allowed_keys(rows_ref[...], columns_ref[...])
    key, value = saved_ref[2], saved_ref[3]
    cosine, sine = cos_ref[...], sin_ref[...]
    scale = HD ** (-0.5)
    over_rows = (((0,), (0,)), ((), ()))
    over_last = (((1,), (1,)), ((), ()))

    def unturn(item):
        return (item * cosine - pltpu.roll(item, HD // 2, 1) * sine).astype(BF)

    @pl.when(pl.program_id(0) == 0)
    def _():
        share_ref[...] = jnp.zeros(share_ref.shape, F32)

    lane = lax.broadcasted_iota(jnp.int32, share_ref.shape, 1)
    grad_key = grad_value = 0.0
    for place in range(2):
        grad = (
            parts[place][...].astype(F32)
            + parts[2 + place][...].astype(F32)
            + parts[4 + place][...].astype(F32)
        )
        share = jnp.sum(grad * mixed_ref[place], axis=1, keepdims=True)
        share_ref[...] += jnp.where(lane == place, share, 0.0)
        grad = (grad * side_ref[:, place : place + 1]).astype(BF)
        query = saved_ref[place]
        probs = weights_of(query, key, allowed)
        grad_value += lax.dot_general(
            probs.astype(BF), grad, over_rows, preferred_element_type=F32
        )
        grad_probs = lax.dot_general(grad, value, over_last, preferred_element_type=F32)
        centred = jnp.sum(probs * grad_probs, axis=1, keepdims=True)
        grad_scores = (probs * (grad_probs - centred)).astype(BF)
        grad_query = jnp.dot(grad_scores, key, preferred_element_type=F32) * scale
        out_ref[place] = unturn(grad_query)
        grad_key += lax.dot_general(
            grad_scores, query, over_rows, preferred_element_type=F32
        )
    out_ref[2] = unturn(grad_key * scale)
    out_ref[3] = grad_value.astype(BF)

    @pl.when(pl.program_id(0) == pl.num_programs(0) - 1)
    def _():
        shares = [
            share_ref[:, place : place + 1] * side_ref[:, 5 + place : 6 + place]
            for place in (0, 1)
        ]
        share = (shares[0] - shares[1]) * side_ref[:, 2:3]
        label = lane.astype(F32)
        signs = (label == side_ref[:, 3:4]).astype(F32) - (label == side_ref[:, 4:5]).astype(F32)
        logit_ref[...] = (share * signs).astype(BF)


def attend_back(side, segments, cosine, sine, saved, mixed, parts):
    length = side.shape[0]
    heads = saved.shape[2] // HD
    whole = lambda array: pl.BlockSpec(array.shape, lambda h: (0, 0))
    part_specs, part_arrays = head_parts(parts, 2, length, heads)
    small = [side, segments.reshape(length, 1), segments.reshape(1, length), cosine, sine]
    return pl.pallas_call(
        attend_back_kernel,
        out_shape=[
            jax.ShapeDtypeStruct((4, length, heads * HD), BF),
            jax.ShapeDtypeStruct((length, 128), BF),
        ],
        grid=(heads,),
        in_specs=[whole(item) for item in small]
        + [pl.BlockSpec((count, length, HD), lambda h: (0, 0, h)) for count in (4, 2)]
        + part_specs,
        out_specs=[
            pl.BlockSpec((4, length, HD), lambda h: (0, 0, h)),
            pl.BlockSpec((length, 128), lambda h: (0, 0)),
        ],
        scratch_shapes=[pltpu.VMEM((length, 128), F32)],
        compiler_params=pltpu.CompilerParams(vmem_limit_bytes=VMEM_BYTES),
        cost_estimate=cost(
            40 * heads * length * length * HD,
            20 * length * heads * HD * 4,
        ),
    )(*small, saved, mixed, *part_arrays)


def swap(value, axes, bits, size):
    if bits == 0:
        return value
    return lax.ppermute(value, axes, [(i, i ^ bits) for i in range(size)])


def row_gather(values):
    return lax.all_gather(values, "row", axis=0, tiled=True)


def row_total(values, *waits):
    total = lax.psum_scatter(values, "row", scatter_dimension=0, tiled=True)
    return (after(total, *waits) if waits else total).astype(F32)


def col_total(values):
    return lax.psum(values, "col")


def small_total(value, axes):
    for axis in axes:
        size = lax.axis_size(axis)
        bits = 1
        while bits < size:
            value = value + swap(value, axis, bits, size)
            bits *= 2
    return value


def norm_factor(rows_in):
    squares = col_total(jnp.sum(rows_in * rows_in, axis=1))
    return lax.rsqrt(squares / D + EPSILON)


def norm_backward(rows_in, factor, gain_row, grad_in):
    scaled = grad_in * gain_row
    inner_sum = col_total(jnp.sum(scaled * rows_in, axis=1))[:, None]
    gain_grad = jnp.sum(grad_in * rows_in * factor, axis=0)
    return (factor * scaled - rows_in * factor**3 * inner_sum / D, gain_grad)


def local(
    hidden_in,
    gain_attn,
    router_attn,
    query_weight,
    kv_weight,
    out_weight,
    gain_ffn,
    router_ffn,
    gate_weight,
    up_weight,
    down_weight,
    attn_routes,
    ffn_routes,
    attn_order,
    ffn_order,
    segment_ids,
    d_out,
):
    dp_count, col_count = lax.axis_size("dp"), lax.axis_size("col")
    dp_index, col_index = lax.axis_index("dp"), lax.axis_index("col")
    owners = dp_count * col_count
    owner = dp_index * col_count + col_index
    batch_rows = attn_routes.shape[0]
    group_rows = batch_rows // col_count
    features = hidden_in.shape[1]
    attn_experts = query_weight.shape[0]
    ffn_experts = gate_weight.shape[0]
    half_experts = attn_experts // dp_count
    attn_capacity = 5 * batch_rows // (2 * attn_experts)
    slots = 5 * batch_rows // (2 * ffn_experts)
    head_width = query_weight.shape[2]
    pair_axes = ("dp", "col")

    def cross(pair, *waits):
        received = swap(pair, "col", 2, col_count)
        hop = swap(lead_block(after(received, *waits), 1), "col", 1, col_count)
        return [(received, 0), (hop, 0)]

    def fence(rows, numbers):
        token = swap(tip(rows), "col", 1, col_count)[0, 0]
        return numbers + (token != token).astype(jnp.int32)

    def arrays(blocks):
        return [item[0] if isinstance(item, tuple) else item for item in blocks]

    def flagged(blocks):
        return [(item, 0) for item in blocks]

    offsets = (owner ^ jnp.arange(owners, dtype=jnp.int32)).astype(jnp.int32)
    block_order = (col_index ^ jnp.arange(col_count, dtype=jnp.int32)).astype(jnp.int32)
    hidden_all = row_gather(hidden_in)
    rows_in = hidden_in.astype(F32)
    factor_a = norm_factor(rows_in)
    gate_cross = cross(take_blocks(gate_weight, after(offsets, factor_a), 2, 1, 2))
    factor_a_all = row_gather(factor_a)
    lane_router_f = jnp.pad(
        after(router_ffn, factor_a), ((0, 0), (0, 128 - ffn_experts))
    )
    router_blocks = [swap(lane_router_f, "col", bits, col_count) for bits in range(col_count)]
    owner_rows, owner_starts = token_slots(
        ffn_routes, after(ffn_order, factor_a), offsets, ffn_experts, slots
    )
    (
        hidden_all,
        owner_rows,
        owner_starts,
        offsets,
        block_order,
    ) = lax.optimization_barrier((hidden_all, owner_rows, owner_starts, offsets, block_order))
    grad_out_all = row_gather(after(d_out, hidden_all))

    gain_a = gain_attn.astype(F32)
    normed_all = (hidden_all.astype(F32) * factor_a_all[:, None] * gain_a).astype(BF)

    def col_scatter(rows, weight, extra_weight, transposed, first_waits, near_waits, near_first):
        def part(blocks, scale):
            kept, *sent = pick_matmul(
                blocks, attn_routes, rows, weight, extra_weight, group_rows, transposed, scale
            )
            return kept, [swap(item, "col", 1, col_count) for item in sent]

        near_order = after(block_order[0:2], *first_waits)
        far_order = after(block_order[2:4], *first_waits)
        if near_first:
            near = part(near_order, COST)
            far_order = after(far_order, near[0])
        kept, received = part(far_order, COST)
        far = join_halves(kept, received)
        if not near_first:
            near = part(after(near_order, far, *near_waits), 1)
        return [[near[0]], near[1], far, [swap(far, "col", 2, col_count)]]

    projected = col_scatter(
        normed_all, query_weight, kv_weight, False, [], [gate_cross[0][0]], False
    )

    far_sent = projected[2]
    logits_sent = block_logits(
        after(block_order, far_sent), normed_all, router_attn, group_rows
    )
    attn_kept = kept_pairs(
        attn_routes, after(attn_order, logits_sent[0]), attn_experts, attn_capacity
    )
    segments = segment_ids.reshape(-1)
    kept_a = attn_kept.reshape(2, batch_rows // TILE, TILE)
    kept_a = lax.dynamic_slice_in_dim(
        kept_a, col_index * (group_rows // TILE), group_rows // TILE, 1
    ).reshape(2, group_rows)
    routes_a = lax.dynamic_slice_in_dim(
        after(attn_routes, far_sent), col_index * group_rows, group_rows, 0
    ).T

    up_pair = take_blocks(up_weight, after(offsets, far_sent), 2, 1, 2)
    route_sums = jnp.sum(after(ffn_routes, far_sent), axis=1).astype(BF)
    route_sums = jnp.broadcast_to(route_sums[:, None], (batch_rows, 128))
    near_sums, far_sums = spread_rows(
        after(owner_starts, logits_sent[0]), owner_rows, route_sums, slots, [(0,), (col_count,)]
    )
    far_sums = swap(far_sums[:, 0:8], pair_axes, col_count, owners)
    slot_other = [item[:, 0:1].astype(jnp.int32) - owner for item in (near_sums, far_sums)]
    logits_sent, _ = lax.optimization_barrier(
        (logits_sent, (up_pair, kept_a, routes_a, slot_other))
    )
    logits_a = sum(
        swap(logits_sent[bits], "col", bits, col_count) for bits in range(col_count)
    )
    saved, attended, gated_out, side, cosine, sine_rows = attend(
        logits_a,
        routes_a,
        kept_a,
        segments,
        projected[0:2] + projected[3:],
    )

    half_bits = (0, 1, col_count, col_count + 1)
    grad_groups = spread_rows(
        after(owner_starts, gated_out),
        owner_rows,
        grad_out_all,
        slots,
        [(bits, bits ^ 2) for bits in half_bits],
    )
    grad_far = [swap(grad_groups[place], pair_axes, col_count, owners) for place in (2, 3)]

    lane_router = jnp.pad(
        after(router_attn, gated_out), ((0, 0), (0, 128 - attn_experts))
    )
    down_sent = [
        take_blocks(down_weight, after(offsets, grad_groups[0]), bits, 2, 2) for bits in (0, 1)
    ]

    def col_blocks(block, *waits):
        far = swap(block, "col", 2, col_count)
        near = swap(block, "col", 1, col_count)
        return [block, near, far, swap(after(far, *waits), "col", 1, col_count)]

    gated_blocks = col_blocks(gated_out, lane_router, *down_sent, *router_blocks)
    up_received = swap(after(up_pair, gated_blocks[2]), "col", 2, col_count)
    attn_part = merge_matmul(block_order, attn_routes, gated_blocks, out_weight, (), False)
    down_pairs = [down_sent[0], swap(down_sent[1], "col", 1, col_count)]

    grad_pairs = [grad_groups[0], swap(grad_groups[1], "col", 1, col_count)]

    def grad_act_part(batch, lead, dtype, *waits):
        return dots(
            [(array, lead) for array in grad_pairs[2 * batch : 2 * batch + 2]],
            [[(after(down_pairs[0], *waits), lead), (down_pairs[1], lead)]],
            True,
            dtype,
        )[0]

    grad_act_out = [grad_act_part(0, 1, BF, attn_part)]
    up_side = lead_block(after(up_received, grad_far[0], *grad_act_out), 1)
    up_cross = [(up_received, 0), (swap(up_side, "col", 1, col_count), 0)]
    middle = rows_in + row_total(attn_part, up_cross[1][0])
    gain_f = gain_ffn.astype(F32)
    factor_f = norm_factor(middle)[:, None]
    normed_f = (middle * factor_f * gain_f).astype(BF)
    normed_f_all = row_gather(normed_f)
    gate_near, gate_own = [
        take_blocks(gate_weight, after(offsets, normed_f), bits, 1, 1) for bits in (1, 0)
    ]
    up_near, up_own = [
        take_blocks(up_weight, after(offsets, gate_own), bits, 1, 1) for bits in (1, 0)
    ]
    gate_blocks = flagged([gate_own, swap(gate_near, "col", 1, col_count)]) + gate_cross
    up_blocks = flagged([up_own, swap(up_near, "col", 1, col_count)]) + up_cross

    grad_act_sent = [swap(after(grad_act_out[0], normed_f), "col", 2, col_count)]
    own_early = grad_act_part(0, 0, F32, normed_f)
    grad_hop = after(grad_far[1], own_early, up_own, up_near, grad_act_sent[0])
    grad_pairs += [grad_far[0], swap(grad_hop, "col", 1, col_count)]
    grad_act_out.append(grad_act_part(1, 1, BF, normed_f))
    grad_act_sent.append(swap(grad_act_out[1], "col", 2, col_count))
    send_starts = after(owner_starts, up_own, up_near, own_early, grad_act_out[1])
    order = [(2, 3), (6,), (7,)], [(4,), (5,), (1,), (0,)]
    slots_f = {}
    for part in order:
        blocks = spread_rows(send_starts, owner_rows, normed_f_all, slots, part)
        for group, block in zip(part, blocks):
            received = swap(block, pair_axes, group[0], owners)
            if len(group) == 1:
                slots_f[group[0]] = received
            else:
                slots_f[group[0]] = (received, 0)
                side_block = swap(lead_block(received, 1), "col", 1, col_count)
                slots_f[group[1]] = (side_block, 0)
        send_starts = after(send_starts, *blocks)
    normed_turned = turn([after(normed_all, blocks[0])[None]])[0][0]
    gated_turned = turn([after(gated_blocks[0], blocks[0])] + gated_blocks[1:])
    acts, grad_gates, grad_ups, grad_logits = [], [], [], []
    back_blocks = {}

    def send_back(pair):
        batch = pair[0] // col_count
        blocks = dots(
            [grad_gates[batch], grad_ups[batch], grad_logits[batch]],
            [
                [part[bits % col_count] for part in (gate_blocks, up_blocks, router_blocks)]
                for bits in pair
            ],
            True,
            BF,
            pair[0] == col_count + 2,
        )
        if len(blocks) == 1:
            received = swap(blocks[0], pair_axes, pair[0], owners)
            back_blocks[pair[0]] = (received, 0)
            hop = swap(lead_block(received, 1), "col", 1, col_count)
            back_blocks[pair[1]] = (hop, 0)
        else:
            for bits, block in zip(pair, blocks):
                back_blocks[bits] = swap(block, pair_axes, bits, owners)
        return blocks[0]

    grad_act_own = [own_early, grad_act_part(1, 0, F32, blocks[0])]
    back_sent = after(blocks[0], normed_turned, gated_turned[0])
    for batch in (0, 1):
        act, grad_gate, grad_up, grad_logit = expert_forward(
            owner.astype(jnp.int32),
            after(slot_other[batch], back_sent),
            grad_act_own[batch],
            grad_act_sent[batch],
            [slots_f[batch * col_count + bits] for bits in range(col_count)],
            gate_blocks,
            up_blocks,
            router_blocks,
        )
        acts.append(act)
        grad_gates.append(grad_gate)
        grad_ups.append(grad_up)
        grad_logits.append(grad_logit)
        back_sent = send_back((2, 3) if batch == 0 else (6, 7))
    back_sent = send_back((4, 5))
    grad_logits[0] = after(grad_logits[0], back_sent)
    back_sent = send_back((1, 0))

    def weight_grads(pair, dtype, wait, merged=False):
        return turned_dots(
            [(slots_f[bits], slots_f[bits + col_count]) for bits in pair],
            [grad_gates, grad_ups, (after(grad_logits[0], wait), grad_logits[1])],
            [dtype, dtype, F32],
            merged,
        )

    both_far, router_far = weight_grads((2, 3), BF, back_sent, True)
    grad_normed_f_part = gather_slots(
        after(owner_starts, both_far),
        owner_rows.T,
        [back_blocks[bits] for bits in range(owners)],
    )
    gate_near, up_near, router_near = weight_grads((0,), F32, grad_normed_f_part)
    gate_side, up_side, router_side = weight_grads((1,), BF, router_near)

    act_near = swap(after(acts[0], grad_normed_f_part), "col", 2, col_count)
    grad_normed_f = row_total(grad_normed_f_part, act_near, router_side)

    middle_norm_grad, gain_ffn_grad = norm_backward(middle, factor_f, gain_f, grad_normed_f)
    grad_middle = d_out.astype(F32) + middle_norm_grad
    grad_middle_low = grad_middle.astype(BF)
    grad_middle_all = row_gather(grad_middle_low)
    act_far = swap(after(acts[1], grad_middle_low), "col", 2, col_count)
    act_pairs = [(acts[0], act_near), (acts[1], act_far)]
    gate_near_sent = swap(gate_side, "col", 1, col_count)
    up_near_sent = swap(up_side, "col", 1, col_count)

    down_blocks = {}

    def down_pair(place, sent, start):
        bits = half_bits[place]
        down_blocks[bits], down_blocks[bits ^ 2] = (sent, start), (sent, start + 1)

    near_down = [
        pair_dots(act_pairs[0], [after(down_pairs[place], grad_middle_low)])
        for place in (0, 1)
    ]
    down_pair(0, near_down[0], 0)
    down_pair(1, swap(near_down[1], "col", 1, col_count), 0)

    far_down = pair_dots(
        act_pairs[1], [after(down_pairs[0], near_down[1]), down_pairs[1]]
    )
    far_sent = swap(far_down, pair_axes, col_count, owners)
    down_pair(2, far_sent, 0)
    down_hop = swap(
        take_blocks(far_sent, after(jnp.arange(4, dtype=jnp.int32), far_down), 2, 1, 2),
        "col",
        1,
        col_count,
    )
    down_pair(3, down_hop, 0)
    grad_gated = col_scatter(
        grad_middle_all, out_weight, None, True, [far_down], [], True
    )
    own_base = dp_index * half_experts
    away_base = (1 - dp_index) * half_experts

    def out_grads(base, dtype):
        return expert_grads(
            left_grad_kernel,
            block_order,
            base,
            half_experts,
            attn_routes.T,
            grad_middle_all,
            gated_turned,
            (head_width, features),
            dtype,
        )

    pieces, grad_logits_a = attend_back(
        side,
        segments,
        cosine,
        sine_rows,
        saved,
        attended,
        grad_gated[0:2] + grad_gated[3:],
    )

    out_away = out_grads(after(away_base, pieces), BF)
    ffn_part = gather_slots(
        fence(out_away, owner_starts),
        owner_rows.T,
        [down_blocks[bits] for bits in range(owners)],
    )
    ffn_total = row_total(ffn_part)
    out_away_sent = swap(out_away, "dp", 1, dp_count)

    def down_grad_part(near, dtype, wait):
        lefts = [(after(acts[0], wait), acts[1]), (act_near, act_far)]
        return [
            turned_dots(
                [lefts[lead]],
                [[(grad_pairs[place], lead) for place in (near, 2 + near)]],
                [dtype],
            )[0]
            for lead in (0, 1)
        ]

    down_away = down_grad_part(1, BF, ffn_part)
    logits_back = col_blocks(grad_logits_a)
    pieces_blocks = col_blocks(pieces, *down_away)
    normed_part = merge_matmul(
        block_order,
        attn_routes,
        pieces_blocks,
        query_weight,
        (logits_back, kv_weight, lane_router),
        True,
    )

    def query_grads(base, dtype):
        return expert_grads(
            right_grad_kernel,
            block_order,
            base,
            half_experts,
            attn_routes,
            normed_turned,
            pieces_blocks,
            (features, head_width),
            dtype,
        )

    query_away = query_grads(after(away_base, normed_part), BF)
    kv_away = plain_grad(
        fence(query_away, block_order), 3 - dp_index, normed_turned, pieces_blocks, BF
    )
    query_sent = swap(query_away, "dp", 1, dp_count)
    kv_sent = swap(kv_away, "dp", 1, dp_count)
    query_own = query_grads(after(own_base, kv_away), F32)
    kv_own = plain_grad(
        block_order, after(2 + dp_index, query_own), normed_turned, pieces_blocks, F32
    )
    router_attn_grad = plain_grad(
        block_order,
        after(0 * dp_index, kv_own),
        normed_turned,
        [item[None] for item in logits_back],
        F32,
        attn_experts,
    )
    both_received = swap(after(both_far, pieces_blocks[2], logits_back[2]), "col", 2, col_count)
    tail = after(block_order, router_attn_grad)
    down_sent = [swap(item, "col", 1, col_count) for item in down_away]
    out_own = out_grads(after(own_base, router_attn_grad), F32)
    down_near = down_grad_part(0, F32, out_own)
    down_grad = assemble(
        after(tail, *down_near),
        [(down_near[0], 0), (down_sent[0], 0), (down_near[1], 0), (down_sent[1], 0)],
    )
    out_grad = add_wide(out_own, after(out_away_sent, down_grad))
    both_side = take_blocks(
        both_received,
        after(jnp.arange(4, dtype=jnp.int32), down_grad, out_grad, query_sent),
        1,
        2,
        2,
    )
    both_side = swap(both_side, "col", 1, col_count)
    grad_normed = row_total(normed_part, both_side)
    input_norm_grad, gain_attn_grad = norm_backward(
        rows_in, factor_a[:, None], gain_a, grad_normed
    )
    input_grad = grad_middle + input_norm_grad
    layer_out = (middle + ffn_total).astype(BF)
    small = jnp.concatenate(
        [
            router_attn_grad,
            gain_ffn_grad[None],
            gain_attn_grad[None],
            router_near[0],
            router_side[0],
            router_far[0],
            router_far[1],
        ],
        axis=0,
    )
    small = small_total(small, ("row", "dp"))
    lines = attn_experts + 2
    gain_ffn_grad, gain_attn_grad = small[lines - 2], small[lines - 1]
    router_ffn_grad = sum(
        swap(
            small[lines + bits * ffn_experts : lines + (bits + 1) * ffn_experts],
            "col",
            bits,
            col_count,
        )
        for bits in range(col_count)
    )
    gate_grad, up_grad = [
        assemble(tail, [(near, 0), (sent, 0), (both_received, 2 * place), (both_side, place)])
        for place, (near, sent) in enumerate(
            ((gate_near, gate_near_sent), (up_near, up_near_sent))
        )
    ]
    query_grad = add_wide(query_own, after(query_sent, up_grad))
    kv_grad = add_wide(kv_own, after(kv_sent, up_grad))
    ffn_half = ffn_experts // dp_count
    router_ffn_grad = lax.dynamic_slice_in_dim(
        router_ffn_grad, dp_index * ffn_half, ffn_half, 0
    ).T
    router_attn_grad = lax.dynamic_slice_in_dim(
        small, dp_index * half_experts, half_experts, 0
    ).T
    return (
        layer_out,
        input_grad,
        gain_attn_grad,
        router_attn_grad,
        query_grad,
        kv_grad,
        out_grad,
        gain_ffn_grad,
        router_ffn_grad,
        gate_grad,
        up_grad,
        down_grad,
    )


def solution(mesh):
    in_specs = (
        P(("dp", "row"), "col"),
        P("col"),
        P("col", None),
        P(None, "col", "row"),
        P(None, "col", "row"),
        P(None, "row", "col"),
        P("col"),
        P("col", None),
        P(None, "col", "row"),
        P(None, "col", "row"),
        P(None, "row", "col"),
        P("dp", None),
        P("dp", None),
        P("dp", None),
        P("dp", None),
        P(("dp", "col"), None),
        P(("dp", "row"), "col"),
    )
    out_specs = (
        P(("dp", "row"), "col"),
        P(("dp", "row"), "col"),
        P("col"),
        P("col", "dp"),
        P("dp", "col", "row"),
        P("dp", "col", "row"),
        P("dp", "row", "col"),
        P("col"),
        P("col", "dp"),
        P("dp", "col", "row"),
        P("dp", "col", "row"),
        P("dp", "row", "col"),
    )
    return jax.shard_map(local, mesh=mesh, in_specs=in_specs, out_specs=out_specs, check_vma=False)
```

```python
import functools
import math

import jax
import jax.numpy as jnp
from jax import lax
from jax.experimental import pallas as pl
from jax.experimental.pallas import tpu as pltpu
from jax.sharding import PartitionSpec as P

D = 2048
HD = 128
SEQ = 512

EPSILON = 1e-06
NEGATIVE = -1e30
VMEM_BYTES = 56 * 1024 * 1024
TILE = 128
WINDOW = TILE + 16
COST = 1 << 20
ASSEMBLE = 2
BF = jnp.bfloat16
F32 = jnp.float32


def cost(flops, size, scale=COST):
    return pl.CostEstimate(flops=flops // scale, bytes_accessed=size // scale, transcendentals=0)


def after(value, *others):
    return lax.optimization_barrier((value,) + others)[0]


def rope_lines(row_segments, column_segments):
    length = row_segments.shape[0]
    query = lax.broadcasted_iota(jnp.int32, (length, length), 0)
    key = lax.broadcasted_iota(jnp.int32, (length, length), 1)
    before = (column_segments == row_segments) & (key < query)
    within = jnp.sum(before.astype(F32), axis=1, keepdims=True)
    prompt = jnp.sum((column_segments == 0).astype(F32), axis=1, keepdims=True)
    places = within + jnp.where(row_segments > 0, prompt, 0.0)
    lane = lax.broadcasted_iota(jnp.int32, (1, HD), 1)
    step = jnp.where(lane < HD // 2, lane, lane - HD // 2).astype(F32)
    frequency = jnp.exp(step * (-2.0 * math.log(10000.0) / HD))
    angles = places * frequency
    sine = jnp.sin(angles)
    return jnp.cos(angles), jnp.where(lane < HD // 2, -sine, sine)


def kept_table(capacity, experts, order_ref, table_ref, turned_ref):
    lines, lanes = table_ref.shape
    pairs = order_ref.shape[1]
    order = order_ref[...]
    token = order // 2
    line = (order % 2) * (lines // 2) + token // lanes
    high = (lax.broadcasted_iota(jnp.int32, (lines, pairs), 0) == line).astype(F32).astype(BF)
    low = lax.broadcasted_iota(jnp.int32, (lanes, pairs), 0) == token % lanes
    low = low.astype(F32).astype(BF)
    chosen = jnp.dot(turned_ref[...].astype(BF), high, preferred_element_type=F32)
    chosen = jnp.sum(chosen * low.astype(F32), axis=0, keepdims=True)
    label = lax.broadcasted_iota(jnp.int32, (experts, pairs), 0).astype(F32)
    member = (label == chosen).astype(F32)
    step = 256
    row = lax.broadcasted_iota(jnp.int32, (step, step), 0)
    upto = row <= lax.broadcasted_iota(jnp.int32, (step, step), 1)
    upto = upto.astype(F32).astype(BF)
    carry = jnp.zeros((experts, 1), F32)
    placed = []
    for start in range(0, pairs, step):
        part = member[:, start : start + step]
        count = jnp.dot(part.astype(BF), upto, preferred_element_type=F32) + carry
        carry = count[:, step - 1 : step]
        ranked = jnp.sum(count * part, axis=0, keepdims=True)
        placed.append((ranked <= capacity).astype(F32))
    placed = jnp.concatenate(placed, axis=1)
    return lax.dot_general(
        high * placed.astype(BF), low, (((1,), (1,)), ((), ())), preferred_element_type=F32
    )


def kept_kernel(capacity, experts, order_ref, table_ref, turned_ref, kept_ref):
    kept_ref[...] = kept_table(capacity, experts, order_ref, table_ref, turned_ref)


def slots_kernel(
    capacity, experts, labels_ref, order_ref, table_ref, turned_ref, places_ref, starts_ref
):
    kept = kept_table(capacity, experts, order_ref, table_ref, turned_ref)
    lines, lanes = table_ref.shape
    tiles = lines // 2
    row = lax.broadcasted_iota(jnp.int32, (lanes, lanes), 0)
    upto = (row <= lax.broadcasted_iota(jnp.int32, (lanes, lanes), 1)).astype(F32).astype(BF)
    first = lax.broadcasted_iota(jnp.int32, (tiles, tiles), 0)
    second = lax.broadcasted_iota(jnp.int32, (tiles, tiles), 1)
    above = (second < first).astype(F32).astype(BF)
    before = (first < second).astype(F32).astype(BF)
    ones = jnp.ones((8, lanes), BF)
    table = table_ref[...]
    for place in range(places_ref.shape[0]):
        member = (table == labels_ref[place].astype(F32)).astype(F32) * kept
        member = member[:tiles] + member[tiles:]
        inside = jnp.dot(member.astype(BF), upto, preferred_element_type=F32)
        past = jnp.dot(above, inside.astype(BF), preferred_element_type=F32)
        count = inside + past[:, lanes - 1 : lanes]
        slot = (count * member - 1.0).astype(jnp.int32)
        for tile in range(tiles):
            places_ref[place : place + 1, tile * lanes : (tile + 1) * lanes] = slot[tile : tile + 1]
        sums = lax.dot_general(
            ones, member.astype(BF), (((1,), (1,)), ((), ())), preferred_element_type=F32
        )
        start = jnp.dot(sums.astype(BF), before, preferred_element_type=F32)[0:1]
        start = start.astype(jnp.int32) // 16 * 16
        starts_ref[place : place + 1, :] = jnp.minimum(start, capacity - WINDOW)


def route_table(routes):
    return routes.astype(F32).T.reshape(-1, TILE)


def kept_pairs(routes, pair_order, experts, capacity):
    table = route_table(routes)
    return pl.pallas_call(
        functools.partial(kept_kernel, capacity, experts),
        out_shape=jax.ShapeDtypeStruct(table.shape, F32),
        compiler_params=pltpu.CompilerParams(vmem_limit_bytes=VMEM_BYTES),
        cost_estimate=cost(0, 0),
    )(pair_order, table, table.T)


def token_slots(routes, pair_order, labels, experts, capacity):
    table = route_table(routes)
    whole = lambda array: pl.BlockSpec(array.shape, lambda i, s: (0, 0))
    tiles = table.shape[0] // 2
    shapes = [(labels.shape[0], routes.shape[0]), (labels.shape[0], tiles)]
    return pl.pallas_call(
        functools.partial(slots_kernel, capacity, experts),
        out_shape=[jax.ShapeDtypeStruct(shape, jnp.int32) for shape in shapes],
        grid_spec=pltpu.PrefetchScalarGridSpec(
            num_scalar_prefetch=1,
            grid=(1,),
            in_specs=[whole(pair_order), whole(table), whole(table.T)],
            out_specs=[pl.BlockSpec(shape, lambda i, s: (0, 0)) for shape in shapes],
        ),
        compiler_params=pltpu.CompilerParams(vmem_limit_bytes=VMEM_BYTES),
        cost_estimate=cost(0, 0),
    )(labels, pair_order, table, table.T)


def copy_kernel(index_ref, block_ref, o_ref):
    o_ref[...] = block_ref[...]


def take_blocks(array, index, start, step, count):
    shape = array.shape[1:]
    return pl.pallas_call(
        copy_kernel,
        out_shape=jax.ShapeDtypeStruct((count,) + shape, array.dtype),
        grid_spec=pltpu.PrefetchScalarGridSpec(
            num_scalar_prefetch=1,
            grid=(count,),
            in_specs=[pl.BlockSpec((1,) + shape, lambda i, s: (s[start + step * i], 0, 0))],
            out_specs=pl.BlockSpec((1,) + shape, lambda i, s: (i, 0, 0)),
        ),
        compiler_params=pltpu.CompilerParams(vmem_limit_bytes=VMEM_BYTES),
        cost_estimate=cost(0, 0),
    )(index, array)


def lead_block(array, place):
    shape = (1,) + array.shape[1:]
    return pl.pallas_call(
        lead_kernel,
        out_shape=jax.ShapeDtypeStruct(shape, array.dtype),
        grid=(1,),
        in_specs=[pl.BlockSpec(shape, lambda i: (place, 0, 0))],
        out_specs=pl.BlockSpec(shape, lambda i: (0, 0, 0)),
        compiler_params=pltpu.CompilerParams(vmem_limit_bytes=VMEM_BYTES),
        cost_estimate=cost(0, 0),
    )(array)


def lead_kernel(block_ref, o_ref):
    o_ref[...] = block_ref[...]


def join_kernel(kept_ref, *refs):
    o_ref = refs[-1]
    start = 0
    for ref in refs[:-1]:
        span = slice(start, start + ref.shape[1])
        o_ref[:, span] = (kept_ref[:, span].astype(F32) + ref[...].astype(F32)).astype(BF)
        start += ref.shape[1]


def join_halves(kept, halves):
    rows, width = kept.shape
    tile = rows // 4 if rows % 64 == 0 else rows
    spec = lambda array: pl.BlockSpec((tile, array.shape[1]), lambda i: (i, 0))
    return pl.pallas_call(
        join_kernel,
        out_shape=jax.ShapeDtypeStruct(kept.shape, BF),
        grid=(rows // tile,),
        in_specs=[spec(kept)] + [spec(half) for half in halves],
        out_specs=spec(kept),
        compiler_params=pltpu.CompilerParams(vmem_limit_bytes=VMEM_BYTES),
        cost_estimate=cost(0, 0),
    )(kept, *halves)


def tip_kernel(rows_ref, o_ref):
    o_ref[...] = rows_ref[...].astype(BF)


def tip(rows):
    lead = rows.ndim - 2
    block = (None,) * lead + (16, 128)
    return pl.pallas_call(
        tip_kernel,
        out_shape=jax.ShapeDtypeStruct((16, 128), BF),
        grid=(1,),
        in_specs=[pl.BlockSpec(block, lambda i: (0,) * rows.ndim)],
        out_specs=pl.BlockSpec((16, 128), lambda i: (0, 0)),
        compiler_params=pltpu.CompilerParams(vmem_limit_bytes=VMEM_BYTES),
        cost_estimate=cost(0, 0),
    )(rows)


def add_kernel(own_ref, away_ref, o_ref):
    o_ref[...] = own_ref[...] + away_ref[...].astype(F32)


def add_wide(own, away):
    spec = pl.BlockSpec((1,) + own.shape[1:], lambda i: (i, 0, 0))
    return pl.pallas_call(
        add_kernel,
        out_shape=jax.ShapeDtypeStruct(own.shape, F32),
        grid=(own.shape[0],),
        in_specs=[spec, spec],
        out_specs=spec,
        compiler_params=pltpu.CompilerParams(vmem_limit_bytes=VMEM_BYTES),
        cost_estimate=cost(0, 0),
    )(own, away)


def pick_kernel(extra, transposed, blocks_ref, routes_ref, x_ref, w_ref, *rest):
    outs = rest[-3:]
    rows = x_ref[...]
    experts = w_ref.shape[0]
    width = w_ref.shape[1] if transposed else w_ref.shape[2]
    contract = (((1,), (1 if transposed else 0,)), ((), ()))
    first = jnp.broadcast_to(routes_ref[:, 0:1], (rows.shape[0], width))
    second = jnp.broadcast_to(routes_ref[:, 1:2], (rows.shape[0], width))
    picked = [jnp.zeros((rows.shape[0], width), F32) for _ in range(2)]
    for expert in range(experts):
        product = lax.dot_general(rows, w_ref[expert], contract, preferred_element_type=F32)
        picked[0] = jnp.where(first == expert, product, picked[0])
        picked[1] = jnp.where(second == expert, product, picked[1])
    for place in range(extra):
        picked.append(
            lax.dot_general(rows, rest[0][place], contract, preferred_element_type=F32)
        )
    picked = [item.astype(BF) for item in picked]
    half = len(picked) // 2

    @pl.when(pl.program_id(0) == 0)
    def _():
        for place, item in enumerate(picked):
            outs[0][:, place * width : (place + 1) * width] = item

    @pl.when(pl.program_id(0) == 1)
    def _():
        for place, item in enumerate(picked):
            start = place % half * width
            outs[1 + place // half][:, start : start + width] = item


def pick_matmul(blocks, routes, rows, weight, extra_weight, block_rows, transposed, scale):
    experts = weight.shape[0]
    depth = rows.shape[1]
    width = weight.shape[1] if transposed else weight.shape[2]
    tile = min(256, block_rows)
    tiles = block_rows // tile
    extra = 0 if extra_weight is None else extra_weight.shape[0]
    total = (2 + extra) * width
    in_specs = [
        pl.BlockSpec((tile, 2), lambda b, i, s: (s[b] * tiles + i, 0)),
        pl.BlockSpec((tile, depth), lambda b, i, s: (s[b] * tiles + i, 0)),
        pl.BlockSpec(weight.shape, lambda b, i, s: (0, 0, 0)),
    ]
    operands = [routes, rows, weight]
    if extra:
        in_specs.append(pl.BlockSpec(extra_weight.shape, lambda b, i, s: (0, 0, 0)))
        operands.append(extra_weight)
    flops = 4 * block_rows * depth * width * (experts + extra)
    return pl.pallas_call(
        functools.partial(pick_kernel, extra, transposed),
        out_shape=[jax.ShapeDtypeStruct((block_rows, total), BF)]
        + [jax.ShapeDtypeStruct((block_rows, total // 2), BF)] * 2,
        grid_spec=pltpu.PrefetchScalarGridSpec(
            num_scalar_prefetch=1,
            grid=(2, tiles),
            in_specs=in_specs,
            out_specs=[
                pl.BlockSpec((tile, total), lambda b, i, s: (jnp.where(b == 0, i, tiles - 1), 0)),
            ]
            + [
                pl.BlockSpec((tile, total // 2), lambda b, i, s: (jnp.where(b == 0, 0, i), 0))
            ]
            * 2,
        ),
        compiler_params=pltpu.CompilerParams(vmem_limit_bytes=VMEM_BYTES),
        cost_estimate=cost(
            flops,
            2 * (weight.size + 2 * block_rows * (depth + total)),
            scale,
        ),
    )(blocks, *operands)


def logits_kernel(order_ref, rows_ref, router_ref, *outs):
    product = lax.dot_general(
        router_ref[...], rows_ref[...], (((0,), (1,)), ((), ())), preferred_element_type=F32
    )
    for block, o_ref in enumerate(outs):

        @pl.when(pl.program_id(0) == block)
        def _():
            o_ref[...] = product


def block_logits(order, rows, router, length):
    depth, experts = router.shape
    count = rows.shape[0] // length
    return pl.pallas_call(
        logits_kernel,
        out_shape=[jax.ShapeDtypeStruct((experts, length), F32)] * count,
        grid_spec=pltpu.PrefetchScalarGridSpec(
            num_scalar_prefetch=1,
            grid=(count,),
            in_specs=[
                pl.BlockSpec((length, depth), lambda i, s: (s[i], 0)),
                pl.BlockSpec((depth, experts), lambda i, s: (0, 0)),
            ],
            out_specs=[pl.BlockSpec((experts, length), lambda i, s: (0, 0))] * count,
        ),
        compiler_params=pltpu.CompilerParams(vmem_limit_bytes=VMEM_BYTES),
        cost_estimate=cost(0, 0),
    )(order, rows, router)


def mixed_rows(routes, rows, expert):
    first = (routes[:, 0:1] == expert).astype(F32).astype(BF)
    second = (routes[:, 1:2] == expert).astype(F32).astype(BF)
    return rows[0] * first + rows[1] * second


def merge_kernel(count, extra, transposed, blocks_ref, routes_ref, *refs):
    rows_refs, refs = refs[:count], refs[count:]
    logit_refs, refs = (refs[:count], refs[count:]) if extra else ((), refs)
    w_ref, o_ref, rows_ref = refs[0], refs[-3], refs[-2]
    logits_ref = refs[-1]
    for block in range(count):

        @pl.when(pl.program_id(0) == block)
        def _():
            rows_ref[...] = rows_refs[block][...]
            if extra:
                logits_ref[...] = logit_refs[block][...]

    experts = w_ref.shape[0]
    contract = (((1,), (1 if transposed else 0,)), ((), ()))
    routes = routes_ref[...]
    total = jnp.zeros(o_ref.shape, F32)
    for expert in range(experts):
        mixed = mixed_rows(routes, rows_ref, expert)
        total += lax.dot_general(mixed, w_ref[expert], contract, preferred_element_type=F32)
    if extra:
        pair_ref, router_ref = refs[1:3]
        for place in range(2):
            total += lax.dot_general(
                rows_ref[2 + place], pair_ref[place], contract, preferred_element_type=F32
            )
        total += lax.dot_general(
            logits_ref[...], router_ref[...], contract, preferred_element_type=F32
        )
    o_ref[...] = total.astype(o_ref.dtype)


def merge_matmul(order, routes, blocks, weight, extras, transposed):
    count = len(blocks)
    parts, length, width = blocks[0].shape
    depth = weight.shape[1] if transposed else weight.shape[2]
    tile = min(256, length)
    tiles = length // tile

    def own_tile(place):
        return lambda b, i: jnp.where(b == place, i, jnp.where(b < place, 0, tiles - 1))

    def rows_spec(place):
        index = own_tile(place)
        return pl.BlockSpec((parts, tile, width), lambda b, i, s: (0, index(b, i), 0))

    def logits_spec(place, lanes):
        index = own_tile(place)
        return pl.BlockSpec((tile, lanes), lambda b, i, s: (index(b, i), 0))

    in_specs = [pl.BlockSpec((tile, 2), lambda b, i, s: (s[b] * tiles + i, 0))]
    in_specs += [rows_spec(place) for place in range(count)]
    operands = [routes, *blocks]
    lanes = 128
    if extras:
        logit_blocks, pair, router = extras
        lanes = logit_blocks[0].shape[1]
        in_specs += [logits_spec(place, lanes) for place in range(count)]
        operands += logit_blocks
    in_specs.append(pl.BlockSpec(weight.shape, lambda b, i, s: (0, 0, 0)))
    operands.append(weight)
    if extras:
        in_specs.append(pl.BlockSpec(pair.shape, lambda b, i, s: (0, 0, 0)))
        in_specs.append(pl.BlockSpec(router.shape, lambda b, i, s: (0, 0)))
        operands += [pair, router]
    return pl.pallas_call(
        functools.partial(merge_kernel, count, bool(extras), transposed),
        out_shape=jax.ShapeDtypeStruct((count * length, depth), BF),
        grid_spec=pltpu.PrefetchScalarGridSpec(
            num_scalar_prefetch=1,
            grid=(count, tiles),
            in_specs=in_specs,
            out_specs=pl.BlockSpec((tile, depth), lambda b, i, s: (s[b] * tiles + i, 0)),
            scratch_shapes=[pltpu.VMEM((parts, tile, width), BF), pltpu.VMEM((tile, lanes), BF)],
        ),
        compiler_params=pltpu.CompilerParams(vmem_limit_bytes=VMEM_BYTES),
        cost_estimate=cost(
            2 * count * length * depth * width * (weight.shape[0] + 2 * bool(extras)),
            2 * (weight.size + count * length * (parts * width + depth)),
        ),
    )(order, *operands)


def right_grad_kernel(scalars_ref, routes_ref, left_ref, *refs):
    blocks, o_ref = refs[:-1], refs[-1]
    expert = scalars_ref[len(blocks)] + pl.program_id(0)
    total = None
    for place, block_ref in enumerate(blocks):
        length = block_ref.shape[1]
        span = pl.ds(pl.multiple_of(scalars_ref[place] * length, length), length)
        mixed = mixed_rows(routes_ref[span, :], block_ref, expert)
        product = jnp.dot(left_ref[:, span], mixed, preferred_element_type=F32)
        total = product if total is None else total + product
    o_ref[0] = total.astype(o_ref.dtype)


def left_grad_kernel(scalars_ref, routes_ref, rows_ref, *refs):
    blocks, o_ref = refs[:-1], refs[-1]
    expert = scalars_ref[len(blocks)] + pl.program_id(0)
    total = None
    for place, block_ref in enumerate(blocks):
        length = block_ref.shape[2]
        span = pl.ds(pl.multiple_of(scalars_ref[place] * length, length), length)
        first = (routes_ref[0:1, span] == expert).astype(F32).astype(BF)
        second = (routes_ref[1:2, span] == expert).astype(F32).astype(BF)
        mixed = block_ref[0] * first + block_ref[1] * second
        product = jnp.dot(mixed, rows_ref[span, :], preferred_element_type=F32)
        total = product if total is None else total + product
    o_ref[0] = total.astype(o_ref.dtype)


def expert_grads(kernel, order, base, count, routes, rows, blocks, shape, dtype):
    whole = lambda array: pl.BlockSpec(array.shape, lambda i, s: (0,) * array.ndim)
    scalars = jnp.concatenate([order, base.astype(jnp.int32).reshape(1)])
    tokens = len(blocks) * blocks[0].shape[1]
    return pl.pallas_call(
        kernel,
        out_shape=jax.ShapeDtypeStruct((count,) + shape, dtype),
        grid_spec=pltpu.PrefetchScalarGridSpec(
            num_scalar_prefetch=1,
            grid=(count,),
            in_specs=[whole(routes), whole(rows)]
            + [pl.BlockSpec((2,) + item.shape[1:], lambda i, s: (0, 0, 0)) for item in blocks],
            out_specs=pl.BlockSpec((1,) + shape, lambda i, s: (i, 0, 0)),
        ),
        compiler_params=pltpu.CompilerParams(vmem_limit_bytes=VMEM_BYTES),
        cost_estimate=cost(
            2 * count * shape[0] * shape[1] * tokens,
            2 * rows.size + 4 * tokens * shape[1] + 4 * count * shape[0] * shape[1],
        ),
    )(scalars, routes, rows, *blocks)


def plain_grad_kernel(scalars_ref, left_ref, *refs):
    blocks, o_ref = refs[:-1], refs[-1]
    total = None
    for place, block_ref in enumerate(blocks):
        length = block_ref.shape[1]
        span = pl.ds(pl.multiple_of(scalars_ref[place] * length, length), length)
        if len(o_ref.shape) == 2:
            product = lax.dot_general(
                block_ref[0], left_ref[:, span], (((0,), (1,)), ((), ())),
                preferred_element_type=F32,
            )[: o_ref.shape[0]]
        else:
            product = jnp.dot(left_ref[:, span], block_ref[0], preferred_element_type=F32)
        total = product if total is None else total + product
    o_ref[...] = total.astype(o_ref.dtype).reshape(o_ref.shape)


def plain_grad(order, part, left, blocks, dtype, lines=0):
    depth = left.shape[0]
    _, length, width = blocks[0].shape
    scalars = jnp.concatenate([order, jnp.asarray(part, jnp.int32).reshape(1)])
    count = len(blocks)
    shape = (lines, depth) if lines else (1, depth, width)
    return pl.pallas_call(
        plain_grad_kernel,
        out_shape=jax.ShapeDtypeStruct(shape, dtype),
        grid_spec=pltpu.PrefetchScalarGridSpec(
            num_scalar_prefetch=1,
            grid=(1,),
            in_specs=[pl.BlockSpec(left.shape, lambda i, s: (0, 0))]
            + [pl.BlockSpec((1, length, width), lambda i, s: (s[count], 0, 0)) for _ in blocks],
            out_specs=pl.BlockSpec(shape, lambda i, s: (0,) * len(shape)),
        ),
        compiler_params=pltpu.CompilerParams(vmem_limit_bytes=VMEM_BYTES),
        cost_estimate=cost(
            2 * left.size * width, 2 * (left.size + count * length * width) + 4 * depth * width
        ),
    )(scalars, left, *blocks)


def turn_kernel(*refs):
    count = len(refs) // 2
    for rows_ref, o_ref in zip(refs[:count], refs[count:]):
        o_ref[0] = rows_ref[0].T


def turn(blocks):
    lead, rows, width = blocks[0].shape
    return pl.pallas_call(
        turn_kernel,
        out_shape=[jax.ShapeDtypeStruct((lead, width, rows), item.dtype) for item in blocks],
        grid=(lead,),
        in_specs=[pl.BlockSpec((1, rows, width), lambda i: (i, 0, 0)) for _ in blocks],
        out_specs=[pl.BlockSpec((1, width, rows), lambda i: (i, 0, 0)) for _ in blocks],
        compiler_params=pltpu.CompilerParams(vmem_limit_bytes=VMEM_BYTES),
        cost_estimate=cost(0, 4 * len(blocks) * lead * rows * width),
    )(*blocks)


def spread_kernel(groups, starts_ref, places_ref, rows_ref, *refs):
    outs, totals = refs[: len(groups)], refs[len(groups) :]
    blocks = [bits for group in groups for bits in group]
    tokens = rows_ref.shape[0]
    for total_ref in totals:
        total_ref[...] = jnp.zeros(total_ref.shape, F32)
    slot = lax.broadcasted_iota(jnp.int32, (WINDOW, TILE), 0)
    for index in range(tokens // TILE):
        span = slice(index * TILE, (index + 1) * TILE)
        rows = rows_ref[span, :]
        for bits, total_ref in zip(blocks, totals):
            start = pl.multiple_of(starts_ref[bits, index], 16)
            hot = (slot == places_ref[bits : bits + 1, span] - start).astype(F32).astype(BF)
            product = jnp.dot(hot, rows, preferred_element_type=F32)
            total_ref[pl.ds(start, WINDOW), :] += product
    place = 0
    for group, o_ref in zip(groups, outs):
        for lead in range(len(group)):
            value = totals[place][...].astype(BF)
            if len(group) == 1:
                o_ref[...] = value
            else:
                o_ref[lead] = value
            place += 1


def spread_rows(starts, places, rows, slots, groups):
    tokens, width = rows.shape
    shapes = [
        (slots, width) if len(group) == 1 else (len(group), slots, width) for group in groups
    ]
    count = sum(len(group) for group in groups)
    return pl.pallas_call(
        functools.partial(spread_kernel, groups),
        out_shape=[jax.ShapeDtypeStruct(shape, BF) for shape in shapes],
        grid_spec=pltpu.PrefetchScalarGridSpec(
            num_scalar_prefetch=1,
            grid=(1,),
            in_specs=[
                pl.BlockSpec(places.shape, lambda i, s: (0, 0)),
                pl.BlockSpec((tokens, width), lambda i, s: (0, 0)),
            ],
            out_specs=[
                pl.BlockSpec(shape, lambda i, s, n=len(shape): (0,) * n) for shape in shapes
            ],
            scratch_shapes=[pltpu.VMEM((slots, width), F32) for _ in range(count)],
        ),
        compiler_params=pltpu.CompilerParams(vmem_limit_bytes=VMEM_BYTES),
        cost_estimate=cost(
            4 * count * WINDOW * tokens * width,
            2 * (tokens + count * slots) * width,
        ),
    )(starts, places, rows)


def gather_kernel(tiles, starts_ref, places_ref, *refs):
    o_ref = refs[-1]
    slot = lax.broadcasted_iota(jnp.int32, (TILE, WINDOW), 1)
    for index in range(tiles):
        span = slice(index * TILE, (index + 1) * TILE)
        total = jnp.zeros((TILE, o_ref.shape[1]), F32)
        for block, block_ref in enumerate(refs[:-1]):
            start = pl.multiple_of(starts_ref[block, pl.program_id(0) * tiles + index], 16)
            hot = (slot == places_ref[span, block : block + 1] - start).astype(F32).astype(BF)
            window = pl.ds(start, WINDOW)
            rows = block_ref[0, window, :] if len(block_ref.shape) == 3 else block_ref[window, :]
            total += jnp.dot(hot, rows, preferred_element_type=F32)
        o_ref[span, :] = total.astype(o_ref.dtype)


def gather_slots(starts, places, blocks):
    tokens = places.shape[0]
    lists = [item if isinstance(item, tuple) else (item, None) for item in blocks]
    slots, width = lists[0][0].shape[-2:]
    tiles = 4

    def spec(place):
        if place is None:
            return pl.BlockSpec((slots, width), lambda i, s: (0, 0))
        return pl.BlockSpec((1, slots, width), lambda i, s: (place, 0, 0))

    tile = tiles * TILE
    return pl.pallas_call(
        functools.partial(gather_kernel, tiles),
        out_shape=jax.ShapeDtypeStruct((tokens, width), BF),
        grid_spec=pltpu.PrefetchScalarGridSpec(
            num_scalar_prefetch=1,
            grid=(tokens // tile,),
            in_specs=[pl.BlockSpec((tile, places.shape[1]), lambda i, s: (i, 0))]
            + [spec(place) for _, place in lists],
            out_specs=pl.BlockSpec((tile, width), lambda i, s: (i, 0)),
        ),
        compiler_params=pltpu.CompilerParams(vmem_limit_bytes=VMEM_BYTES),
        cost_estimate=cost(
            4 * WINDOW * tokens * width * len(blocks),
            2 * (tokens + slots * len(blocks)) * width,
        ),
    )(starts, places, *[item for item, _ in lists])


def dots_kernel(transposed, lead, terms, count, stacked, *refs):
    outs = refs[terms * (1 + count) :]
    contract = (((1,), (1 if transposed else 0,)), ((), ()))
    operands = [ref[0] if flag else ref[...] for ref, flag in zip(refs, lead)]
    for place in range(count):
        o_ref = outs[0 if stacked else place]
        total = None
        for term in range(terms):
            right = operands[terms * (1 + place) + term]
            product = lax.dot_general(
                operands[term], right, contract, preferred_element_type=F32
            )
            total = product if total is None else total + product
        if stacked:
            outs[0][place] = total.astype(outs[0].dtype)
        else:
            o_ref[...] = total.astype(o_ref.dtype)


def dots(lefts, right_lists, transposed, dtype, stacked=False):
    operands, specs, lead = [], [], []
    rows = lefts[0][0].shape[1] if isinstance(lefts[0], tuple) else lefts[0].shape[0]
    tile = rows // 2 if rows % 32 == 0 else rows
    flops, size = 0, 0
    for side, items in enumerate([lefts] + list(right_lists)):
        for item in items:
            array, place = item if isinstance(item, tuple) else (item, None)
            shape = array.shape[-2:]
            block = (tile, shape[1]) if side == 0 else shape
            if place is None:
                specs.append(
                    pl.BlockSpec(block, (lambda i: (i, 0)) if side == 0 else (lambda i: (0, 0)))
                )
            elif side == 0:
                specs.append(pl.BlockSpec((1,) + block, lambda i, p=place: (p, i, 0)))
            else:
                specs.append(pl.BlockSpec((1,) + block, lambda i, p=place: (p, 0, 0)))
            operands.append(array)
            lead.append(place is not None)
            size += 2 * shape[0] * shape[1]
            if side:
                flops += 2 * rows * shape[0] * shape[1]
    width = shape[0] if transposed else shape[1]
    count = len(right_lists)
    if stacked:
        out_shape = [jax.ShapeDtypeStruct((count, rows, width), dtype)]
        out_specs = [pl.BlockSpec((count, tile, width), lambda i: (0, i, 0))]
    else:
        out_shape = [jax.ShapeDtypeStruct((rows, width), dtype)] * count
        out_specs = [pl.BlockSpec((tile, width), lambda i: (i, 0))] * count
    return pl.pallas_call(
        functools.partial(dots_kernel, transposed, lead, len(lefts), count, stacked),
        out_shape=out_shape,
        grid=(rows // tile,),
        in_specs=specs,
        out_specs=out_specs,
        compiler_params=pltpu.CompilerParams(vmem_limit_bytes=VMEM_BYTES),
        cost_estimate=cost(
            2 * flops,
            size + 2 * count * rows * width,
        ),
    )(*operands)


def pair_kernel(count, own_ref, other_ref, *refs):
    for place in range(count):
        for lead, left_ref in enumerate((own_ref, other_ref)):

            @pl.when(pl.program_id(0) == 2 * place + lead)
            def _():
                product = jnp.dot(left_ref[...], refs[place][0], preferred_element_type=F32)
                refs[count][0] = product.astype(refs[count].dtype)


def pair_dots(lefts, right_list, scale=COST):
    rows, depth = lefts[0].shape
    width = right_list[0].shape[2]
    count = len(right_list)

    def spec(place):
        return pl.BlockSpec(
            (1, depth, width), lambda i: (jnp.clip(i - 2 * place, 0, 1), 0, 0)
        )

    return pl.pallas_call(
        functools.partial(pair_kernel, count),
        out_shape=jax.ShapeDtypeStruct((2 * count, rows, width), BF),
        grid=(2 * count,),
        in_specs=[pl.BlockSpec((rows, depth), lambda i: (0, 0))] * 2
        + [spec(place) for place in range(count)],
        out_specs=pl.BlockSpec((1, rows, width), lambda i: (i, 0, 0)),
        compiler_params=pltpu.CompilerParams(vmem_limit_bytes=VMEM_BYTES),
        cost_estimate=cost(4 * count * rows * depth * width, 4 * rows * depth, scale),
    )(*lefts, *right_list)


def turned_kernel(pairs, rights, lead, merged, *refs):
    contract = (((0,), (0,)), ((), ()))
    outs = list(refs[2 * pairs + 2 * rights :])
    operands = [ref[0] if flag else ref[...] for ref, flag in zip(refs, lead)]
    for pair in range(pairs):
        for place, o_ref in enumerate(outs):
            total = None
            for batch in (0, 1):
                left = operands[2 * pair + batch]
                right = operands[2 * pairs + 2 * place + batch]
                if len(outs) == 3 and place == 2:
                    left, right = right, left
                product = lax.dot_general(left, right, contract, preferred_element_type=F32)
                total = product if total is None else total + product
            lead = pair
            if merged and place == 1:
                o_ref, lead = (outs[0], pairs) if pair else (o_ref, 0)
            o_ref[lead] = total[: o_ref.shape[1]].astype(o_ref.dtype)


def turned_dots(lefts, rights, dtypes, merged=False):
    operands, specs, lead, shapes = [], [], [], []
    for item in [each for pair in list(lefts) + list(rights) for each in pair]:
        array, place = item if isinstance(item, tuple) else (item, None)
        shape = array.shape[-2:]
        if place is None:
            specs.append(pl.BlockSpec(shape, lambda i: (0, 0)))
        else:
            specs.append(pl.BlockSpec((1,) + shape, lambda i, p=place: (p, 0, 0)))
        operands.append(array)
        lead.append(place is not None)
        shapes.append(shape)
    pairs, depth = len(lefts), shapes[0][1]
    outs = []
    flops = 0
    for place, dtype in enumerate(dtypes):
        width = shapes[2 * pairs + 2 * place][1]
        flops += 4 * pairs * shapes[0][0] * depth * width
        shape = (pairs, 8, depth) if place == 2 else (pairs, depth, width)
        if merged and place < 2:
            shape = (1 if place else pairs + 1, depth, width)
        outs.append(jax.ShapeDtypeStruct(shape, dtype))
    return pl.pallas_call(
        functools.partial(turned_kernel, pairs, len(rights), lead, merged),
        out_shape=outs,
        grid=(1,),
        in_specs=specs,
        out_specs=[pl.BlockSpec(out.shape, lambda i: (0, 0, 0)) for out in outs],
        compiler_params=pltpu.CompilerParams(vmem_limit_bytes=VMEM_BYTES),
        cost_estimate=cost(flops, flops // 300),
    )(*operands)


def flat(ref):
    return ref[0] if len(ref.shape) == 3 else ref[...]


def expert_kernel(count, owner_ref, other_ref, own_ref, sent_ref, *refs):
    rows_refs, gate_refs = refs[:count], refs[count : 2 * count]
    up_refs, router_refs = refs[2 * count : 3 * count], refs[3 * count : 4 * count]
    act_ref, gate_out, up_out, logit_out = refs[4 * count :]
    gate_pre = up_pre = logits = None
    for index in range(count):
        rows = flat(rows_refs[index])
        gate_part = jnp.dot(rows, flat(gate_refs[index]), preferred_element_type=F32)
        up_part = jnp.dot(rows, flat(up_refs[index]), preferred_element_type=F32)
        logit_part = jnp.dot(rows, router_refs[index][...], preferred_element_type=F32)
        gate_pre = gate_part if index == 0 else gate_pre + gate_part
        up_pre = up_part if index == 0 else up_pre + up_part
        logits = logit_part if index == 0 else logits + logit_part
    lane = lax.broadcasted_iota(jnp.int32, logits.shape, 1)
    signs = (lane == owner_ref[0]).astype(F32) - (lane == other_ref[...]).astype(F32)
    gate = jax.nn.sigmoid(jnp.sum(logits * signs, axis=1, keepdims=True))
    grad_act = own_ref[...] + sent_ref[...].astype(F32)
    sigmoid_gate = jax.nn.sigmoid(gate_pre)
    swish_gate = gate_pre * sigmoid_gate
    activation = swish_gate * up_pre
    act_ref[...] = (activation * gate).astype(BF)
    share = jnp.sum(grad_act * activation, axis=1, keepdims=True) * gate * (1.0 - gate)
    logit_out[...] = (share * signs).astype(BF)
    grad_activation = grad_act * gate
    swish_slope = sigmoid_gate * (1.0 + gate_pre * (1.0 - sigmoid_gate))
    gate_out[...] = (grad_activation * up_pre * swish_slope).astype(BF)
    up_out[...] = (grad_activation * swish_gate).astype(BF)


def expert_forward(owner, other, own, sent, rows, gates, ups, routers):
    slots, depth = own.shape[0], routers[0].shape[0]
    hidden = own.shape[1]
    lanes = routers[0].shape[1]
    tile = slots // 2 if slots % 32 == 0 else slots
    row_spec = lambda width: pl.BlockSpec((tile, width), lambda i, s: (i, 0))

    def rows_spec(item):
        if isinstance(item, tuple):
            return pl.BlockSpec((1, tile, depth), lambda i, s: (item[1], i, 0))
        return row_spec(depth)


    def whole(item):
        if isinstance(item, tuple):
            return pl.BlockSpec((1,) + item[0].shape[1:], lambda i, s: (item[1], 0, 0))
        return pl.BlockSpec(item.shape, lambda i, s: (0, 0))

    weights = list(gates) + list(ups) + list(routers)
    out_shapes = [jax.ShapeDtypeStruct((slots, hidden), BF)] * 3
    out_shapes.append(jax.ShapeDtypeStruct((slots, lanes), BF))
    return pl.pallas_call(
        functools.partial(expert_kernel, len(rows)),
        out_shape=out_shapes,
        grid_spec=pltpu.PrefetchScalarGridSpec(
            num_scalar_prefetch=1,
            grid=(slots // tile,),
            in_specs=[row_spec(1), row_spec(hidden), row_spec(hidden)]
            + [rows_spec(item) for item in rows]
            + [whole(item) for item in weights],
            out_specs=[row_spec(item.shape[1]) for item in out_shapes],
        ),
        compiler_params=pltpu.CompilerParams(vmem_limit_bytes=VMEM_BYTES),
        cost_estimate=cost(
            4 * len(rows) * slots * depth * hidden,
            4 * len(rows) * depth * hidden + 12 * slots * hidden,
        ),
    )(
        owner.reshape(1),
        other,
        own,
        sent,
        *[item[0] if isinstance(item, tuple) else item for item in list(rows) + weights],
    )


def assemble_kernel(chained, order_ref, *refs):
    for block, ref in enumerate(refs[1:-1] if chained else refs[:-1]):

        @pl.when(pl.program_id(0) == block)
        def _():
            refs[-1][0] = flat(ref).astype(F32)


def assemble(order, start, total, blocks, before=None):
    count = len(blocks)
    chained = before is not None
    arrays = [item[0] if isinstance(item, tuple) else item for item in blocks]
    rows, width = arrays[0].shape[-2:]
    tiles = ASSEMBLE if rows % (16 * ASSEMBLE) == 0 else 1

    def spec(place, item):
        def tile_of(b, i):
            return jnp.where(b == place, i, jnp.where(b < place, 0, tiles - 1))

        if isinstance(item, tuple):
            return pl.BlockSpec(
                (1, rows // tiles, width), lambda b, i, s: (item[1], tile_of(b, i), 0)
            )
        return pl.BlockSpec((rows // tiles, width), lambda b, i, s: (tile_of(b, i), 0))

    return pl.pallas_call(
        functools.partial(assemble_kernel, chained),
        out_shape=jax.ShapeDtypeStruct((total, rows, width), F32),
        input_output_aliases={1: 0} if chained else {},
        grid_spec=pltpu.PrefetchScalarGridSpec(
            num_scalar_prefetch=1,
            grid=(count, tiles),
            in_specs=[pl.BlockSpec(memory_space=pl.ANY)] * chained
            + [spec(place, item) for place, item in enumerate(blocks)],
            out_specs=pl.BlockSpec(
                (1, rows // tiles, width), lambda b, i, s: (s[start + b], i, 0)
            ),
        ),
        compiler_params=pltpu.CompilerParams(vmem_limit_bytes=VMEM_BYTES),
        cost_estimate=cost(0, 7 * count * rows * width),
    )(order, *([before] if chained else []), *arrays)


def allowed_keys(row_segments, column_segments):
    length = row_segments.shape[0]
    query = lax.broadcasted_iota(jnp.int32, (length, length), 0)
    key = lax.broadcasted_iota(jnp.int32, (length, length), 1)
    same = (column_segments == 0) | (column_segments == row_segments)
    return same & (key <= query)


def weights_of(query, key, allowed):
    scores = lax.dot_general(query, key, (((1,), (1,)), ((), ())), preferred_element_type=F32)
    scores = jnp.where(allowed, scores * HD ** (-0.5), NEGATIVE)
    weights = jnp.exp(scores - jnp.max(scores, axis=1, keepdims=True))
    return weights / jnp.sum(weights, axis=1, keepdims=True)


def attend_kernel(
    logits_ref, routes_ref, kept_ref, rows_ref, columns_ref, *refs
):
    parts, refs = refs[:12], refs[12:]
    saved_ref, mixed_ref, gated_ref, side_ref, cos_ref, sin_ref = refs

    @pl.when(pl.program_id(0) == 0)
    def _():
        logits = logits_ref[...]
        label = lax.broadcasted_iota(jnp.int32, logits.shape, 0)
        picked = [
            jnp.sum(jnp.where(label == routes_ref[place : place + 1, :], logits, 0.0), axis=0)
            for place in (0, 1)
        ]
        gates = [
            jax.nn.sigmoid(picked[place] - picked[1 - place])[None, :] for place in (0, 1)
        ]
        lines = [gates[place] * kept_ref[place : place + 1, :] for place in (0, 1)]
        lines.append(gates[0] * gates[1])
        lines += [routes_ref[place : place + 1, :].astype(F32) for place in (0, 1)]
        lines += [kept_ref[place : place + 1, :] for place in (0, 1)]
        lines.append(jnp.zeros((128 - len(lines), logits.shape[1]), F32))
        side_ref[...] = jnp.concatenate(lines, axis=0).T
        cos_ref[...], sin_ref[...] = rope_lines(rows_ref[...], columns_ref[...])

    summed = [
        parts[place][...].astype(F32)
        + parts[4 + place][...].astype(F32)
        + parts[8 + place][...].astype(F32)
        for place in range(4)
    ]
    cosine, sine = cos_ref[...], sin_ref[...]
    turned = [
        (item * cosine + pltpu.roll(item, HD // 2, 1) * sine).astype(BF) for item in summed[:3]
    ]
    turned.append(summed[3].astype(BF))
    for place in range(4):
        saved_ref[place] = turned[place]
    allowed = allowed_keys(rows_ref[...], columns_ref[...])
    for place in range(2):
        probs = weights_of(turned[place], turned[2], allowed).astype(BF)
        mixed = jnp.dot(probs, turned[3], preferred_element_type=F32)
        mixed_ref[place] = mixed
        gated_ref[place] = (mixed * side_ref[:, place : place + 1]).astype(BF)


def head_parts(parts, count, length, heads):
    specs, arrays = [], []
    for part in parts:
        each = count // len(part)
        for place in range(count):
            start = place % each * heads
            specs.append(pl.BlockSpec((length, HD), lambda h, s=start: (0, s + h)))
            arrays.append(part[place // each])
    return specs, arrays


def attend(logits, routes, kept, segments, parts):
    length = logits.shape[1]
    heads = parts[0][0].shape[1] // (4 * HD)
    whole = lambda array: pl.BlockSpec(array.shape, lambda h: (0, 0))
    part_specs, part_arrays = head_parts(parts, 4, length, heads)
    small = [logits, routes, kept, segments.reshape(length, 1), segments.reshape(1, length)]
    return pl.pallas_call(
        attend_kernel,
        out_shape=[
            jax.ShapeDtypeStruct((4, length, heads * HD), BF),
            jax.ShapeDtypeStruct((2, length, heads * HD), F32),
            jax.ShapeDtypeStruct((2, length, heads * HD), BF),
        ]
        + [jax.ShapeDtypeStruct((length, 128), F32)] * 3,
        grid=(heads,),
        in_specs=[whole(item) for item in small] + part_specs,
        out_specs=[
            pl.BlockSpec((count, length, HD), lambda h: (0, 0, h)) for count in (4, 2, 2)
        ]
        + [pl.BlockSpec((length, 128), lambda h: (0, 0))] * 3,
        compiler_params=pltpu.CompilerParams(vmem_limit_bytes=VMEM_BYTES),
        cost_estimate=cost(
            16 * heads * length * length * HD,
            12 * length * heads * HD * 4,
        ),
    )(*small, *part_arrays)


def attend_back_kernel(
    side_ref, rows_ref, columns_ref, cos_ref, sin_ref, saved_ref, mixed_ref, *refs
):
    parts, (out_ref, logit_ref, share_ref) = refs[:6], refs[6:]
    allowed = allowed_keys(rows_ref[...], columns_ref[...])
    key, value = saved_ref[2], saved_ref[3]
    cosine, sine = cos_ref[...], sin_ref[...]
    scale = HD ** (-0.5)
    over_rows = (((0,), (0,)), ((), ()))
    over_last = (((1,), (1,)), ((), ()))

    def unturn(item):
        return (item * cosine - pltpu.roll(item, HD // 2, 1) * sine).astype(BF)

    @pl.when(pl.program_id(0) == 0)
    def _():
        share_ref[...] = jnp.zeros(share_ref.shape, F32)

    lane = lax.broadcasted_iota(jnp.int32, share_ref.shape, 1)
    grad_key = grad_value = 0.0
    for place in range(2):
        grad = (
            parts[place][...].astype(F32)
            + parts[2 + place][...].astype(F32)
            + parts[4 + place][...].astype(F32)
        )
        share = jnp.sum(grad * mixed_ref[place], axis=1, keepdims=True)
        share_ref[...] += jnp.where(lane == place, share, 0.0)
        grad = (grad * side_ref[:, place : place + 1]).astype(BF)
        query = saved_ref[place]
        probs = weights_of(query, key, allowed)
        grad_value += lax.dot_general(
            probs.astype(BF), grad, over_rows, preferred_element_type=F32
        )
        grad_probs = lax.dot_general(grad, value, over_last, preferred_element_type=F32)
        centred = jnp.sum(probs * grad_probs, axis=1, keepdims=True)
        grad_scores = (probs * (grad_probs - centred)).astype(BF)
        grad_query = jnp.dot(grad_scores, key, preferred_element_type=F32) * scale
        out_ref[place] = unturn(grad_query)
        grad_key += lax.dot_general(
            grad_scores, query, over_rows, preferred_element_type=F32
        )
    out_ref[2] = unturn(grad_key * scale)
    out_ref[3] = grad_value.astype(BF)

    @pl.when(pl.program_id(0) == pl.num_programs(0) - 1)
    def _():
        shares = [
            share_ref[:, place : place + 1] * side_ref[:, 5 + place : 6 + place]
            for place in (0, 1)
        ]
        share = (shares[0] - shares[1]) * side_ref[:, 2:3]
        label = lane.astype(F32)
        signs = (label == side_ref[:, 3:4]).astype(F32) - (label == side_ref[:, 4:5]).astype(F32)
        logit_ref[...] = (share * signs).astype(BF)


def attend_back(side, segments, cosine, sine, saved, mixed, parts):
    length = side.shape[0]
    heads = saved.shape[2] // HD
    whole = lambda array: pl.BlockSpec(array.shape, lambda h: (0, 0))
    part_specs, part_arrays = head_parts(parts, 2, length, heads)
    small = [side, segments.reshape(length, 1), segments.reshape(1, length), cosine, sine]
    return pl.pallas_call(
        attend_back_kernel,
        out_shape=[
            jax.ShapeDtypeStruct((4, length, heads * HD), BF),
            jax.ShapeDtypeStruct((length, 128), BF),
        ],
        grid=(heads,),
        in_specs=[whole(item) for item in small]
        + [pl.BlockSpec((count, length, HD), lambda h: (0, 0, h)) for count in (4, 2)]
        + part_specs,
        out_specs=[
            pl.BlockSpec((4, length, HD), lambda h: (0, 0, h)),
            pl.BlockSpec((length, 128), lambda h: (0, 0)),
        ],
        scratch_shapes=[pltpu.VMEM((length, 128), F32)],
        compiler_params=pltpu.CompilerParams(vmem_limit_bytes=VMEM_BYTES),
        cost_estimate=cost(
            40 * heads * length * length * HD,
            20 * length * heads * HD * 4,
        ),
    )(*small, saved, mixed, *part_arrays)


def swap(value, axes, bits, size):
    if bits == 0:
        return value
    return lax.ppermute(value, axes, [(i, i ^ bits) for i in range(size)])


def row_gather(values):
    return lax.all_gather(values, "row", axis=0, tiled=True)


def row_total(values, *waits):
    total = lax.psum_scatter(values, "row", scatter_dimension=0, tiled=True)
    return (after(total, *waits) if waits else total).astype(F32)


def col_total(values):
    return lax.psum(values, "col")


def small_total(value, axes):
    for axis in axes:
        size = lax.axis_size(axis)
        bits = 1
        while bits < size:
            value = value + swap(value, axis, bits, size)
            bits *= 2
    return value


def norm_factor(rows_in):
    squares = col_total(jnp.sum(rows_in * rows_in, axis=1))
    return lax.rsqrt(squares / D + EPSILON)


def norm_backward(rows_in, factor, gain_row, grad_in, *waits):
    scaled = grad_in * gain_row
    inner_sum = jnp.sum(scaled * rows_in, axis=1)
    inner_sum = col_total(after(inner_sum, *waits) if waits else inner_sum)[:, None]
    gain_grad = jnp.sum(grad_in * rows_in * factor, axis=0)
    return (factor * scaled - rows_in * factor**3 * inner_sum / D, gain_grad)


def local(
    hidden_in,
    gain_attn,
    router_attn,
    query_weight,
    kv_weight,
    out_weight,
    gain_ffn,
    router_ffn,
    gate_weight,
    up_weight,
    down_weight,
    attn_routes,
    ffn_routes,
    attn_order,
    ffn_order,
    segment_ids,
    d_out,
):
    dp_count, col_count = lax.axis_size("dp"), lax.axis_size("col")
    dp_index, col_index = lax.axis_index("dp"), lax.axis_index("col")
    owners = dp_count * col_count
    owner = dp_index * col_count + col_index
    batch_rows = attn_routes.shape[0]
    group_rows = batch_rows // col_count
    features = hidden_in.shape[1]
    attn_experts = query_weight.shape[0]
    ffn_experts = gate_weight.shape[0]
    half_experts = attn_experts // dp_count
    attn_capacity = 5 * batch_rows // (2 * attn_experts)
    slots = 5 * batch_rows // (2 * ffn_experts)
    head_width = query_weight.shape[2]
    pair_axes = ("dp", "col")

    def cross(pair, *waits):
        received = swap(pair, "col", 2, col_count)
        hop = swap(lead_block(after(received, *waits), 1), "col", 1, col_count)
        return [(received, 0), (hop, 0)]

    def fence(rows, numbers, times=1):
        token = tip(rows)
        for _ in range(times):
            token = swap(token, "col", 1, col_count)
        token = token[0, 0]
        return numbers + (token != token).astype(jnp.int32)

    def arrays(blocks):
        return [item[0] if isinstance(item, tuple) else item for item in blocks]

    def flagged(blocks):
        return [(item, 0) for item in blocks]

    offsets = (owner ^ jnp.arange(owners, dtype=jnp.int32)).astype(jnp.int32)
    block_order = (col_index ^ jnp.arange(col_count, dtype=jnp.int32)).astype(jnp.int32)
    hidden_all = row_gather(hidden_in)
    rows_in = hidden_in.astype(F32)
    factor_a = norm_factor(rows_in)
    gate_cross = cross(take_blocks(gate_weight, after(offsets, factor_a), 2, 1, 2))
    factor_a_all = row_gather(factor_a)
    lane_router_f = jnp.pad(
        after(router_ffn, factor_a), ((0, 0), (0, 128 - ffn_experts))
    )
    router_blocks = [swap(lane_router_f, "col", bits, col_count) for bits in range(col_count)]
    owner_rows, owner_starts = token_slots(
        ffn_routes, after(ffn_order, factor_a), offsets, ffn_experts, slots
    )
    (
        hidden_all,
        owner_rows,
        owner_starts,
        offsets,
        block_order,
    ) = lax.optimization_barrier((hidden_all, owner_rows, owner_starts, offsets, block_order))
    grad_out_all = row_gather(after(d_out, hidden_all))

    gain_a = gain_attn.astype(F32)
    normed_all = (hidden_all.astype(F32) * factor_a_all[:, None] * gain_a).astype(BF)

    def col_scatter(
        rows, weight, extra_weight, transposed, first_waits, near_waits, near_first, *far_waits
    ):
        def part(blocks, scale):
            kept, *sent = pick_matmul(
                blocks, attn_routes, rows, weight, extra_weight, group_rows, transposed, scale
            )
            return kept, [swap(item, "col", 1, col_count) for item in sent]

        near_order = after(block_order[0:2], *first_waits)
        far_order = after(block_order[2:4], *first_waits)
        if near_first:
            near = part(near_order, COST)
            far_order = after(far_order, near[0])
        kept, received = part(far_order, COST)
        far = join_halves(after(kept, *far_waits) if far_waits else kept, received)
        if not near_first:
            near = part(after(near_order, far, *near_waits), 1)
        return [[near[0]], near[1], far, [swap(far, "col", 2, col_count)]]

    projected = col_scatter(
        normed_all, query_weight, kv_weight, False, [], [gate_cross[0][0]], False
    )

    far_sent = projected[2]
    logits_sent = block_logits(
        after(block_order, far_sent), normed_all, router_attn, group_rows
    )
    attn_kept = kept_pairs(
        attn_routes, after(attn_order, logits_sent[0]), attn_experts, attn_capacity
    )
    segments = segment_ids.reshape(-1)
    kept_a = attn_kept.reshape(2, batch_rows // TILE, TILE)
    kept_a = lax.dynamic_slice_in_dim(
        kept_a, col_index * (group_rows // TILE), group_rows // TILE, 1
    ).reshape(2, group_rows)
    routes_a = lax.dynamic_slice_in_dim(
        after(attn_routes, far_sent), col_index * group_rows, group_rows, 0
    ).T

    up_pair = take_blocks(up_weight, after(offsets, far_sent), 2, 1, 2)
    route_sums = jnp.sum(after(ffn_routes, far_sent), axis=1).astype(BF)
    route_sums = jnp.broadcast_to(route_sums[:, None], (batch_rows, 128))
    near_sums, far_sums = spread_rows(
        after(owner_starts, logits_sent[0]), owner_rows, route_sums, slots, [(0,), (col_count,)]
    )
    far_sums = swap(far_sums[:, 0:8], pair_axes, col_count, owners)
    slot_other = [item[:, 0:1].astype(jnp.int32) - owner for item in (near_sums, far_sums)]
    logits_sent, _ = lax.optimization_barrier(
        (logits_sent, (up_pair, kept_a, routes_a, slot_other))
    )
    logits_a = sum(
        swap(logits_sent[bits], "col", bits, col_count) for bits in range(col_count)
    )
    saved, attended, gated_out, side, cosine, sine_rows = attend(
        logits_a,
        routes_a,
        kept_a,
        segments,
        projected[0:2] + projected[3:],
    )

    half_bits = (0, 1, col_count, col_count + 1)
    grad_groups = spread_rows(
        after(owner_starts, gated_out),
        owner_rows,
        grad_out_all,
        slots,
        [(bits, bits ^ 2) for bits in half_bits],
    )
    grad_far = [swap(grad_groups[place], pair_axes, col_count, owners) for place in (2, 3)]

    lane_router = jnp.pad(
        after(router_attn, gated_out), ((0, 0), (0, 128 - attn_experts))
    )
    down_sent = [
        take_blocks(down_weight, after(offsets, grad_groups[0]), bits, 2, 2) for bits in (0, 1)
    ]

    def col_blocks(block, *waits):
        far = swap(block, "col", 2, col_count)
        near = swap(block, "col", 1, col_count)
        return [block, near, far, swap(after(far, *waits), "col", 1, col_count)]

    gated_blocks = col_blocks(gated_out, lane_router, *down_sent, *router_blocks)
    up_received = swap(after(up_pair, gated_blocks[2]), "col", 2, col_count)
    attn_part = merge_matmul(block_order, attn_routes, gated_blocks, out_weight, (), False)
    down_pairs = [down_sent[0], swap(down_sent[1], "col", 1, col_count)]

    grad_pairs = [grad_groups[0], swap(grad_groups[1], "col", 1, col_count)]

    def grad_act_part(batch, lead, dtype, *waits):
        return dots(
            [(array, lead) for array in grad_pairs[2 * batch : 2 * batch + 2]],
            [[(after(down_pairs[0], *waits), lead), (down_pairs[1], lead)]],
            True,
            dtype,
        )[0]

    grad_act_out = [grad_act_part(0, 1, BF, attn_part)]
    up_side = lead_block(after(up_received, grad_far[0], *grad_act_out), 1)
    up_cross = [(up_received, 0), (swap(up_side, "col", 1, col_count), 0)]
    middle = rows_in + row_total(attn_part, up_cross[1][0])
    gain_f = gain_ffn.astype(F32)
    factor_f = norm_factor(middle)[:, None]
    normed_f = (middle * factor_f * gain_f).astype(BF)
    normed_f_all = row_gather(normed_f)
    gate_near, gate_own = [
        take_blocks(gate_weight, after(offsets, normed_f), bits, 1, 1) for bits in (1, 0)
    ]
    up_near, up_own = [
        take_blocks(up_weight, after(offsets, gate_own), bits, 1, 1) for bits in (1, 0)
    ]
    gate_blocks = flagged([gate_own, swap(gate_near, "col", 1, col_count)]) + gate_cross
    up_blocks = flagged([up_own, swap(up_near, "col", 1, col_count)]) + up_cross

    grad_act_sent = [swap(after(grad_act_out[0], normed_f), "col", 2, col_count)]
    own_early = grad_act_part(0, 0, F32, normed_f)
    grad_hop = after(grad_far[1], own_early, up_own, up_near, grad_act_sent[0])
    grad_pairs += [grad_far[0], swap(grad_hop, "col", 1, col_count)]
    grad_act_out.append(grad_act_part(1, 1, BF, normed_f))
    grad_act_sent.append(swap(grad_act_out[1], "col", 2, col_count))
    send_starts = after(owner_starts, up_own, up_near, own_early, grad_act_out[1])
    order = [(2, 3), (6,), (7,)], [(4,), (5,), (1,), (0,)]
    slots_f = {}
    for part in order:
        blocks = spread_rows(send_starts, owner_rows, normed_f_all, slots, part)
        for group, block in zip(part, blocks):
            received = swap(block, pair_axes, group[0], owners)
            if len(group) == 1:
                slots_f[group[0]] = received
            else:
                slots_f[group[0]] = (received, 0)
                side_block = swap(lead_block(received, 1), "col", 1, col_count)
                slots_f[group[1]] = (side_block, 0)
        send_starts = after(send_starts, *blocks)
    normed_turned = turn([after(normed_all, blocks[0])[None]])[0][0]
    gated_turned = turn([after(gated_blocks[0], blocks[0])] + gated_blocks[1:])
    acts, grad_gates, grad_ups, grad_logits = [], [], [], []
    back_blocks = {}

    def send_back(pair):
        batch = pair[0] // col_count
        blocks = dots(
            [grad_gates[batch], grad_ups[batch], grad_logits[batch]],
            [
                [part[bits % col_count] for part in (gate_blocks, up_blocks, router_blocks)]
                for bits in pair
            ],
            True,
            BF,
            pair[0] == col_count + 2,
        )
        if len(blocks) == 1:
            received = swap(blocks[0], pair_axes, pair[0], owners)
            back_blocks[pair[0]] = (received, 0)
            hop = swap(lead_block(received, 1), "col", 1, col_count)
            back_blocks[pair[1]] = (hop, 0)
        else:
            for bits, block in zip(pair, blocks):
                back_blocks[bits] = swap(block, pair_axes, bits, owners)
        return blocks[0]

    grad_act_own = [own_early, grad_act_part(1, 0, F32, blocks[0])]
    back_sent = after(blocks[0], normed_turned, gated_turned[0])
    for batch in (0, 1):
        act, grad_gate, grad_up, grad_logit = expert_forward(
            owner.astype(jnp.int32),
            after(slot_other[batch], back_sent),
            grad_act_own[batch],
            grad_act_sent[batch],
            [slots_f[batch * col_count + bits] for bits in range(col_count)],
            gate_blocks,
            up_blocks,
            router_blocks,
        )
        acts.append(act)
        grad_gates.append(grad_gate)
        grad_ups.append(grad_up)
        grad_logits.append(grad_logit)
        back_sent = send_back((2, 3) if batch == 0 else (6, 7))
    back_sent = send_back((4, 5))
    grad_logits[0] = after(grad_logits[0], back_sent)
    back_sent = send_back((1, 0))

    def weight_grads(pair, dtype, wait, merged=False):
        return turned_dots(
            [(slots_f[bits], slots_f[bits + col_count]) for bits in pair],
            [grad_gates, grad_ups, (after(grad_logits[0], wait), grad_logits[1])],
            [dtype, dtype, F32],
            merged,
        )

    both_far, up_far, router_far = weight_grads((2, 3), BF, back_sent, True)
    grad_normed_f_part = gather_slots(
        after(owner_starts, both_far),
        owner_rows.T,
        [back_blocks[bits] for bits in range(owners)],
    )
    gate_near, up_near, router_near = weight_grads((0,), F32, grad_normed_f_part)
    gate_side, up_side, router_side = weight_grads((1,), BF, router_near)

    act_near = swap(after(acts[0], grad_normed_f_part), "col", 2, col_count)
    grad_normed_f = row_total(grad_normed_f_part, act_near, router_side)

    middle_norm_grad, gain_ffn_grad = norm_backward(middle, factor_f, gain_f, grad_normed_f)
    grad_middle = d_out.astype(F32) + middle_norm_grad
    grad_middle_low = grad_middle.astype(BF)
    grad_middle_all = row_gather(grad_middle_low)
    act_far = swap(after(acts[1], grad_middle_low), "col", 2, col_count)
    act_pairs = [(acts[0], act_near), (acts[1], act_far)]
    gate_near_sent = swap(gate_side, "col", 1, col_count)
    up_near_sent = swap(up_side, "col", 1, col_count)

    down_blocks = {}

    def down_pair(place, sent, start):
        bits = half_bits[place]
        down_blocks[bits], down_blocks[bits ^ 2] = (sent, start), (sent, start + 1)

    near_down = [
        pair_dots(act_pairs[0], [after(down_pairs[place], grad_middle_low)])
        for place in (0, 1)
    ]
    down_pair(0, near_down[0], 0)
    down_pair(1, swap(near_down[1], "col", 1, col_count), 0)

    gate_early = assemble(
        after(block_order, grad_middle_low),
        0,
        col_count,
        [(gate_near, 0), (gate_near_sent, 0)],
    )
    far_down = pair_dots(
        act_pairs[1], [after(down_pairs[0], near_down[1], gate_early), down_pairs[1]]
    )
    far_sent = swap(far_down, pair_axes, col_count, owners)
    down_pair(2, far_sent, 0)
    down_hop = swap(
        take_blocks(far_sent, after(jnp.arange(4, dtype=jnp.int32), far_down), 2, 1, 2),
        "col",
        1,
        col_count,
    )
    down_pair(3, down_hop, 0)
    up_received = swap(after(up_far, grad_middle_low), "col", 2, col_count)
    grad_gated = col_scatter(
        grad_middle_all, out_weight, None, True, [far_down], [], True, up_received
    )
    own_base = dp_index * half_experts
    away_base = (1 - dp_index) * half_experts

    grad_order = fence(grad_gated[2], block_order)

    def out_grads(base, dtype):
        return expert_grads(
            left_grad_kernel,
            grad_order,
            base,
            half_experts,
            attn_routes.T,
            grad_middle_all,
            gated_turned,
            (head_width, features),
            dtype,
        )

    out_away = out_grads(away_base, BF)
    out_own = out_grads(own_base, F32)
    pieces, grad_logits_a = attend_back(
        after(side, out_away, out_own),
        segments,
        cosine,
        sine_rows,
        saved,
        attended,
        grad_gated[0:2] + grad_gated[3:],
    )

    ffn_part = gather_slots(
        after(owner_starts, pieces),
        owner_rows.T,
        [down_blocks[bits] for bits in range(owners)],
    )
    ffn_total = row_total(ffn_part)
    out_away_sent = swap(out_away, "dp", 1, dp_count)

    def down_grad_part(near, dtype, wait):
        lefts = [(after(acts[0], wait), acts[1]), (act_near, act_far)]
        return [
            turned_dots(
                [lefts[lead]],
                [[(grad_pairs[place], lead) for place in (near, 2 + near)]],
                [dtype],
            )[0]
            for lead in (0, 1)
        ]

    down_away = down_grad_part(1, BF, ffn_part)
    down_near = down_grad_part(0, F32, down_away[0])
    logits_back = col_blocks(grad_logits_a)
    pieces_blocks = col_blocks(pieces, out_away_sent, *down_away, *down_near)
    normed_part = merge_matmul(
        block_order,
        attn_routes,
        pieces_blocks,
        query_weight,
        (logits_back, kv_weight, lane_router),
        True,
    )

    def query_grads(base, dtype):
        return expert_grads(
            right_grad_kernel,
            block_order,
            base,
            half_experts,
            attn_routes,
            normed_turned,
            pieces_blocks,
            (features, head_width),
            dtype,
        )

    query_away = query_grads(after(away_base, normed_part), BF)
    kv_away = plain_grad(
        fence(query_away, block_order), 3 - dp_index, normed_turned, pieces_blocks, BF
    )
    query_sent = swap(query_away, "dp", 1, dp_count)
    kv_sent = swap(kv_away, "dp", 1, dp_count)
    query_own = query_grads(after(own_base, kv_away), F32)
    kv_own = plain_grad(
        block_order, after(2 + dp_index, query_own), normed_turned, pieces_blocks, F32
    )
    router_attn_grad = plain_grad(
        block_order,
        after(0 * dp_index, kv_own),
        normed_turned,
        [item[None] for item in logits_back],
        F32,
        attn_experts,
    )
    both_received = swap(after(both_far, pieces_blocks[2], logits_back[2]), "col", 2, col_count)
    tail = after(block_order, router_attn_grad)
    down_sent = [swap(item, "col", 1, col_count) for item in down_away]
    down_grad = assemble(
        after(tail, *down_near),
        0,
        col_count,
        [(down_near[0], 0), (down_sent[0], 0), (down_near[1], 0), (down_sent[1], 0)],
    )
    up_early = assemble(
        after(tail, down_grad),
        0,
        col_count,
        [(up_near, 0), (up_near_sent, 0), (up_received, 0)],
    )
    out_grad = add_wide(out_own, after(out_away_sent, down_grad))
    query_grad = add_wide(query_own, after(query_sent, out_grad))
    kv_grad = add_wide(kv_own, after(kv_sent, out_grad))
    grad_normed = row_total(normed_part, router_attn_grad)
    gain_attn_grad = jnp.sum(grad_normed * rows_in * factor_a[:, None], axis=0)
    small = jnp.concatenate(
        [
            router_attn_grad,
            gain_ffn_grad[None],
            gain_attn_grad[None],
            router_near[0],
            router_side[0],
            router_far[0],
            router_far[1],
        ],
        axis=0,
    )
    small = small_total(small, ("row", "dp"))
    both_received = after(
        both_received, gate_early, up_early, out_grad, query_grad, kv_grad, small
    )
    both_side = take_blocks(
        both_received, fence(both_received, jnp.arange(4, dtype=jnp.int32)), 1, 1, 2
    )
    both_side = swap(both_side, "col", 1, col_count)
    input_norm_grad, _ = norm_backward(
        rows_in, factor_a[:, None], gain_a, grad_normed, both_side
    )
    input_grad = grad_middle + input_norm_grad
    layer_out = (middle + ffn_total).astype(BF)
    lines = attn_experts + 2
    gain_ffn_grad, gain_attn_grad = small[lines - 2], small[lines - 1]
    router_ffn_grad = sum(
        swap(
            small[lines + bits * ffn_experts : lines + (bits + 1) * ffn_experts],
            "col",
            bits,
            col_count,
        )
        for bits in range(col_count)
    )
    gate_grad = assemble(
        tail, 2, col_count, [(both_received, 0), (both_side, 0)], gate_early
    )
    up_grad = assemble(tail, 3, col_count, [(both_side, 1)], up_early)
    ffn_half = ffn_experts // dp_count
    router_ffn_grad = lax.dynamic_slice_in_dim(
        router_ffn_grad, dp_index * ffn_half, ffn_half, 0
    ).T
    router_attn_grad = lax.dynamic_slice_in_dim(
        small, dp_index * half_experts, half_experts, 0
    ).T
    return (
        layer_out,
        input_grad,
        gain_attn_grad,
        router_attn_grad,
        query_grad,
        kv_grad,
        out_grad,
        gain_ffn_grad,
        router_ffn_grad,
        gate_grad,
        up_grad,
        down_grad,
    )


def solution(mesh):
    in_specs = (
        P(("dp", "row"), "col"),
        P("col"),
        P("col", None),
        P(None, "col", "row"),
        P(None, "col", "row"),
        P(None, "row", "col"),
        P("col"),
        P("col", None),
        P(None, "col", "row"),
        P(None, "col", "row"),
        P(None, "row", "col"),
        P("dp", None),
        P("dp", None),
        P("dp", None),
        P("dp", None),
        P(("dp", "col"), None),
        P(("dp", "row"), "col"),
    )
    out_specs = (
        P(("dp", "row"), "col"),
        P(("dp", "row"), "col"),
        P("col"),
        P("col", "dp"),
        P("dp", "col", "row"),
        P("dp", "col", "row"),
        P("dp", "row", "col"),
        P("col"),
        P("col", "dp"),
        P("dp", "col", "row"),
        P("dp", "col", "row"),
        P("dp", "row", "col"),
    )
    return jax.shard_map(local, mesh=mesh, in_specs=in_specs, out_specs=out_specs, check_vma=False)
```
